128 devices in a mesh: fsdp: 16 (over z, x), seq: 8 (over y, core).
Axes of the slice: x: 4, y: 4, z: 4, core: 2. Of those that a mesh axis runs over, the one named last changes fastest.
Arguments:
- tokens: bfloat16 [16384, 768], P(('fsdp', 'seq')), may hold values from -6 to 6
- segments: int32 [16, 1024], P('fsdp'), may hold values from 0 to 2, as said below
- routes: int32 [16384, 1], P(('fsdp', 'seq')), may hold values from 0 to 127; in each aligned block of 128 rows (0 to 127, 128 to 255, ...) at most 2 rows name the same one
- gain_attn: bfloat16 [768], P(('fsdp', 'seq')), may hold values from 0.25 to 1.75
- w_query: bfloat16 [768, 768], P(('fsdp', 'seq')), may hold values from -0.21875 to 0.21875
- w_key: bfloat16 [768, 768], P(('fsdp', 'seq')), may hold values from -0.21875 to 0.21875
- w_value: bfloat16 [768, 768], P(('fsdp', 'seq')), may hold values from -0.21875 to 0.21875
- w_output: bfloat16 [768, 768], P(('fsdp', 'seq')), may hold values from -0.875 to 0.875
- rel_table: bfloat16 [384], P(('fsdp', 'seq')), may hold values from -6 to 6
- gain_moe: bfloat16 [768], P(('fsdp', 'seq')), may hold values from 0.25 to 1.75
- w_router: bfloat16 [768, 128], P(('fsdp', 'seq')), may hold values from -0.15625 to 0.15625
- w_inner: bfloat16 [128, 768, 3072], P(('fsdp', 'seq')), may hold values from -0.21875 to 0.21875
- w_outer: bfloat16 [128, 3072, 768], P(('fsdp', 'seq')), may hold values from -12 to 12
- cotangent: bfloat16 [16384, 768], P(('fsdp', 'seq')), may hold values from -6 to 6
Outputs:
- layer_out: bfloat16 [16384, 768], P(('fsdp', 'seq'))
- tokens_grad: float32 [16384, 768], P(('fsdp', 'seq'))
- gain_attn_grad: bfloat16 [768], P(('fsdp', 'seq'))
- w_query_grad: bfloat16 [768, 768], P(('fsdp', 'seq'))
- w_key_grad: bfloat16 [768, 768], P(('fsdp', 'seq'))
- w_value_grad: bfloat16 [768, 768], P(('fsdp', 'seq'))
- w_output_grad: bfloat16 [768, 768], P(('fsdp', 'seq'))
- rel_table_grad: bfloat16 [384], P(('fsdp', 'seq'))
- gain_moe_grad: bfloat16 [768], P(('fsdp', 'seq'))
- w_router_grad: bfloat16 [768, 128], P(('fsdp', 'seq'))
- w_inner_grad: bfloat16 [128, 768, 3072], P(('fsdp', 'seq'))
- w_outer_grad: bfloat16 [128, 3072, 768], P(('fsdp', 'seq'))
The draws below stay inside these ranges and needn't reach their ends.
Inputs may be any that keep to these rules, and one draw needn't show every extreme that they name: `routes`: among the 128 rows of one device no expert is named more than 2 times; some expert is named exactly 2 times in some device's rows. `segments`: document numbers never fall along a sequence and every sequence has all three. Document 0 fills the first 96 to 127 positions, document 2 the last 96 to 127 positions, and document 1 the rest.
All inputs are finite; a program needn't handle non-finite values.
Results may differ from the reference program's by a relative error of at most 0.03.
Values may be sent and summed in bfloat16 or wider, within the bound.
No kernel may reach another device: no remote copies, remote signals or barrier semaphores. Data moves between devices by JAX's collectives and lax.ppermute only.
A program may use at most 128 MiB of HBM per device.

```python
import math
import jax
import jax.numpy as jnp
import numpy as np
from jax import lax

D = 768
HEADS = 12
HEAD_DIM = 64
FF = 3072
BUCKETS = 32
TOK_DEV = 128
EXPERTS = 128
CAP = 2
LEN = 1024
SEQS = 16
TOKENS = 16384
N_FSDP = 16
N_SEQ = 8


def draw_segments(key, part):
    key = jax.random.fold_in(key, 7)
    keys = jax.random.split(key, 2)
    least = max(1, 3 * TOK_DEV // 4)
    begin_long = jax.random.randint(keys[0], (SEQS, 1), least, TOK_DEV, dtype=jnp.int32)
    end_long = jax.random.randint(keys[1], (SEQS, 1), LEN - TOK_DEV + 1, LEN - least + 1, dtype=jnp.int32)
    places = jnp.arange(LEN, dtype=jnp.int32)[None, :]
    found = (places >= begin_long).astype(jnp.int32) + (places >= end_long).astype(jnp.int32)
    return found


def block_levels(own_key, extent, cuts, low, top_value):
    factor_of = 1.0
    for dim, blocks in cuts:
        draws = jax.random.uniform(jax.random.fold_in(jax.random.fold_in(own_key, 6), dim), (blocks,), jnp.float32, low / len(cuts), top_value / len(cuts))
        factor_of = factor_of * jnp.repeat(jnp.exp(draws), extent[dim] // blocks).reshape((-1,) + (1,) * (len(extent) - 1 - dim))
    return factor_of


def routed_block(own_key, own, number, rows, count, top, most, slope):
    ranking = jax.random.permutation(own_key, count)
    crowded, common = load_shares(count, rows * top, most, slope, True), load_shares(count, rows * top, most, slope, False)
    places = jnp.arange(count)

    def named(lengths, turn):
        used = int((lengths > 0).sum())
        fixed = max(1, used // 4)
        shifted = fixed + (places - fixed + turn * (used - fixed)) % max(1, count - fixed)
        return jnp.zeros((count,), jnp.int32).at[ranking[jnp.where(places < fixed, places, shifted)]].set(jnp.asarray(lengths, jnp.int32))

    lengths = jnp.where(number % 4 == 0, named(crowded, number // 4), named(common, number - number // 4 - 1))
    mixed = jax.random.permutation(jax.random.fold_in(own, 3), count)
    giver, receiver = mixed[0:count // 2 * 2:2], mixed[1:count // 2 * 2:2]
    slack = jnp.minimum(lengths[giver] - 1, most - lengths[receiver]) // 2
    slack = jnp.where((giver == ranking[0]) | (receiver == ranking[0]) | (lengths[receiver] == 0), 0, jnp.maximum(slack, 0))
    shifted = jax.random.randint(jax.random.fold_in(own, 4), (count // 2,), 0, 1 << 20) % (slack + 1)
    lengths = lengths.at[giver].add(-shifted).at[receiver].add(shifted)
    members = jnp.searchsorted(jnp.cumsum(lengths), jnp.arange(rows * top), side="right").astype(jnp.int32)
    grid = members.reshape(top, rows).T
    grid = grid[jax.random.permutation(jax.random.fold_in(own, 1), rows)]
    turn = jax.random.randint(jax.random.fold_in(own, 2), (rows, 1), 0, top)
    return jnp.take_along_axis(grid, (jnp.arange(top)[None, :] + turn) % top, axis=1)


def load_shares(number_of, total, reach, lean, full):
    loads = [(1 << 20) // math.isqrt(standing ** lean) + 1 for standing in range(1, number_of + 1)]
    largest = reach if full else min(reach, max(-(-total // number_of), total * loads[0] // sum(loads)))
    least = 1 if total - largest >= number_of - 1 else 0
    holding, surplus = [largest] + [least] * (number_of - 1), total - largest - least * (number_of - 1)
    while surplus > 0:
        candidates = [i for i in range(1, number_of) if holding[i] < largest] or [i for i in range(1, number_of) if holding[i] < reach]
        mass, left = sum([loads[i] for i in candidates]), surplus
        for i in candidates:
            more = min(reach - holding[i], max(1, left * loads[i] // mass), surplus)
            holding[i] = holding[i] + more
            surplus = surplus - more
    return np.array(holding)


def noise(own_key, extent, scale, bound, cuts=(), kind=jnp.bfloat16):
    entries = scale * jax.random.normal(own_key, extent, jnp.float32)
    if cuts:
        entries = entries * block_levels(own_key, extent, cuts, -0.22, 0.18)
    return jnp.clip(entries, -bound, bound).astype(kind)


def setup_inputs(seed: int = 0) -> dict:
    seeds = jax.random.split(jax.random.key(seed), 15)
    tokens = noise(seeds[0], (TOKENS, D), 1.0, 6.0, ((0, 128),))
    segments = draw_segments(jax.random.fold_in(seeds[14], 71), 0)
    routes_keys = jax.random.split(jax.random.fold_in(seeds[2], 1), TOKENS // TOK_DEV)
    routes_turns = jax.random.permutation(jax.random.fold_in(seeds[2], 3), TOKENS // TOK_DEV)
    routes = jax.vmap(lambda own, number: routed_block(jax.random.fold_in(seeds[2], 2), own, number, TOK_DEV, EXPERTS, 1, CAP, 1))(routes_keys, routes_turns).reshape((TOKENS, 1))
    gain_attn = jnp.clip(1.0 + 0.15 * jax.random.normal(seeds[3], (D,), jnp.float32), 0.25, 1.75).astype(jnp.bfloat16)
    w_query = noise(seeds[4], (D, D), D ** -0.5, 0.21875, ((0, 128),))
    w_key = noise(seeds[5], (D, D), D ** -0.5, 0.21875, ((0, 128),))
    w_value = noise(seeds[6], (D, D), D ** -0.5, 0.21875, ((0, 128),))
    w_output = noise(seeds[7], (D, D), (D // 16) ** -0.5, 0.875, ((0, 128),))
    rel_table = noise(seeds[8], (HEADS * BUCKETS,), 1.0, 6.0, ((0, 128),))
    gain_moe = jnp.clip(1.0 + 0.15 * jax.random.normal(seeds[9], (D,), jnp.float32), 0.25, 1.75).astype(jnp.bfloat16)
    w_router = noise(seeds[10], (D, EXPERTS), 0.025, 0.15625, ((0, 128),))
    w_inner = noise(seeds[11], (EXPERTS, D, FF), D ** -0.5, 0.21875, ((0, 128),))
    w_outer = noise(seeds[12], (EXPERTS, FF, D), (EXPERTS / 64), 12.0, ((0, 128),))
    cotangent = noise(seeds[13], (TOKENS, D), 1.0, 6.0, ((0, 128),))
    return {"tokens": tokens, "segments": segments, "routes": routes, "gain_attn": gain_attn, "w_query": w_query, "w_key": w_key, "w_value": w_value, "w_output": w_output, "rel_table": rel_table, "gain_moe": gain_moe, "w_router": w_router, "w_inner": w_inner, "w_outer": w_outer, "cotangent": cotangent}


@jax.custom_vjp
def low(v):
    return lax.optimization_barrier(v.astype(jnp.bfloat16)).astype(jnp.float32)

@jax.custom_vjp
def low_back(v):
    return v

def low_keep(v):
    return (low(v), None)

def low_pass(kept, grad):
    return (grad,)

def back_keep(v):
    return (v, None)

def back_low(kept, grad):
    return (low(grad),)
low.defvjp(low_keep, low_pass)
low_back.defvjp(back_keep, back_low)
eps = 1e-06
bucket_edges = (12, 16, 23, 32, 46, 64, 91)
highest = lax.Precision.HIGHEST

def normed(values, gain):
    return values * lax.rsqrt(lax.optimization_barrier(jnp.mean(values * values, axis=-1, keepdims=True)) + eps) * gain

def bucket_of(offsets):
    spread = jnp.abs(offsets)
    bucket_ids = (offsets > 0).astype(jnp.int32) * 16 + jnp.minimum(spread, 8)
    for border in bucket_edges:
        bucket_ids = bucket_ids + (spread >= border).astype(jnp.int32)
    return bucket_ids

def attend_sequence(query_seq, key_seq, value_seq, doc_ids, table_f):
    block_rows = min(512, LEN)
    scale = HEAD_DIM ** (-0.5)
    key_pos = jnp.arange(LEN, dtype=jnp.int32)

    def one_block(block_index):
        anchor = (block_index * block_rows).astype(jnp.int32)
        query_blk = lax.dynamic_slice_in_dim(query_seq, anchor, block_rows, 0)
        query_pos = anchor + jnp.arange(block_rows, dtype=jnp.int32)
        bucket_ids = bucket_of(key_pos[None, :] - query_pos[:, None])
        bias = jnp.take(table_f, bucket_ids, axis=1)
        scores = jnp.einsum('rhd,khd->hrk', query_blk, key_seq, precision=highest) * scale + bias
        scores = low_back(scores)
        query_doc = lax.dynamic_slice_in_dim(doc_ids, anchor, block_rows, 0)
        same_doc = query_doc[:, None] == doc_ids[None, :]
        scores = jnp.where(same_doc[None], scores, -1e+30)
        top_score = lax.optimization_barrier(jnp.max(scores, axis=-1, keepdims=True))
        exp_scores = jnp.exp(scores - top_score)
        exp_total = lax.optimization_barrier(jnp.sum(exp_scores, axis=-1, keepdims=True))
        soft = low(exp_scores / exp_total)
        return jnp.einsum('hrk,khd->rhd', soft, value_seq, precision=highest)
    blocks = lax.map(jax.checkpoint(one_block), jnp.arange(LEN // block_rows, dtype=jnp.int32))
    return blocks.reshape(LEN, HEADS * HEAD_DIM)

def one_expert(operands):
    rows_in, inner_w, outer_w = operands
    pre_act = low_back(jnp.dot(rows_in, inner_w, precision=highest))
    act_low = low(jax.nn.gelu(pre_act))
    return low(low_back(jnp.dot(act_low, outer_w, precision=highest)))

def reference(tokens, segments, routes, gain_attn, w_query, w_key, w_value, w_output, rel_table, gain_moe, w_router, w_inner, w_outer, cotangent):
    device_count = N_FSDP * N_SEQ
    route_col = routes[:, 0].astype(jnp.int32)
    picked = (route_col[:, None] == jnp.arange(EXPERTS, dtype=jnp.int32)[None, :]).astype(jnp.int32)
    per_block = picked.reshape(device_count, TOK_DEV, EXPERTS)
    earlier = (jnp.cumsum(per_block, axis=1) - per_block).astype(jnp.int32)
    local_slot = lax.optimization_barrier(jnp.sum(earlier * per_block, axis=-1)).reshape(TOKENS).astype(jnp.int32)
    global_slot = (jnp.arange(TOKENS, dtype=jnp.int32) // TOK_DEV * CAP + local_slot).astype(jnp.int32)
    onehot_f = picked.astype(jnp.float32)
    shape_four = (SEQS, LEN, HEADS, HEAD_DIM)

    def forward(inputs, gain_one, query_w, key_w, value_w, output_w, table_flat, gain_two, router_w, inner_w, outer_w):
        normed_low = low(normed(inputs, gain_one))
        query_all = low(low_back(jnp.dot(normed_low, query_w, precision=highest)))
        key_all = low(low_back(jnp.dot(normed_low, key_w, precision=highest)))
        value_all = low(low_back(jnp.dot(normed_low, value_w, precision=highest)))
        table_f = table_flat.reshape(HEADS, BUCKETS)

        def one_sequence(operands):
            query_seq, key_seq, value_seq, doc_ids = operands
            return attend_sequence(query_seq, key_seq, value_seq, doc_ids, table_f)
        mixed = lax.map(jax.checkpoint(one_sequence), (query_all.reshape(shape_four), key_all.reshape(shape_four), value_all.reshape(shape_four), segments))
        mixed_low = low(low_back(mixed.reshape(TOKENS, D)))
        hidden = inputs + low_back(jnp.dot(mixed_low, output_w, precision=highest))
        second_low = low(normed(hidden, gain_two))
        logits = low_back(jnp.dot(second_low, router_w, precision=highest))
        exp_logits = jnp.exp(logits - lax.optimization_barrier(jnp.max(logits, axis=-1, keepdims=True)))
        router_prob = exp_logits / lax.optimization_barrier(jnp.sum(exp_logits, axis=-1, keepdims=True))
        gate_prob = lax.optimization_barrier(jnp.sum(router_prob * onehot_f, axis=-1, keepdims=True))
        send_rows = low_back(second_low)
        buffer = jnp.zeros((EXPERTS, device_count * CAP, D), jnp.float32).at[route_col, global_slot].set(send_rows)
        expert_rows = lax.map(jax.checkpoint(one_expert), (buffer, inner_w, outer_w))
        returned = expert_rows[route_col, global_slot]
        return hidden + gate_prob * returned
    floats = (tokens.astype(jnp.float32), gain_attn.astype(jnp.float32), w_query.astype(jnp.float32), w_key.astype(jnp.float32), w_value.astype(jnp.float32), w_output.astype(jnp.float32), rel_table.astype(jnp.float32), gain_moe.astype(jnp.float32), w_router.astype(jnp.float32), w_inner.astype(jnp.float32), w_outer.astype(jnp.float32))
    layer_value, pull_back = jax.vjp(forward, *floats)
    grads = pull_back(cotangent.astype(jnp.float32))
    return (layer_value.astype(jnp.bfloat16), grads[0], grads[1].astype(jnp.bfloat16), grads[2].astype(jnp.bfloat16), grads[3].astype(jnp.bfloat16), grads[4].astype(jnp.bfloat16), grads[5].astype(jnp.bfloat16), grads[6].astype(jnp.bfloat16), grads[7].astype(jnp.bfloat16), grads[8].astype(jnp.bfloat16), grads[9].astype(jnp.bfloat16), grads[10].astype(jnp.bfloat16))
```

```python
import functools

import jax
import jax.numpy as jnp
from jax import lax
from jax.experimental import pallas as pl
from jax.experimental.pallas import tpu as pltpu
from jax.sharding import PartitionSpec as P

bf16 = jnp.bfloat16
f32 = jnp.float32

WIDTH = 768
TOK = 128
LEN = 1024
FF = 3072
GROUP = 3
HD = 64
COLS = GROUP * HD
BAND = 15 * TOK
PACK = 1152
HALF = WIDTH // 2
FF_TILE = 512
eps = 1e-06
bucket_edges = (12, 16, 23, 32, 46, 64, 91)
BOTH = ("fsdp", "seq")

params = pltpu.CompilerParams(vmem_limit_bytes=56 << 20)
smem = pl.BlockSpec(memory_space=pltpu.SMEM)
vmem = pl.BlockSpec(memory_space=pltpu.VMEM)


def iota(shape, dim):
    return lax.broadcasted_iota(jnp.int32, shape, dim)


def sixth(n):
    return (n * 10923) >> 16


def third(n):
    return (n * 21846) >> 16


def bucket_of(offsets):
    spread = jnp.abs(offsets)
    ids = (offsets > 0).astype(jnp.int32) * 16 + jnp.minimum(spread, 8)
    for border in bucket_edges:
        ids = ids + (spread >= border).astype(jnp.int32)
    return ids


def mm(a, b):
    return jnp.dot(a, b, preferred_element_type=f32)


def mm_nt(a, b):
    return lax.dot_general(a, b, (((1,), (1,)), ((), ())), preferred_element_type=f32)


def mm_tn(a, b):
    return lax.dot_general(a, b, (((0,), (0,)), ((), ())), preferred_element_type=f32)


def exact(a, b):
    return lax.dot_general(
        a,
        b,
        (((1,), (0,)), ((), ())),
        precision=lax.Precision.HIGHEST,
        preferred_element_type=f32,
    )


def call(kernel, outs, ins, scratch=(), **kw):
    return pl.pallas_call(
        kernel,
        out_shape=outs,
        in_specs=ins,
        out_specs=jax.tree.map(lambda _: vmem, outs),
        scratch_shapes=list(scratch),
        compiler_params=params,
        **kw,
    )


def load_rows(ref, start, stride):
    return jnp.concatenate(
        [ref[j, pl.ds(start, 128, stride=stride), :] for j in range(ref.shape[0])], axis=1
    )


def store_rows(ref, start, stride, value):
    for j in range(value.shape[1] // 128):
        ref[j, pl.ds(start, 128, stride=stride), :] = value[:, 128 * j : 128 * j + 128]


def whole(ref, first, last):
    return jnp.concatenate([ref[j] for j in range(first, last)], axis=1)


def fill(ref, value):
    for j in range(ref.shape[0]):
        ref[j] = value[:, 128 * j : 128 * j + 128].astype(f32)


def sds(*shape, dtype=bf16):
    return jax.ShapeDtypeStruct(shape, dtype)


def attend_kernel(
    idx_ref, x_ref, pack_ref, seg_ref,
    o0_ref, o1_ref, o2_ref, o3_ref, h_ref, wqkv_ref, wo_ref, router_ref, gain_ref,
    qe_ref, ke_ref, v_ref, band_ref, lse_ref,
    pf_ref, wf_ref, tail_ref, rf_ref, os_ref,
):
    y, c = idx_ref[0], idx_ref[1]
    fill(pf_ref, pack_ref)
    for r in range(6):
        store_rows(wf_ref, r, 6, load_rows(pf_ref, r, 8))
    row6 = load_rows(pf_ref, 6, 8)
    row7 = load_rows(pf_ref, 7, 8)
    blank = jnp.zeros((128, 64), f32)
    for r in range(6):
        tail = jnp.concatenate([row6[:, 192 * r : 192 * r + 192], blank], axis=1)
        store_rows(tail_ref, r, 6, tail)
        rf_ref[pl.ds(r, 128, stride=6), :] = row7[:, 128 * r : 128 * r + 128]
    wqkv_ref[...] = whole(wf_ref, 0, 5)[:, : 3 * COLS].astype(bf16)
    left = whole(wf_ref, 4, 9)[:, 64:]
    wo_ref[...] = jnp.concatenate([left, whole(tail_ref, 0, 2)[:, :COLS]], axis=1).astype(bf16)
    router_ref[...] = rf_ref[...].astype(bf16)
    small = row7[:, WIDTH : WIDTH + 128].astype(bf16)

    lanes = iota((128, WIDTH), 1)
    rows = iota((128, WIDTH), 0)
    own = sixth(lanes) == rows
    within = lanes - 6 * sixth(lanes)
    gains = []
    for base in (0, 6):
        spread = mm(small, (rows == within + base).astype(bf16))
        gains.append(jnp.sum(jnp.where(own, spread, 0.0), axis=0, keepdims=True))
    gain_ref[...] = jnp.concatenate([gains[0], gains[1], jnp.zeros((6, WIDTH), f32)], axis=0)
    lanes = iota((128, 384), 1)
    rows = iota((128, 384), 0)
    spread = mm(small, (rows == lanes - 3 * third(lanes) + 12).astype(bf16))
    table = jnp.sum(jnp.where(third(lanes) == rows, spread, 0.0), axis=0, keepdims=True)
    table = jnp.broadcast_to(table, (8, 384)).astype(bf16)
    ids = bucket_of(iota((384, 512), 1) - 255)
    entry = iota((384, 512), 0)
    for h in range(GROUP):
        hot = (entry == ids + 32 * (3 * y + h)).astype(bf16)
        line = mm(table, hot)[:1]
        wide = pltpu.roll(
            jnp.broadcast_to(line, (TOK, 512)), 385, 1, stride=1, stride_axis=0
        )
        band_ref[h, :, : 6 * TOK] = jnp.broadcast_to(line[:, :1], (TOK, 6 * TOK))
        band_ref[h, :, 6 * TOK : 9 * TOK] = wide[:, : 3 * TOK]
        band_ref[h, :, 9 * TOK :] = jnp.broadcast_to(line[:, 511:], (TOK, 6 * TOK))

    gain = gains[0]

    def project(i, _):
        at = pl.ds(pl.multiple_of(i * TOK, TOK), TOK)
        x = x_ref[at, :].astype(f32)
        hb = (x * lax.rsqrt(jnp.mean(x * x, axis=-1, keepdims=True) + eps) * gain).astype(bf16)
        h_ref[at, :] = hb
        qkv = mm(hb, wqkv_ref[...])
        doc = seg_ref[at, :]
        lane = iota((TOK, HD), 1)
        same = lane == doc
        q_mark = jnp.where(same, -1e30, 0.0)
        k_mark = jnp.where((lane < 3) & jnp.logical_not(same), 1.0, 0.0)
        q_parts, k_parts = [], []
        for h in range(GROUP):
            q = qkv[:, HD * h : HD * h + HD]
            k = qkv[:, COLS + HD * h : COLS + HD * h + HD]
            q_parts += [q.astype(bf16).astype(f32) * 0.125, q_mark]
            k_parts += [k, k_mark]
        qe_ref[at, :] = jnp.concatenate(q_parts, axis=1).astype(bf16)
        ke_ref[at, :] = jnp.concatenate(k_parts, axis=1).astype(bf16)
        v_ref[at, :] = qkv[:, 2 * COLS :].astype(bf16)
        return 0

    lax.fori_loop(0, 8, project, 0)

    def attend(k, _):
        yq = lax.rem(y + k, 4)
        pq = 2 * yq + c
        at = pl.ds(pl.multiple_of(pq * TOK, TOK), TOK)
        shift = pl.ds(pl.multiple_of((7 - pq) * TOK, TOK), LEN)
        lane = iota((TOK, 128), 1)
        lse_all = jnp.zeros((TOK, 128), f32)
        outs = []
        for h in range(GROUP):
            s = mm_nt(qe_ref[at, 128 * h : 128 * h + 128], ke_ref[:, 128 * h : 128 * h + 128])
            s = s + band_ref[h, :, shift]
            top = jnp.max(s, axis=-1, keepdims=True)
            e = jnp.exp(s - top)
            total = jnp.sum(e, axis=-1, keepdims=True)
            p = (e * (1.0 / total)).astype(bf16)
            outs.append(mm(p, v_ref[:, HD * h : HD * h + HD]))
            lse_all = jnp.where(lane == h, top + jnp.log(total), lse_all)
        os_ref[k] = jnp.concatenate(outs, axis=1).astype(bf16)
        lse_ref[yq] = lse_all
        return 0

    lax.fori_loop(0, 4, attend, 0)
    o0_ref[...] = os_ref[0]
    o1_ref[...] = os_ref[1]
    o2_ref[...] = os_ref[2]
    o3_ref[...] = os_ref[3]


def attend(idx, x_all, pack, seg_col):
    outs = (
        [sds(TOK, COLS)] * 4
        + [sds(LEN, WIDTH), sds(WIDTH, 3 * COLS), sds(WIDTH, WIDTH), sds(WIDTH, 128)]
        + [sds(8, WIDTH, dtype=f32), sds(LEN, 384), sds(LEN, 384), sds(LEN, COLS)]
        + [sds(GROUP, TOK, BAND, dtype=f32), sds(4, TOK, 128, dtype=f32)]
    )
    return call(
        attend_kernel,
        outs,
        [smem, vmem, vmem, vmem],
        [
            pltpu.VMEM((9, LEN, 128), f32),
            pltpu.VMEM((9, WIDTH, 128), f32),
            pltpu.VMEM((2, WIDTH, 128), f32),
            pltpu.VMEM((WIDTH, 128), f32),
            pltpu.VMEM((4, TOK, COLS), bf16),
        ],
        name="attend",
    )(idx, x_all, pack, seg_col)


def dispatch_kernel(
    idx_ref, x_ref, o0_ref, o1_ref, o2_ref, o3_ref, wo_ref, router_ref, gain_ref,
    route_ref, cot_ref,
    x1_ref, h2_ref, prob_ref, hot_ref, send_ref,
    sf_ref,
):
    y = idx_ref[0]
    x1 = x_ref[...].astype(f32)
    for k, o_ref in enumerate((o0_ref, o1_ref, o2_ref, o3_ref)):
        src = lax.rem(y + 4 - k, 4)
        x1 = x1 + mm(o_ref[...], wo_ref[pl.ds(pl.multiple_of(src * COLS, COLS), COLS), :])
    x1_ref[...] = x1
    r2 = lax.rsqrt(jnp.mean(x1 * x1, axis=-1, keepdims=True) + eps)
    h2 = (x1 * r2 * gain_ref[1:2, :]).astype(bf16)
    h2_ref[...] = h2
    logits = mm(h2, router_ref[...])
    e = jnp.exp(logits - jnp.max(logits, axis=-1, keepdims=True))
    prob = e / jnp.sum(e, axis=-1, keepdims=True)
    prob_ref[...] = prob
    expert = iota((TOK, 128), 1)
    picked = (route_ref[...] == expert).astype(f32)
    gate = jnp.sum(prob * picked, axis=-1, keepdims=True)
    earlier = (iota((TOK, TOK), 0) > iota((TOK, TOK), 1)).astype(bf16)
    slot = jnp.sum(mm(earlier, picked.astype(bf16)) * picked, axis=-1, keepdims=True)
    geo = (gate * cot_ref[...].astype(f32)).astype(bf16)
    for s in range(2):
        hot = jnp.where((slot > 0.5) == (s == 1), picked, 0.0).astype(bf16)
        hot_ref[s] = hot
        for kind, src in enumerate((h2, geo)):
            placed = mm_tn(hot, src)
            for half in range(2):
                part = placed[:, HALF * half : HALF * half + HALF]
                store_rows(sf_ref, kind * 4 + s * 2 + half, 8, part)
    send_ref[...] = whole(sf_ref, 0, 3).astype(bf16)


def dispatch(idx, x_own, o_parts, wo, router, gains, route_col, cot):
    outs = [
        sds(TOK, WIDTH, dtype=f32), sds(TOK, WIDTH), sds(TOK, 128, dtype=f32),
        sds(2, TOK, 128), sds(LEN, HALF),
    ]
    return call(
        dispatch_kernel,
        outs,
        [smem] + [vmem] * 10,
        [pltpu.VMEM((3, LEN, 128), f32)],
        name="dispatch",
    )(idx, x_own, *o_parts, wo, router, gains, route_col, cot)


def expert_kernel(
    recv_ref, wi_ref, wo_ref, ret_ref, gi_ref, go_ref, rf_ref, x_ref, xt_ref, g_ref, eo_ref, gx_ref
):
    step = pl.program_id(0)

    @pl.when(step == 0)
    def _():
        fill(rf_ref, recv_ref)
        for kind, dst in enumerate((x_ref, g_ref)):
            for s in range(2):
                for half in range(2):
                    dst[TOK * s : TOK * s + TOK, HALF * half : HALF * half + HALF] = load_rows(
                        rf_ref, kind * 4 + s * 2 + half, 8
                    ).astype(bf16)
        xt_ref[...] = x_ref[...].T
        eo_ref[...] = jnp.zeros_like(eo_ref)
        gx_ref[...] = jnp.zeros_like(gx_ref)

    wi = wi_ref[...]
    wo = wo_ref[...]
    g = g_ref[...]
    a = mm(x_ref[...], wi)
    cc = 0.7978845608028654
    sq = a * a
    t = jnp.tanh(cc * (a + 0.044715 * (sq * a)))
    u = (0.5 * a * (1.0 + t)).astype(bf16)
    slope = 0.5 * (1.0 + t) + (0.5 * cc) * a * (1.0 - t * t) * (1.0 + 0.134145 * sq)
    eo_ref[...] += mm(u, wo)
    ga = (mm_nt(g, wo) * slope).astype(bf16)
    go_ref[...] = mm_tn(u, g).astype(bf16)
    gi_ref[...] = mm(xt_ref[...], ga).astype(bf16)
    gx_ref[...] += mm_nt(ga, wi)

    @pl.when(step == FF // FF_TILE - 1)
    def _():
        for kind, src in enumerate((eo_ref, gx_ref)):
            for s in range(2):
                for half in range(2):
                    part = src[TOK * s : TOK * s + TOK, HALF * half : HALF * half + HALF]
                    store_rows(rf_ref, kind * 4 + s * 2 + half, 8, part)
        ret_ref[...] = whole(rf_ref, 0, 3).astype(bf16)


def experts(recv, w_inner, w_outer):
    return pl.pallas_call(
        expert_kernel,
        grid=(FF // FF_TILE,),
        out_shape=[sds(LEN, HALF), sds(1, WIDTH, FF), sds(1, FF, WIDTH)],
        in_specs=[
            pl.BlockSpec((LEN, HALF), lambda i: (0, 0)),
            pl.BlockSpec((None, WIDTH, FF_TILE), lambda i: (0, 0, i)),
            pl.BlockSpec((None, FF_TILE, WIDTH), lambda i: (0, i, 0)),
        ],
        out_specs=[
            pl.BlockSpec((LEN, HALF), lambda i: (0, 0)),
            pl.BlockSpec((None, WIDTH, FF_TILE), lambda i: (0, 0, i)),
            pl.BlockSpec((None, FF_TILE, WIDTH), lambda i: (0, i, 0)),
        ],
        scratch_shapes=[
            pltpu.VMEM((3, LEN, 128), f32),
            pltpu.VMEM((2 * TOK, WIDTH), bf16),
            pltpu.VMEM((WIDTH, 2 * TOK), bf16),
            pltpu.VMEM((2 * TOK, WIDTH), bf16),
            pltpu.VMEM((2 * TOK, WIDTH), f32),
            pltpu.VMEM((2 * TOK, WIDTH), f32),
        ],
        compiler_params=params,
        name="experts",
    )(recv, w_inner, w_outer)


def return_kernel(
    idx_ref, back_ref, x1_ref, h2_ref, prob_ref, hot_ref, cot_ref, router_ref, gain_ref, wo_ref,
    o0_ref, o1_ref, o2_ref, o3_ref,
    out_ref, dx1_ref, g0_ref, g1_ref, g2_ref, g3_ref, dwo_ref, drouter_ref, dgain_ref,
    bf_ref,
):
    y = idx_ref[0]
    fill(bf_ref, back_ref)
    parts = []
    for kind in range(2):
        halves = []
        for half in range(2):
            got = jnp.zeros((TOK, HALF), f32)
            for s in range(2):
                rows = load_rows(bf_ref, kind * 4 + s * 2 + half, 8).astype(bf16)
                got = got + mm(hot_ref[s], rows)
            halves.append(got)
        parts.append(jnp.concatenate(halves, axis=1))
    eo, gx = parts
    x1 = x1_ref[...]
    prob = prob_ref[...]
    picked = hot_ref[0].astype(f32) + hot_ref[1].astype(f32)
    gate = jnp.sum(prob * picked, axis=-1, keepdims=True)
    out_ref[...] = (x1 + gate * eo).astype(bf16)
    dy = cot_ref[...].astype(f32)
    dgate = jnp.sum(dy * eo, axis=-1, keepdims=True)
    gz = (dgate * gate * (picked - prob)).astype(bf16)
    dh2 = gx + mm_nt(gz, router_ref[...])
    drouter_ref[...] = mm_tn(h2_ref[...], gz)
    r2 = lax.rsqrt(jnp.mean(x1 * x1, axis=-1, keepdims=True) + eps)
    scaled = x1 * r2
    dgain = jnp.sum(dh2 * scaled, axis=0, keepdims=True)
    dgain_ref[...] = jnp.broadcast_to(dgain, (8, WIDTH))
    gd = gain_ref[1:2, :] * dh2
    dx1 = dy + r2 * (gd - scaled * jnp.mean(gd * scaled, axis=-1, keepdims=True))
    dx1_ref[...] = dx1
    gw = dx1.astype(bf16)
    for k, g_ref in enumerate((g0_ref, g1_ref, g2_ref, g3_ref)):
        dst = lax.rem(y + k, 4)
        rows = wo_ref[pl.ds(pl.multiple_of(dst * COLS, COLS), COLS), :]
        g_ref[...] = mm_nt(gw, rows).astype(bf16)
    for k, o_ref in enumerate((o0_ref, o1_ref, o2_ref, o3_ref)):
        src = lax.rem(y + 4 - k, 4)
        terms = mm_tn(o_ref[...], gw)
        for j in range(6):
            dwo_ref[j, pl.ds(pl.multiple_of(src * COLS, COLS), COLS), :] = terms[
                :, 128 * j : 128 * j + 128
            ]


def returned(idx, back, x1, h2, prob, hot, cot, router, gains, wo, o_parts):
    outs = (
        [sds(TOK, WIDTH), sds(TOK, WIDTH, dtype=f32)]
        + [sds(TOK, COLS)] * 4
        + [sds(6, WIDTH, 128, dtype=f32), sds(WIDTH, 128, dtype=f32), sds(8, WIDTH, dtype=f32)]
    )
    return call(
        return_kernel,
        outs,
        [smem] + [vmem] * 13,
        [pltpu.VMEM((3, LEN, 128), f32)],
        name="returned",
    )(idx, back, x1, h2, prob, hot, cot, router, gains, wo, *o_parts)


def two_parts(v):
    high = v.astype(bf16)
    return high, (v - high.astype(f32)).astype(bf16)


def backward_kernel(
    idx_ref, g0_ref, g1_ref, g2_ref, g3_ref, x_ref, h_ref, wqkv_ref, qe_ref, ke_ref, v_ref,
    band_ref, lse_ref, dwo_ref, drouter_ref, dgain_ref,
    send_ref, own_ref, other_ref,
    gs_ref, gk_ref, gv_ref, dq_ref, acc_ref, sf_ref, dw_ref, line_ref,
):
    y, c = idx_ref[0], idx_ref[1]
    for k, g_ref in enumerate((g0_ref, g1_ref, g2_ref, g3_ref)):
        gs_ref[k] = g_ref[...]
    gk_ref[...] = jnp.zeros_like(gk_ref)
    gv_ref[...] = jnp.zeros_like(gv_ref)
    dq_ref[...] = jnp.zeros_like(dq_ref)
    acc_ref[...] = jnp.zeros_like(acc_ref)

    def block(k, _):
        yq = lax.rem(y + 4 - k, 4)
        pq = 2 * yq + c
        at = pl.ds(pl.multiple_of(pq * TOK, TOK), TOK)
        shift = pl.ds(pl.multiple_of((7 - pq) * TOK, TOK), LEN)
        lse = lse_ref[yq]
        go = gs_ref[k]
        outs = []
        for h in range(GROUP):
            q = qe_ref[at, 128 * h : 128 * h + 128]
            keys = ke_ref[:, 128 * h : 128 * h + 128]
            g = go[:, HD * h : HD * h + HD]
            s = mm_nt(q, keys) + band_ref[h, :, shift]
            p = jnp.exp(s - lse[:, h : h + 1])
            pd = p * mm_nt(g, v_ref[:, HD * h : HD * h + HD])
            gs = pd - p * jnp.sum(pd, axis=-1, keepdims=True)
            acc_ref[h, :, shift] += gs
            low = gs.astype(bf16)
            outs.append(mm(low, keys)[:, :HD] * 0.125)
            gk_ref[HD * h : HD * h + HD, :] += mm_tn(q, low)[:HD]
            gv_ref[HD * h : HD * h + HD, :] += mm_tn(g, p.astype(bf16))
        dq_ref[at, :COLS] = jnp.concatenate(outs, axis=1).astype(bf16)
        return 0

    lax.fori_loop(0, 4, block, 0)
    dq_ref[:, COLS : 2 * COLS] = gk_ref[...].T.astype(bf16)
    dq_ref[:, 2 * COLS :] = gv_ref[...].T.astype(bf16)

    line_ref[...] = jnp.zeros_like(line_ref)

    def spread(i, _):
        own = (i & 1) == c
        at = pl.ds(pl.multiple_of(i * TOK, TOK), TOK)
        d = mm_nt(dq_ref[at, :], wqkv_ref[...])
        x = x_ref[at, :].astype(f32)
        r1 = lax.rsqrt(jnp.mean(x * x, axis=-1, keepdims=True) + eps)
        line_ref[...] += jnp.broadcast_to(jnp.sum(d * (x * r1), axis=0, keepdims=True), (8, WIDTH))

        @pl.when(own)
        def _():
            own_ref[i >> 1] = d

        @pl.when(jnp.logical_not(own))
        def _():
            other_ref[i >> 1] = d.astype(bf16)

        return 0

    lax.fori_loop(0, 8, spread, 0)

    def weights(j, _):
        at = pl.ds(pl.multiple_of(j * 128, 128), 128)
        terms = mm_tn(h_ref[:, at], dq_ref[...])
        terms = jnp.concatenate([terms, jnp.zeros((128, 64), f32)], axis=1)
        for m in range(5):
            dw_ref[m, at, :] = terms[:, 128 * m : 128 * m + 128]
        return 0

    lax.fori_loop(0, 6, weights, 0)

    tails = []
    for r in range(6):
        mine = load_rows(dwo_ref, r, 6)
        tails.append(mine[:, 3 * COLS :])
        mine = jnp.concatenate([load_rows(dw_ref, r, 6)[:, : 3 * COLS], mine[:, : 3 * COLS]], axis=1)
        store_rows(sf_ref, r, 8, mine)
        sf_ref[r, pl.ds(7, 128, stride=8), :] = drouter_ref[pl.ds(r, 128, stride=6), :]
    store_rows(sf_ref, 6, 8, jnp.concatenate(tails, axis=1))

    rows = iota((128, WIDTH), 0)
    lanes = iota((128, WIDTH), 1)
    own = sixth(lanes) == rows
    lane = iota((WIDTH, 128), 1)
    part = iota((WIDTH, 128), 0)
    part = part - 6 * sixth(part)
    extra = jnp.zeros((128, 128), f32)
    for base, line in ((0, line_ref[:1, :]), (12, dgain_ref[:1, :])):
        for off, v in zip((0, 6), two_parts(jnp.where(own, line, 0.0))):
            extra = extra + mm(v, (lane == part + base + off).astype(bf16))

    ids = bucket_of(iota((512, 128), 0) - 255)
    flat = iota((512, 128), 1)
    turn = (iota((TOK, TOK), 0) + iota((TOK, TOK), 1) == TOK - 1).astype(f32)
    table = jnp.zeros((8, 128), f32)
    flat_lane = iota((8, 128), 1)
    for h in range(GROUP):
        near = exact(turn, acc_ref[h, :, 6 * TOK : 9 * TOK])
        near = jnp.concatenate([near, jnp.zeros((TOK, TOK), f32)], axis=1)
        near = pltpu.roll(near, 0, 1, stride=1, stride_axis=0)
        diag = jnp.broadcast_to(jnp.sum(near, axis=0, keepdims=True), (8, 512))
        table = table + exact(diag, (flat == ids + 32 * h).astype(f32))
        low = jnp.sum(acc_ref[h, :, : 6 * TOK])
        high = jnp.sum(acc_ref[h, :, 9 * TOK :])
        table = table + jnp.where(flat_lane == 32 * h + 15, low, 0.0)
        table = table + jnp.where(flat_lane == 32 * h + 31, high, 0.0)
    lanes = iota((32, 128), 1)
    mine = third(lanes) == iota((32, 128), 0)
    lane = iota((128, 128), 1)
    part = iota((128, 128), 0)
    part = part - 3 * third(part)
    entries = jnp.zeros((32, 128), f32)
    for off, v in zip((24, 27), two_parts(jnp.where(mine, table[:1], 0.0))):
        entries = entries + mm(v, (lane == part + off).astype(bf16))
    zero = jnp.zeros((32, 128), f32)
    entries = jnp.concatenate([jnp.where(y == q, entries, zero) for q in range(4)], axis=0)
    last = pl.ds(7, 128, stride=8)
    sf_ref[6, last, :] = extra + entries
    sf_ref[7, last, :] = jnp.zeros((128, 128), f32)
    sf_ref[8, last, :] = jnp.zeros((128, 128), f32)
    send_ref[...] = whole(sf_ref, 0, 9).astype(bf16)


def attend_back(idx, go_parts, x_all, h, wqkv, qe, ke, v, band, lse, dwo, drouter, dgain):
    outs = [sds(LEN, PACK), sds(4, TOK, WIDTH, dtype=f32), sds(4, TOK, WIDTH)]
    return call(
        backward_kernel,
        outs,
        [smem] + [vmem] * 15,
        [
            pltpu.VMEM((4, TOK, COLS), bf16),
            pltpu.VMEM((COLS, LEN), f32),
            pltpu.VMEM((COLS, LEN), f32),
            pltpu.VMEM((LEN, 3 * COLS), bf16),
            pltpu.VMEM((GROUP, TOK, BAND), f32),
            pltpu.VMEM((9, LEN, 128), f32),
            pltpu.VMEM((5, WIDTH, 128), f32),
            pltpu.VMEM((8, WIDTH), f32),
        ],
        name="attend_back",
    )(idx, *go_parts, x_all, h, wqkv, qe, ke, v, band, lse, dwo, drouter, dgain)


def pair_kernel(idx_ref, own_ref, got_ref, d0_ref, d1_ref, d2_ref, d3_ref):
    y = idx_ref[0]
    for k, d_ref in enumerate((d0_ref, d1_ref, d2_ref, d3_ref)):
        dst = lax.rem(y + k, 4)
        d_ref[...] = (own_ref[dst] + got_ref[dst].astype(f32)).astype(d_ref.dtype)


def pair_sum(idx, own, got):
    outs = [sds(TOK, WIDTH, dtype=f32)] + [sds(TOK, WIDTH)] * 3
    return call(pair_kernel, outs, [smem, vmem, vmem], name="pair_sum")(idx, own, got)


def tokens_kernel(d0_ref, d1_ref, d2_ref, d3_ref, x_ref, gain_ref, dx1_ref, out_ref):
    dh = d0_ref[...] + d1_ref[...].astype(f32) + d2_ref[...].astype(f32) + d3_ref[...].astype(f32)
    x = x_ref[...].astype(f32)
    r1 = lax.rsqrt(jnp.mean(x * x, axis=-1, keepdims=True) + eps)
    gd = gain_ref[:1, :] * dh
    scaled = x * r1
    out_ref[...] = dx1_ref[...] + r1 * (gd - scaled * jnp.mean(gd * scaled, axis=-1, keepdims=True))


def tokens_last(d_parts, x_own, gains, dx1):
    return call(tokens_kernel, [sds(TOK, WIDTH, dtype=f32)], [vmem] * 7, name="tokens_last")(
        *d_parts, x_own, gains, dx1
    )[0]


def sums_kernel(recv_ref, q_ref, k_ref, v_ref, o_ref, router_ref, small_ref, acc_ref):
    acc_ref[...] = recv_ref[:64, :].astype(f32)

    def add(f, _):
        acc_ref[...] += recv_ref[pl.ds(pl.multiple_of(f * 64, 64), 64), :].astype(f32)
        return 0

    lax.fori_loop(1, 16, add, 0)
    quads = [acc_ref[16 * q : 16 * q + 8, :] + acc_ref[16 * q + 8 : 16 * q + 16, :] for q in range(4)]
    for m, ref in enumerate((q_ref, k_ref, v_ref)):
        whole = jnp.concatenate([a[:, COLS * m : COLS * m + COLS] for a in quads], axis=1)
        ref[...] = whole[:6].astype(bf16)
    every = quads[0] + quads[1] + quads[2] + quads[3]
    tail = [every[6:7, 192 * r : 192 * r + 192] for r in range(6)]
    o_ref[:, : 3 * COLS] = every[:6, 3 * COLS :].astype(bf16)
    o_ref[:, 3 * COLS :] = jnp.concatenate(tail, axis=0).astype(bf16)
    router = [every[7:8, 128 * r : 128 * r + 128] for r in range(6)]
    router_ref[...] = jnp.concatenate(router, axis=0).astype(bf16)
    small_ref[...] = every[:, WIDTH : WIDTH + 128]


def sums_last(recv):
    outs = [sds(6, WIDTH)] * 4 + [sds(6, 128), sds(8, 128, dtype=f32)]
    return call(sums_kernel, outs, [vmem], [pltpu.VMEM((64, PACK), f32)], name="sums_last")(recv)


def along_y(v, k):
    return lax.ppermute(v, "seq", [(s, (s + 2 * k) % 8) for s in range(8)])


def every_device(v):
    return lax.all_to_all(v, BOTH, split_axis=0, concat_axis=0, tiled=True)


def on_device(
    tokens, segments, routes, gain_attn, w_query, w_key, w_value, w_output, rel_table, gain_moe,
    w_router, w_inner, w_outer, cotangent,
):
    seq = lax.axis_index("seq")
    idx = jnp.stack([seq // 2, seq % 2]).astype(jnp.int32)
    x_all = lax.all_gather(tokens, "seq", axis=0, tiled=True)

    qkv = jnp.stack([w_query, w_key, w_value]).reshape(3, 6, 4, COLS)
    qkv = qkv.transpose(2, 1, 0, 3).reshape(4, 6, 3 * COLS)
    left = jnp.broadcast_to(w_output[None, :, : 3 * COLS], (4, 6, 3 * COLS))
    six = jnp.concatenate([qkv, left], axis=2)
    row6 = w_output[:, 3 * COLS :].reshape(1, 1, PACK)
    row7 = jnp.concatenate(
        [
            w_router.reshape(-1), gain_attn, gain_moe, rel_table,
            jnp.zeros((PACK - WIDTH - 15,), bf16),
        ]
    ).reshape(1, 1, PACK)
    two = jnp.broadcast_to(jnp.concatenate([row6, row7], axis=1), (4, 2, PACK))
    eight = jnp.concatenate([six, two], axis=1)
    pack = jnp.broadcast_to(eight[None, :, None], (16, 4, 2, 8, PACK)).reshape(LEN, PACK)
    pack = every_device(pack)

    attended = attend(idx, x_all, pack, segments.reshape(LEN, 1))
    o_parts = attended[:4]
    h, wqkv, wo, router, gains, qe, ke, v, band, lse = attended[4:]
    o_parts = [o_parts[0]] + [along_y(o_parts[k], k) for k in (1, 2, 3)]
    x1, h2, prob, hot, send = dispatch(
        idx, tokens, o_parts, wo, router, gains, routes, cotangent
    )
    ret, grad_inner, grad_outer = experts(every_device(send), w_inner, w_outer)
    back = every_device(ret)
    layer_out, dx1, *rest = returned(
        idx, back, x1, h2, prob, hot, cotangent, router, gains, wo, o_parts
    )
    go_parts = [rest[0]] + [along_y(rest[k], k) for k in (1, 2, 3)]
    dwo, drouter, dgain = rest[4:]
    terms, own, other = attend_back(
        idx, go_parts, x_all, h, wqkv, qe, ke, v, band, lse, dwo, drouter, dgain
    )
    got = lax.ppermute(other, "seq", [(s, s ^ 1) for s in range(8)])
    d_parts = pair_sum(idx, own, got)
    d_parts = [d_parts[0]] + [along_y(d_parts[k], k) for k in (1, 2, 3)]
    dq, dk, dv, do, dr, small = sums_last(every_device(terms))
    tokens_grad = tokens_last(d_parts, tokens, gains, dx1)
    line = small[7]
    return (
        layer_out,
        tokens_grad,
        (line[0:6] + line[6:12]).astype(bf16),
        dq,
        dk,
        dv,
        do,
        (line[24:27] + line[27:30]).astype(bf16),
        (line[12:18] + line[18:24]).astype(bf16),
        dr,
        grad_inner,
        grad_outer,
    )


def solution(mesh):
    rows = P(BOTH, None)
    flat = P(BOTH)
    cube = P(BOTH, None, None)
    return jax.shard_map(
        on_device,
        mesh=mesh,
        in_specs=(
            rows, P("fsdp", None), rows, flat, rows, rows, rows, rows, flat, flat, rows, cube, cube,
            rows,
        ),
        out_specs=(rows, rows, flat, rows, rows, rows, rows, flat, flat, rows, cube, cube),
        check_vma=False,
    )
```

```python
import functools

import jax
import jax.numpy as jnp
from jax import lax
from jax.experimental import pallas as pl
from jax.experimental.pallas import tpu as pltpu
from jax.sharding import PartitionSpec as P

bf16 = jnp.bfloat16
f32 = jnp.float32

WIDTH = 768
TOK = 128
LEN = 1024
FF = 3072
GROUP = 3
HD = 64
COLS = GROUP * HD
BAND = 5 * TOK
HALF = WIDTH // 2
PACK = 896
SENT = 640
LATE = 512
FF_TILE = 512
eps = 1e-06
bucket_edges = (12, 16, 23, 32, 46, 64, 91)
BOTH = ("fsdp", "seq")


def params(mib):
    return pltpu.CompilerParams(vmem_limit_bytes=mib << 20)


smem = pl.BlockSpec(memory_space=pltpu.SMEM)
vmem = pl.BlockSpec(memory_space=pltpu.VMEM)


def iota(shape, dim):
    return lax.broadcasted_iota(jnp.int32, shape, dim)


def sixth(n):
    return (n * 10923) >> 16


def third(n):
    return (n * 21846) >> 16


def bucket_of(offsets):
    spread = jnp.abs(offsets)
    ids = (offsets > 0).astype(jnp.int32) * 16 + jnp.minimum(spread, 8)
    for border in bucket_edges:
        ids = ids + (spread >= border).astype(jnp.int32)
    return ids


def mm(a, b):
    return jnp.dot(a, b, preferred_element_type=f32)


def mm_nt(a, b):
    return lax.dot_general(a, b, (((1,), (1,)), ((), ())), preferred_element_type=f32)


def mm_tn(a, b):
    return lax.dot_general(a, b, (((0,), (0,)), ((), ())), preferred_element_type=f32)


def exact(a, b):
    return lax.dot_general(
        a,
        b,
        (((1,), (0,)), ((), ())),
        precision=lax.Precision.HIGHEST,
        preferred_element_type=f32,
    )


def cost(us):
    return pl.CostEstimate(flops=int(us * 1.15e9), bytes_accessed=1 << 20, transcendentals=0)


def call(kernel, outs, ins, scratch=(), mib=16, us=2, **kw):
    return pl.pallas_call(
        kernel,
        out_shape=outs,
        in_specs=ins,
        out_specs=jax.tree.map(lambda _: vmem, outs),
        scratch_shapes=list(scratch),
        compiler_params=params(mib),
        cost_estimate=cost(us),
        **kw,
    )


def load_rows(ref, start, stride):
    return jnp.concatenate(
        [ref[j, pl.ds(start, 128, stride=stride), :] for j in range(ref.shape[0])], axis=1
    )


def store_rows(ref, start, stride, value):
    for j in range(value.shape[1] // 128):
        ref[j, pl.ds(start, 128, stride=stride), :] = value[:, 128 * j : 128 * j + 128]


def whole(ref, first, last):
    return jnp.concatenate([ref[j] for j in range(first, last)], axis=1)


def fill(ref, value):
    for j in range(ref.shape[0]):
        ref[j] = value[:, 128 * j : 128 * j + 128].astype(f32)


def sds(*shape, dtype=bf16):
    return jax.ShapeDtypeStruct(shape, dtype)


def pack_kernel(q_ref, k_ref, v_ref, o_ref, r_ref, small_ref, out_ref):
    zero = jnp.zeros((2, 576), f32)
    q, k, v, o, r = (ref[...].astype(f32) for ref in (q_ref, k_ref, v_ref, o_ref, r_ref))
    small = small_ref[...].astype(f32)
    blocks = []
    for y in range(4):
        at = slice(COLS * y, COLS * y + COLS)
        three = jnp.concatenate([q[:, at], k[:, at], v[:, at]], axis=1)
        for c in range(2):
            left = o[:, HALF * c : HALF * c + 320]
            right = [o[i : i + 1, HALF * c + 320 : HALF * c + HALF] for i in range(6)]
            routed = [r[i : i + 1, 64 * c : 64 * c + 64] for i in range(6)]
            row6 = jnp.concatenate(right + routed + [small], axis=1)
            six = jnp.concatenate([three, left], axis=1)
            blocks.append(jnp.concatenate([six, row6, jnp.zeros((1, PACK), f32)], axis=0))
    block = jnp.concatenate(blocks, axis=0).astype(bf16)
    for f in range(16):
        out_ref[64 * f : 64 * f + 64, :] = block


def pack_weights(w_query, w_key, w_value, w_output, w_router, small):
    return call(pack_kernel, [sds(LEN, PACK)], [vmem] * 6, name="pack_weights", mib=56)(
        w_query, w_key, w_value, w_output, w_router, small
    )[0]


def unpack_kernel(
    idx_ref, pack_ref, wqkv_ref, half_ref, gain_ref, band_ref, pf_ref, wf_ref, tail_ref
):
    y = idx_ref[0]
    fill(pf_ref, pack_ref)
    for r in range(6):
        store_rows(wf_ref, r, 6, load_rows(pf_ref, r, 8))
    row6 = load_rows(pf_ref, 6, 8)
    for r in range(6):
        tail = [row6[:, 64 * r : 64 * r + 64], row6[:, HALF + 64 * r : HALF + 64 * r + 64]]
        tail_ref[pl.ds(r, 128, stride=6), :] = jnp.concatenate(tail, axis=1)
    wqkv_ref[...] = whole(wf_ref, 0, 5)[:, : 3 * COLS].astype(bf16)
    left = whole(wf_ref, 4, 7)[:, 64:]
    blank = jnp.zeros((WIDTH, 64), f32)
    half_ref[...] = jnp.concatenate([left, tail_ref[...], blank], axis=1).astype(bf16)
    small = row6[:, WIDTH:].astype(bf16)

    lanes = iota((128, WIDTH), 1)
    rows = iota((128, WIDTH), 0)
    own = sixth(lanes) == rows
    within = lanes - 6 * sixth(lanes)
    gains = []
    for base in (0, 6):
        spread = mm(small, (rows == within + base).astype(bf16))
        gains.append(jnp.sum(jnp.where(own, spread, 0.0), axis=0, keepdims=True))
    gain_ref[...] = jnp.concatenate([gains[0], gains[1], jnp.zeros((6, WIDTH), f32)], axis=0)
    lanes = iota((128, 384), 1)
    rows = iota((128, 384), 0)
    spread = mm(small, (rows == lanes - 3 * third(lanes) + 12).astype(bf16))
    table = jnp.sum(jnp.where(third(lanes) == rows, spread, 0.0), axis=0, keepdims=True)
    table = jnp.broadcast_to(table, (8, 384)).astype(bf16)
    ids = bucket_of(iota((384, 512), 1) - 255)
    entry = iota((384, 512), 0)
    for h in range(GROUP):
        hot = (entry == ids + 32 * (3 * y + h)).astype(bf16)
        line = mm(table, hot)[:1]
        wide = pltpu.roll(
            jnp.broadcast_to(line, (TOK, 512)), 385, 1, stride=1, stride_axis=0
        )
        band_ref[h, :, :TOK] = jnp.broadcast_to(line[:, :1], (TOK, TOK))
        band_ref[h, :, TOK : 4 * TOK] = wide[:, : 3 * TOK]
        band_ref[h, :, 4 * TOK :] = jnp.broadcast_to(line[:, 511:], (TOK, TOK))


def unpack_weights(idx, pack):
    outs = [
        sds(WIDTH, 3 * COLS), sds(WIDTH, 512), sds(8, WIDTH, dtype=f32),
        sds(GROUP, TOK, BAND, dtype=f32),
    ]
    return call(
        unpack_kernel,
        outs,
        [smem, vmem],
        [
            pltpu.VMEM((7, LEN, 128), f32),
            pltpu.VMEM((7, WIDTH, 128), f32),
            pltpu.VMEM((WIDTH, 128), f32),
        ],
        name="unpack_weights",
        mib=56,
        us=4,
    )(idx, pack)


def banded(band_ref, h, pq):
    parts = []
    for j in range(8):
        at = jnp.clip(j - pq + 2, 0, 4) * TOK
        parts.append(band_ref[h, :, pl.ds(pl.multiple_of(at, TOK), TOK)])
    return jnp.concatenate(parts, axis=1)


def attend_kernel(
    idx_ref, x_ref, seg_ref, wqkv_ref, gain_ref, band_ref,
    o0_ref, o1_ref, o2_ref, o3_ref, h_ref, qe_ref, ke_ref, v_ref, lse_ref,
    os_ref,
):
    y, c = idx_ref[0], idx_ref[1]
    gain = gain_ref[:1, :]

    def project(i, _):
        at = pl.ds(pl.multiple_of(i * TOK, TOK), TOK)
        x = x_ref[at, :].astype(f32)
        hb = (x * lax.rsqrt(jnp.mean(x * x, axis=-1, keepdims=True) + eps) * gain).astype(bf16)
        h_ref[at, :] = hb
        qkv = mm(hb, wqkv_ref[...])
        doc = seg_ref[at, :]
        lane = iota((TOK, HD), 1)
        same = lane == doc
        q_mark = jnp.where(same, -1e30, 0.0)
        k_mark = jnp.where((lane < 3) & jnp.logical_not(same), 1.0, 0.0)
        q_parts, k_parts = [], []
        for h in range(GROUP):
            q = qkv[:, HD * h : HD * h + HD]
            k = qkv[:, COLS + HD * h : COLS + HD * h + HD]
            q_parts += [q.astype(bf16).astype(f32) * 0.125, q_mark]
            k_parts += [k, k_mark]
        qe_ref[at, :] = jnp.concatenate(q_parts, axis=1).astype(bf16)
        ke_ref[at, :] = jnp.concatenate(k_parts, axis=1).astype(bf16)
        v_ref[at, :] = qkv[:, 2 * COLS :].astype(bf16)
        return 0

    lax.fori_loop(0, 8, project, 0)

    def attend(k, _):
        yq = lax.rem(y + k, 4)
        pq = 2 * yq + c
        at = pl.ds(pl.multiple_of(pq * TOK, TOK), TOK)
        lane = iota((TOK, 128), 1)
        lse_all = jnp.zeros((TOK, 128), f32)
        outs = []
        for h in range(GROUP):
            s = mm_nt(qe_ref[at, 128 * h : 128 * h + 128], ke_ref[:, 128 * h : 128 * h + 128])
            s = s + banded(band_ref, h, pq)
            top = jnp.max(s, axis=-1, keepdims=True)
            e = jnp.exp(s - top)
            total = jnp.sum(e, axis=-1, keepdims=True)
            p = (e * (1.0 / total)).astype(bf16)
            outs.append(mm(p, v_ref[:, HD * h : HD * h + HD]))
            lse_all = jnp.where(lane == h, top + jnp.log(total), lse_all)
        os_ref[k] = jnp.concatenate(outs, axis=1).astype(bf16)
        lse_ref[yq] = lse_all
        return 0

    lax.fori_loop(0, 4, attend, 0)
    o0_ref[...] = os_ref[0]
    o1_ref[...] = os_ref[1]
    o2_ref[...] = os_ref[2]
    o3_ref[...] = os_ref[3]


def attend(idx, x_all, seg_col, wqkv, gains, band):
    outs = [sds(TOK, COLS)] * 4 + [
        sds(LEN, WIDTH), sds(LEN, 384), sds(LEN, 384), sds(LEN, COLS),
        sds(4, TOK, 128, dtype=f32),
    ]
    return call(
        attend_kernel,
        outs,
        [smem] + [vmem] * 5,
        [pltpu.VMEM((4, TOK, COLS), bf16)],
        name="attend",
        mib=56,
        us=12,
    )(idx, x_all, seg_col, wqkv, gains, band)


def dispatch_kernel(
    idx_ref, x_ref, o0_ref, o1_ref, o2_ref, o3_ref, half_ref, rest_ref, gain_ref,
    route_ref, cot_ref,
    x1_ref, h2_ref, prob_ref, hot_ref, send_ref, wo_ref, router_ref,
    sf_ref,
):
    y, c = idx_ref[0], idx_ref[1]
    wo_ref[:, pl.ds(pl.multiple_of(c * HALF, 128), HALF)] = half_ref[:, :HALF]
    wo_ref[:, pl.ds(pl.multiple_of((1 - c) * HALF, 128), HALF)] = rest_ref[:, :HALF]
    here = half_ref[:, HALF : HALF + 128].astype(f32)[:, :64]
    there = rest_ref[:, HALF : HALF + 128].astype(f32)[:, :64]
    router_ref[...] = jnp.where(
        c == 0,
        jnp.concatenate([here, there], axis=1),
        jnp.concatenate([there, here], axis=1),
    ).astype(bf16)
    x1 = x_ref[...].astype(f32)
    for k, o_ref in enumerate((o0_ref, o1_ref, o2_ref, o3_ref)):
        src = lax.rem(y + 4 - k, 4)
        x1 = x1 + mm(o_ref[...], wo_ref[pl.ds(pl.multiple_of(src * COLS, COLS), COLS), :])
    x1_ref[...] = x1
    r2 = lax.rsqrt(jnp.mean(x1 * x1, axis=-1, keepdims=True) + eps)
    h2 = (x1 * r2 * gain_ref[1:2, :]).astype(bf16)
    h2_ref[...] = h2
    logits = mm(h2, router_ref[...])
    e = jnp.exp(logits - jnp.max(logits, axis=-1, keepdims=True))
    prob = e / jnp.sum(e, axis=-1, keepdims=True)
    prob_ref[...] = prob
    expert = iota((TOK, 128), 1)
    picked = (route_ref[...] == expert).astype(f32)
    gate = jnp.sum(prob * picked, axis=-1, keepdims=True)
    earlier = (iota((TOK, TOK), 0) > iota((TOK, TOK), 1)).astype(bf16)
    slot = jnp.sum(mm(earlier, picked.astype(bf16)) * picked, axis=-1, keepdims=True)
    geo = (gate * cot_ref[...].astype(f32)).astype(bf16)
    for s in range(2):
        hot = jnp.where((slot > 0.5) == (s == 1), picked, 0.0).astype(bf16)
        hot_ref[s] = hot
        for kind, src in enumerate((h2, geo)):
            placed = mm_tn(hot, src)
            for half in range(2):
                part = placed[:, HALF * half : HALF * half + HALF]
                store_rows(sf_ref, kind * 4 + s * 2 + half, 8, part)
    send_ref[...] = whole(sf_ref, 0, 3).astype(bf16)


def dispatch(idx, x_own, o_parts, half, rest, gains, route_col, cot):
    outs = [
        sds(TOK, WIDTH, dtype=f32), sds(TOK, WIDTH), sds(TOK, 128, dtype=f32),
        sds(2, TOK, 128), sds(LEN, HALF), sds(WIDTH, WIDTH), sds(WIDTH, 128),
    ]
    return call(
        dispatch_kernel,
        outs,
        [smem] + [vmem] * 10,
        [pltpu.VMEM((3, LEN, 128), f32)],
        name="dispatch",
        mib=10,
    )(idx, x_own, *o_parts, half, rest, gains, route_col, cot)


def expert_kernel(
    recv_ref, wi_ref, wo_ref, ret_ref, gi_ref, go_ref, rf_ref, x_ref, xt_ref, g_ref, eo_ref, gx_ref
):
    step = pl.program_id(0)

    @pl.when(step == 0)
    def _():
        fill(rf_ref, recv_ref)
        for kind, dst in enumerate((x_ref, g_ref)):
            for s in range(2):
                for half in range(2):
                    dst[TOK * s : TOK * s + TOK, HALF * half : HALF * half + HALF] = load_rows(
                        rf_ref, kind * 4 + s * 2 + half, 8
                    ).astype(bf16)
        xt_ref[...] = x_ref[...].T
        eo_ref[...] = jnp.zeros_like(eo_ref)
        gx_ref[...] = jnp.zeros_like(gx_ref)

    wi = wi_ref[...]
    wo = wo_ref[...]
    g = g_ref[...]
    a = mm(x_ref[...], wi)
    cc = 0.7978845608028654
    sq = a * a
    t = jnp.tanh(cc * (a + 0.044715 * (sq * a)))
    u = (0.5 * a * (1.0 + t)).astype(bf16)
    slope = 0.5 * (1.0 + t) + (0.5 * cc) * a * (1.0 - t * t) * (1.0 + 0.134145 * sq)
    eo_ref[...] += mm(u, wo)
    ga = (mm_nt(g, wo) * slope).astype(bf16)
    go_ref[...] = mm_tn(u, g).astype(bf16)
    gi_ref[...] = mm(xt_ref[...], ga).astype(bf16)
    gx_ref[...] += mm_nt(ga, wi)

    @pl.when(step == FF // FF_TILE - 1)
    def _():
        for kind, src in enumerate((eo_ref, gx_ref)):
            for s in range(2):
                for half in range(2):
                    part = src[TOK * s : TOK * s + TOK, HALF * half : HALF * half + HALF]
                    store_rows(rf_ref, kind * 4 + s * 2 + half, 8, part)
        ret_ref[...] = whole(rf_ref, 0, 3).astype(bf16)


def experts(recv, w_inner, w_outer):
    return pl.pallas_call(
        expert_kernel,
        grid=(FF // FF_TILE,),
        out_shape=[sds(LEN, HALF), sds(1, WIDTH, FF), sds(1, FF, WIDTH)],
        in_specs=[
            pl.BlockSpec((LEN, HALF), lambda i: (0, 0)),
            pl.BlockSpec((None, WIDTH, FF_TILE), lambda i: (0, 0, i)),
            pl.BlockSpec((None, FF_TILE, WIDTH), lambda i: (0, i, 0)),
        ],
        out_specs=[
            pl.BlockSpec((LEN, HALF), lambda i: (0, 0)),
            pl.BlockSpec((None, WIDTH, FF_TILE), lambda i: (0, 0, i)),
            pl.BlockSpec((None, FF_TILE, WIDTH), lambda i: (0, i, 0)),
        ],
        scratch_shapes=[
            pltpu.VMEM((3, LEN, 128), f32),
            pltpu.VMEM((2 * TOK, WIDTH), bf16),
            pltpu.VMEM((WIDTH, 2 * TOK), bf16),
            pltpu.VMEM((2 * TOK, WIDTH), bf16),
            pltpu.VMEM((2 * TOK, WIDTH), f32),
            pltpu.VMEM((2 * TOK, WIDTH), f32),
        ],
        compiler_params=params(56),
        cost_estimate=cost(14),
        name="experts",
    )(recv, w_inner, w_outer)


def return_kernel(
    idx_ref, back_ref, x1_ref, h2_ref, prob_ref, hot_ref, cot_ref, router_ref, gain_ref, wo_ref,
    o0_ref, o1_ref, o2_ref, o3_ref,
    out_ref, dx1_ref, g0_ref, g1_ref, g2_ref, g3_ref, keep_ref, give_ref, dgain_ref,
    bf_ref,
):
    y, c = idx_ref[0], idx_ref[1]
    fill(bf_ref, back_ref)
    parts = []
    for kind in range(2):
        halves = []
        for half in range(2):
            got = jnp.zeros((TOK, HALF), f32)
            for s in range(2):
                rows = load_rows(bf_ref, kind * 4 + s * 2 + half, 8).astype(bf16)
                got = got + mm(hot_ref[s], rows)
            halves.append(got)
        parts.append(jnp.concatenate(halves, axis=1))
    eo, gx = parts
    x1 = x1_ref[...]
    prob = prob_ref[...]
    picked = hot_ref[0].astype(f32) + hot_ref[1].astype(f32)
    gate = jnp.sum(prob * picked, axis=-1, keepdims=True)
    out_ref[...] = (x1 + gate * eo).astype(bf16)
    dy = cot_ref[...].astype(f32)
    dgate = jnp.sum(dy * eo, axis=-1, keepdims=True)
    gz = (dgate * gate * (picked - prob)).astype(bf16)
    dh2 = gx + mm_nt(gz, router_ref[...])
    routed = mm_tn(h2_ref[...], gz)
    blank = jnp.zeros((WIDTH, 64), f32)
    near = jnp.concatenate([routed[:, :64], blank], axis=1)
    far = jnp.concatenate([routed[:, 64:], blank], axis=1)
    keep_ref[:, HALF:] = jnp.where(c == 0, near, far).astype(bf16)
    give_ref[:, HALF:] = jnp.where(c == 0, far, near).astype(bf16)
    r2 = lax.rsqrt(jnp.mean(x1 * x1, axis=-1, keepdims=True) + eps)
    scaled = x1 * r2
    dgain = jnp.sum(dh2 * scaled, axis=0, keepdims=True)
    dgain_ref[...] = jnp.broadcast_to(dgain, (8, WIDTH))
    gd = gain_ref[1:2, :] * dh2
    dx1 = dy + r2 * (gd - scaled * jnp.mean(gd * scaled, axis=-1, keepdims=True))
    dx1_ref[...] = dx1
    gw = dx1.astype(bf16)
    for k, g_ref in enumerate((g0_ref, g1_ref, g2_ref, g3_ref)):
        dst = lax.rem(y + k, 4)
        rows = wo_ref[pl.ds(pl.multiple_of(dst * COLS, COLS), COLS), :]
        g_ref[...] = mm_nt(gw, rows).astype(bf16)
    for k, o_ref in enumerate((o0_ref, o1_ref, o2_ref, o3_ref)):
        src = lax.rem(y + 4 - k, 4)
        rows = pl.ds(pl.multiple_of(src * COLS, COLS), COLS)
        terms = mm_tn(o_ref[...], gw)
        near, far = terms[:, :HALF], terms[:, HALF:]
        keep_ref[rows, :HALF] = jnp.where(c == 0, near, far).astype(bf16)
        give_ref[rows, :HALF] = jnp.where(c == 0, far, near).astype(bf16)


def returned(idx, back, x1, h2, prob, hot, cot, router, gains, wo, o_parts):
    outs = (
        [sds(TOK, WIDTH), sds(TOK, WIDTH, dtype=f32)]
        + [sds(TOK, COLS)] * 4
        + [sds(WIDTH, LATE), sds(WIDTH, LATE), sds(8, WIDTH, dtype=f32)]
    )
    return call(
        return_kernel,
        outs,
        [smem] + [vmem] * 13,
        [pltpu.VMEM((3, LEN, 128), f32)],
        name="returned",
        mib=14,
    )(idx, back, x1, h2, prob, hot, cot, router, gains, wo, *o_parts)


def backward_kernel(
    idx_ref, g0_ref, g1_ref, g2_ref, g3_ref, x_ref, wqkv_ref, qe_ref, ke_ref, v_ref,
    band_ref, lse_ref,
    own_ref, other_ref, dq_ref, line_ref, acc_ref,
    gs_ref, gk_ref, gv_ref,
):
    y, c = idx_ref[0], idx_ref[1]
    for k, g_ref in enumerate((g0_ref, g1_ref, g2_ref, g3_ref)):
        gs_ref[k] = g_ref[...]
    gk_ref[...] = jnp.zeros_like(gk_ref)
    gv_ref[...] = jnp.zeros_like(gv_ref)
    acc_ref[...] = jnp.zeros_like(acc_ref)

    def block(k, _):
        yq = lax.rem(y + 4 - k, 4)
        pq = 2 * yq + c
        at = pl.ds(pl.multiple_of(pq * TOK, TOK), TOK)
        not_at = pl.ds(pl.multiple_of((pq + 1 - 2 * c) * TOK, TOK), TOK)
        lse = lse_ref[yq]
        go = gs_ref[k]
        outs = []
        for h in range(GROUP):
            q = qe_ref[at, 128 * h : 128 * h + 128]
            keys = ke_ref[:, 128 * h : 128 * h + 128]
            g = go[:, HD * h : HD * h + HD]
            s = mm_nt(q, keys) + banded(band_ref, h, pq)
            p = jnp.exp(s - lse[:, h : h + 1])
            pd = p * mm_nt(g, v_ref[:, HD * h : HD * h + HD])
            gs = pd - p * jnp.sum(pd, axis=-1, keepdims=True)
            for j in range(8):
                to = pl.multiple_of(jnp.clip(j - pq + 2, 0, 4) * TOK, TOK)
                acc_ref[h, :, pl.ds(to, TOK)] += gs[:, TOK * j : TOK * j + TOK]
            low = gs.astype(bf16)
            outs.append(mm(low, keys)[:, :HD] * 0.125)
            gk_ref[HD * h : HD * h + HD, :] += mm_tn(q, low)[:HD]
            gv_ref[HD * h : HD * h + HD, :] += mm_tn(g, p.astype(bf16))
        dq_ref[at, :COLS] = jnp.concatenate(outs, axis=1).astype(bf16)
        dq_ref[not_at, :COLS] = jnp.zeros((TOK, COLS), bf16)
        return 0

    lax.fori_loop(0, 4, block, 0)
    dq_ref[:, COLS : 2 * COLS] = gk_ref[...].T.astype(bf16)
    dq_ref[:, 2 * COLS :] = gv_ref[...].T.astype(bf16)
    line_ref[...] = jnp.zeros_like(line_ref)

    def spread(yq, _):
        lines = jnp.zeros((1, WIDTH), f32)
        for side in range(2):
            pq = 2 * yq + (c if side == 0 else 1 - c)
            at = pl.ds(pl.multiple_of(pq * TOK, TOK), TOK)
            d = mm_nt(dq_ref[at, :], wqkv_ref[...])
            x = x_ref[at, :].astype(f32)
            r1 = lax.rsqrt(jnp.mean(x * x, axis=-1, keepdims=True) + eps)
            lines = lines + jnp.sum(d * (x * r1), axis=0, keepdims=True)
            if side == 0:
                own_ref[yq] = d
            else:
                other_ref[yq] = d.astype(bf16)
        line_ref[...] += jnp.broadcast_to(lines, (8, WIDTH))
        return 0

    lax.fori_loop(0, 4, spread, 0)


def attend_back(idx, go_parts, x_all, wqkv, qe, ke, v, band, lse):
    outs = [
        sds(4, TOK, WIDTH, dtype=f32), sds(4, TOK, WIDTH), sds(LEN, 3 * COLS),
        sds(8, WIDTH, dtype=f32), sds(GROUP, TOK, BAND, dtype=f32),
    ]
    return call(
        backward_kernel,
        outs,
        [smem] + [vmem] * 11,
        [
            pltpu.VMEM((4, TOK, COLS), bf16),
            pltpu.VMEM((COLS, LEN), f32),
            pltpu.VMEM((COLS, LEN), f32),
        ],
        name="attend_back",
        mib=24,
        us=12,
    )(idx, *go_parts, x_all, wqkv, qe, ke, v, band, lse)


def terms_kernel(
    idx_ref, h_ref, dq_ref, line_ref, dgain_ref, acc_ref, keep_ref, got_ref, send_ref
):
    y = idx_ref[0]
    ids = bucket_of(iota((512, 128), 0) - 255)
    flat = iota((512, 128), 1)
    turn = (iota((TOK, TOK), 0) + iota((TOK, TOK), 1) == TOK - 1).astype(f32)
    table = jnp.zeros((8, 128), f32)
    flat_lane = iota((8, 128), 1)
    for h in range(GROUP):
        near = exact(turn, acc_ref[h, :, TOK : 4 * TOK])
        near = jnp.concatenate([near, jnp.zeros((TOK, TOK), f32)], axis=1)
        near = pltpu.roll(near, 0, 1, stride=1, stride_axis=0)
        diag = jnp.broadcast_to(jnp.sum(near, axis=0, keepdims=True), (8, 512))
        table = table + exact(diag, (flat == ids + 32 * h).astype(f32))
        low = jnp.sum(acc_ref[h, :, :TOK])
        high = jnp.sum(acc_ref[h, :, 4 * TOK :])
        table = table + jnp.where(flat_lane == 32 * h + 15, low, 0.0)
        table = table + jnp.where(flat_lane == 32 * h + 31, high, 0.0)
    lanes = iota((128, WIDTH), 1)
    entry = iota((128, WIDTH), 0)
    group = sixth(lanes)
    within = lanes - 6 * group
    place = (within < 3) & (entry + 96 * y == 3 * group + within) & (entry < 96)
    table = exact(table, place.astype(f32))
    lines = []
    for v in (line_ref[:1, :], dgain_ref[:1, :], table[:1, :]):
        high = v.astype(bf16).astype(f32)
        lines += [high, v - high]
    block = jnp.concatenate(lines + [jnp.zeros((122, WIDTH), f32)], axis=0).T
    block = jnp.concatenate([jnp.zeros((WIDTH, 64), f32), block[:, :64]], axis=1)
    send_ref[:, 512:SENT] = block.astype(bf16)
    send_ref[:, SENT:] = (keep_ref[...].astype(f32) + got_ref[...].astype(f32)).astype(bf16)

    def weights(j, _):
        at = pl.ds(pl.multiple_of(j * 128, 128), 128)
        terms = mm_tn(h_ref[:, at], dq_ref[...])
        send_ref[at, :512] = terms[:, :512].astype(bf16)
        extra = send_ref[at, 512:SENT].astype(f32)
        last = jnp.concatenate([terms[:, 512:], extra[:, 64:]], axis=1)
        send_ref[at, 512:SENT] = last.astype(bf16)
        return 0

    lax.fori_loop(0, 6, weights, 0)


def weight_terms(idx, h, dq, line, dgain, acc, keep, got):
    return call(
        terms_kernel,
        [sds(WIDTH, SENT + LATE)],
        [smem] + [vmem] * 7,
        name="weight_terms",
        mib=14,
        us=5,
    )(idx, h, dq, line, dgain, acc, keep, got)[0]


def pair_kernel(idx_ref, own_ref, got_ref, d0_ref, d1_ref, d2_ref, d3_ref):
    y = idx_ref[0]
    for k, d_ref in enumerate((d0_ref, d1_ref, d2_ref, d3_ref)):
        dst = lax.rem(y + k, 4)
        d_ref[...] = (own_ref[dst] + got_ref[dst].astype(f32)).astype(d_ref.dtype)


def pair_sum(idx, own, got):
    outs = [sds(TOK, WIDTH, dtype=f32)] + [sds(TOK, WIDTH)] * 3
    return call(pair_kernel, outs, [smem, vmem, vmem], name="pair_sum")(idx, own, got)


def tokens_kernel(d0_ref, d1_ref, d2_ref, d3_ref, x_ref, gain_ref, dx1_ref, out_ref):
    dh = d0_ref[...] + d1_ref[...].astype(f32) + d2_ref[...].astype(f32) + d3_ref[...].astype(f32)
    x = x_ref[...].astype(f32)
    r1 = lax.rsqrt(jnp.mean(x * x, axis=-1, keepdims=True) + eps)
    gd = gain_ref[:1, :] * dh
    scaled = x * r1
    out_ref[...] = dx1_ref[...] + r1 * (gd - scaled * jnp.mean(gd * scaled, axis=-1, keepdims=True))


def tokens_last(d_parts, x_own, gains, dx1):
    return call(tokens_kernel, [sds(TOK, WIDTH, dtype=f32)], [vmem] * 7, name="tokens_last")(
        *d_parts, x_own, gains, dx1
    )[0]


def middle_kernel(got_ref, out_ref):
    def total(a, b):
        sums = got_ref[:48, a:b].astype(f32)
        for f in range(1, 16):
            sums = sums + got_ref[48 * f : 48 * f + 48, a:b].astype(f32)
        return sums

    pieces = [total(0, 512)]
    last = total(512, SENT)
    lane = iota((48, 128), 1)
    both = last + pltpu.roll(last, 127, 1)
    high = both.astype(bf16).astype(f32)
    rest = pltpu.roll(both - high, 1, 1)
    last = jnp.where(lane < 64, last, jnp.where(lane % 2 == 0, high, rest))
    pieces += [last, total(SENT, SENT + LATE)]
    sums = jnp.concatenate(pieces, axis=1)
    blank = jnp.zeros((2, SENT + LATE), f32)
    rows = []
    for s in range(8):
        rows += [sums[6 * s : 6 * s + 6], blank]
    out_ref[...] = jnp.concatenate(rows, axis=0).astype(bf16)


def middle_sums(got):
    return call(middle_kernel, [sds(64, SENT + LATE)], [vmem], name="middle_sums", mib=8)(got)[0]


def sums_kernel(recv_ref, q_ref, k_ref, v_ref, o_ref, router_ref, small_ref):
    got = recv_ref[...].astype(f32)
    parts = [got[8 * s : 8 * s + 8] for s in range(8)]
    quads = [parts[2 * y] + parts[2 * y + 1] for y in range(4)]
    for m, ref in enumerate((q_ref, k_ref, v_ref)):
        cols = jnp.concatenate([a[:, COLS * m : COLS * m + COLS] for a in quads], axis=1)
        ref[...] = cols[:6].astype(bf16)
    halves = [parts[c] + parts[2 + c] + parts[4 + c] + parts[6 + c] for c in range(2)]
    o_ref[...] = jnp.concatenate([a[:6, SENT : SENT + HALF] for a in halves], axis=1).astype(bf16)
    routed = [a[:6, SENT + HALF : SENT + HALF + 64] for a in halves]
    router_ref[...] = jnp.concatenate(routed, axis=1).astype(bf16)
    small_ref[...] = halves[0][:, 512:SENT] + halves[1][:, 512:SENT]


def sums_last(recv):
    outs = [sds(6, WIDTH)] * 4 + [sds(6, 128), sds(8, 128, dtype=f32)]
    return call(sums_kernel, outs, [vmem], name="sums_last", mib=4)(recv)


def along_y(v, k):
    return lax.ppermute(v, "seq", [(s, (s + 2 * k) % 8) for s in range(8)])


def exchange(v, axes):
    return lax.all_to_all(v, axes, split_axis=0, concat_axis=0, tiled=True)


def other_core(v):
    return lax.ppermute(v, "seq", [(s, s ^ 1) for s in range(8)])


def on_device(
    tokens, segments, routes, gain_attn, w_query, w_key, w_value, w_output, rel_table, gain_moe,
    w_router, w_inner, w_outer, cotangent,
):
    seq = lax.axis_index("seq")
    idx = jnp.stack([seq // 2, seq % 2]).astype(jnp.int32)
    x_all = lax.all_gather(tokens, "seq", axis=0, tiled=True)
    small = jnp.concatenate([gain_attn, gain_moe, rel_table, jnp.zeros((113,), bf16)])
    pack = pack_weights(w_query, w_key, w_value, w_output, w_router, small.reshape(1, 128))
    wqkv, half, gains, band = unpack_weights(idx, exchange(pack, BOTH))
    rest = other_core(half)
    attended = attend(idx, x_all, segments.reshape(LEN, 1), wqkv, gains, band)
    o_parts = attended[:4]
    h, qe, ke, v, lse = attended[4:]
    o_parts = [o_parts[0]] + [along_y(o_parts[k], k) for k in (1, 2, 3)]
    x1, h2, prob, hot, send, wo, router = dispatch(
        idx, tokens, o_parts, half, rest, gains, routes, cotangent
    )
    ret, grad_inner, grad_outer = experts(exchange(send, BOTH), w_inner, w_outer)
    back = exchange(ret, BOTH)
    layer_out, dx1, *more = returned(
        idx, back, x1, h2, prob, hot, cotangent, router, gains, wo, o_parts
    )
    go_parts = [more[0]] + [along_y(more[k], k) for k in (1, 2, 3)]
    keep, give, dgain = more[4:]
    late = other_core(give)
    own, other, dq_all, line, acc = attend_back(idx, go_parts, x_all, wqkv, qe, ke, v, band, lse)
    got = other_core(other)
    terms = weight_terms(idx, h, dq_all, line, dgain, acc, keep, late)
    d_parts = pair_sum(idx, own, got)
    d_parts = [d_parts[0]] + [along_y(d_parts[k], k) for k in (1, 2, 3)]
    sums = exchange(middle_sums(exchange(terms, "fsdp")), "seq")
    dq, dk, dv, do, dr, small = sums_last(sums)
    tokens_grad = tokens_last(d_parts, tokens, gains, dx1)
    lines = small[:6, 64:70]
    lines = lines[:, 0::2] + lines[:, 1::2]
    return (
        layer_out,
        tokens_grad,
        lines[:, 0].astype(bf16),
        dq,
        dk,
        dv,
        do,
        lines[:3, 2].astype(bf16),
        lines[:, 1].astype(bf16),
        dr,
        grad_inner,
        grad_outer,
    )


def solution(mesh):
    rows = P(BOTH, None)
    flat = P(BOTH)
    cube = P(BOTH, None, None)
    return jax.shard_map(
        on_device,
        mesh=mesh,
        in_specs=(
            rows, P("fsdp", None), rows, flat, rows, rows, rows, rows, flat, flat, rows, cube, cube,
            rows,
        ),
        out_specs=(rows, rows, flat, rows, rows, rows, rows, flat, flat, rows, cube, cube),
        check_vma=False,
    )
```

```python
import functools

import jax
import jax.numpy as jnp
from jax import lax
from jax.experimental import pallas as pl
from jax.experimental.pallas import tpu as pltpu
from jax.sharding import PartitionSpec as P

bf16 = jnp.bfloat16
f32 = jnp.float32

WIDTH = 768
TOK = 128
LEN = 1024
FF = 3072
GROUP = 3
HD = 64
COLS = GROUP * HD
BAND = 5 * TOK
HALF = WIDTH // 2
PACK = 2432
MORE = 896
SENT = 640
LATE = 512
FF_TILE = 768
PROJ = 512
eps = 1e-06
bucket_edges = (12, 16, 23, 32, 46, 64, 91)
BOTH = ("fsdp", "seq")


def params(mib):
    return pltpu.CompilerParams(vmem_limit_bytes=mib << 20)


smem = pl.BlockSpec(memory_space=pltpu.SMEM)
vmem = pl.BlockSpec(memory_space=pltpu.VMEM)


def iota(shape, dim):
    return lax.broadcasted_iota(jnp.int32, shape, dim)


def sixth(n):
    return (n * 10923) >> 16


def third(n):
    return (n * 21846) >> 16


def bucket_of(offsets):
    spread = jnp.abs(offsets)
    ids = (offsets > 0).astype(jnp.int32) * 16 + jnp.minimum(spread, 8)
    for border in bucket_edges:
        ids = ids + (spread >= border).astype(jnp.int32)
    return ids


def mm(a, b):
    return jnp.dot(a, b, preferred_element_type=f32)


def mm_nt(a, b):
    return lax.dot_general(a, b, (((1,), (1,)), ((), ())), preferred_element_type=f32)


def mm_tn(a, b):
    return lax.dot_general(a, b, (((0,), (0,)), ((), ())), preferred_element_type=f32)


def exact(a, b):
    return lax.dot_general(
        a,
        b,
        (((1,), (0,)), ((), ())),
        precision=lax.Precision.HIGHEST,
        preferred_element_type=f32,
    )


def cost(us):
    return pl.CostEstimate(flops=int(us * 1.15e9), bytes_accessed=1 << 20, transcendentals=0)


def call(kernel, outs, ins, scratch=(), mib=16, us=2, **kw):
    return pl.pallas_call(
        kernel,
        out_shape=outs,
        in_specs=ins,
        out_specs=jax.tree.map(lambda _: vmem, outs),
        scratch_shapes=list(scratch),
        compiler_params=params(mib),
        cost_estimate=cost(us),
        **kw,
    )


def load_rows(ref, start, stride, count=128):
    return jnp.concatenate(
        [ref[j, pl.ds(start, count, stride=stride), :] for j in range(ref.shape[0])], axis=1
    )


def store_rows(ref, start, stride, value, first=0):
    for j in range(value.shape[1] // 128):
        ref[first + j, pl.ds(start, value.shape[0], stride=stride), :] = value[
            :, 128 * j : 128 * j + 128
        ]


def whole(ref, first, last):
    return jnp.concatenate([ref[j] for j in range(first, last)], axis=1)


def fill(ref, value):
    for j in range(ref.shape[0]):
        ref[j] = value[:, 128 * j : 128 * j + 128].astype(f32)


def sds(*shape, dtype=bf16):
    return jax.ShapeDtypeStruct(shape, dtype)


def pack_kernel(q_ref, k_ref, v_ref, o_ref, r_ref, small_ref, out_ref):
    q, k, v, o, r = (ref[...].astype(f32) for ref in (q_ref, k_ref, v_ref, o_ref, r_ref))
    six = jnp.concatenate([q, k, v, r], axis=1)
    row6 = jnp.concatenate([o[0:1], o[1:2], o[2:3], small_ref[...].astype(f32)], axis=1)
    row7 = jnp.concatenate([o[3:4], o[4:5], o[5:6], jnp.zeros((1, 128), f32)], axis=1)
    block = jnp.concatenate([six, row6, row7] * 2, axis=0).astype(bf16)
    for f in range(8):
        out_ref[16 * f : 16 * f + 16, :] = block


def pack_weights(w_query, w_key, w_value, w_output, w_router, small):
    return call(pack_kernel, [sds(128, PACK)], [vmem] * 6, name="pack_weights", mib=56)(
        w_query, w_key, w_value, w_output, w_router, small
    )[0]


def split_kernel(got_ref, heads_ref, more_ref, gf_ref, qf_ref, mf_ref):
    fill(gf_ref, got_ref)
    small = gf_ref[18, pl.ds(6, 16, stride=8), :]
    for r in range(6):
        for j in range(18):
            qf_ref[j, pl.ds(r, 16, stride=6), :] = gf_ref[j, pl.ds(r, 16, stride=8), :]
        mf_ref[6, pl.ds(r, 16, stride=6), :] = gf_ref[18, pl.ds(r, 16, stride=8), :]
        for j in range(6):
            mf_ref[j, pl.ds(r, 16, stride=6), :] = gf_ref[
                6 * (r % 3) + j, pl.ds(6 + r // 3, 16, stride=8), :
            ]
        third_lane = small[:, 12 + r : 13 + r] if r < 3 else jnp.zeros((16, 1), f32)
        cols = [small[:, r : r + 1], small[:, 6 + r : 7 + r], third_lane, jnp.zeros((16, 125), f32)]
        qf_ref[18, pl.ds(r, 16, stride=6), :] = jnp.concatenate(cols, axis=1)
    q, k, v = (whole(qf_ref, 6 * m, 6 * m + 6) for m in range(3))
    small = qf_ref[18][:, :64]
    for y in range(4):
        at = slice(COLS * y, COLS * y + COLS)
        rows = jnp.concatenate([q[:, at], k[:, at], v[:, at], small], axis=1).astype(bf16)
        heads_ref[192 * y : 192 * y + 96, :] = rows
        heads_ref[192 * y + 96 : 192 * y + 192, :] = rows
    more_ref[...] = whole(mf_ref, 0, 7).astype(bf16)


def split_weights(got):
    return call(
        split_kernel,
        [sds(WIDTH, SENT), sds(96, MORE)],
        [vmem],
        [
            pltpu.VMEM((19, 128, 128), f32),
            pltpu.VMEM((19, 96, 128), f32),
            pltpu.VMEM((7, 96, 128), f32),
        ],
        name="split_weights",
        mib=56,
    )(got)


def output_kernel(idx_ref, *refs):
    blocks, refs = refs[:8], refs[8:]
    wo_ref, router_ref, src_ref, dst_ref = refs
    y, c = idx_ref[0], idx_ref[1]
    for side in range(2):
        for k in range(4):
            place = 2 * lax.rem(y + 4 - k, 4) + (c if side == 0 else 1 - c)
            n = 4 * side + k
            for j in range(7):
                src_ref[n, j] = blocks[n][:, 128 * j : 128 * j + 128].astype(f32)
                for r in range(6):
                    dst_ref[j, pl.ds(place * 6 + r, 16, stride=48), :] = src_ref[
                        n, j, pl.ds(r, 16, stride=6), :
                    ]
    wo_ref[...] = whole(dst_ref, 0, 6).astype(bf16)
    router_ref[...] = dst_ref[6].astype(bf16)


def output_weights(idx, blocks):
    return call(
        output_kernel,
        [sds(WIDTH, WIDTH), sds(WIDTH, 128)],
        [smem] + [vmem] * 8,
        [pltpu.VMEM((8, 7, 96, 128), f32), pltpu.VMEM((7, WIDTH, 128), f32)],
        name="output_weights",
        mib=24,
        us=3,
    )(idx, *blocks)


def unpack(y, pack_ref, wqkv_ref, gain_ref, band_ref, pf_ref, wf_ref):
    fill(pf_ref, pack_ref)
    for s in range(8):
        for r in range(6):
            rows = load_rows(pf_ref, 96 * s + r, 6, 16)
            store_rows(wf_ref, 6 * s + r, 48, rows)
    wqkv_ref[...] = whole(wf_ref, 0, 5)[:, : 3 * COLS].astype(bf16)
    small = wf_ref[4].T
    gain_ref[...] = jnp.concatenate([small[64:66], jnp.zeros((6, WIDTH), f32)], axis=0)
    lanes = iota((8, WIDTH), 1)
    group = sixth(lanes)
    entry = 3 * group + lanes - 6 * group
    mine = (lanes - 6 * group < 3) & ((entry >> 5) == 3 * y + iota((8, WIDTH), 0))
    table = jnp.where(mine, small[66:67], 0.0).astype(bf16)
    rows = iota((WIDTH, 128), 0)
    group = sixth(rows)
    entry = 3 * group + rows - 6 * group
    table = mm(table, ((entry & 31) == iota((WIDTH, 128), 1)).astype(bf16)).astype(bf16)
    hot = bucket_of(iota((128, 512), 1) - 255) == iota((128, 512), 0)
    lines = mm(table, hot.astype(bf16))
    for h in range(GROUP):
        line = lines[h : h + 1]
        wide = pltpu.roll(
            jnp.broadcast_to(line, (TOK, 512)), 385, 1, stride=1, stride_axis=0
        )
        band_ref[h, :, :TOK] = jnp.broadcast_to(line[:, :1], (TOK, TOK))
        band_ref[h, :, TOK : 4 * TOK] = wide[:, : 3 * TOK]
        band_ref[h, :, 4 * TOK :] = jnp.broadcast_to(line[:, 511:], (TOK, TOK))


def banded(band_ref, h, pq):
    parts = []
    for j in range(8):
        at = jnp.clip(j - pq + 2, 0, 4) * TOK
        parts.append(band_ref[h, :, pl.ds(pl.multiple_of(at, TOK), TOK)])
    return jnp.concatenate(parts, axis=1)


def attend_kernel(
    idx_ref, pack_ref, seg_ref, *refs
):
    blocks, refs = refs[:8], refs[8:]
    o0_ref, o1_ref, o2_ref, o3_ref, gain_ref, lse_ref = refs[:6]
    saved, refs = refs[6:12], refs[12:]
    wqkv_ref, band_ref, x_ref, qe_ref, ke_ref, v_ref = refs[:6]
    pf_ref, wf_ref, os_ref, in_sem, out_sem = refs[6:]
    y, c = idx_ref[0], idx_ref[1]
    loads = []
    for side in range(2):
        for k in range(4):
            place = 2 * lax.rem(y + 4 - k, 4) + (c if side == 0 else 1 - c)
            at = pl.ds(pl.multiple_of(place * TOK, TOK), TOK)
            n = 4 * side + k
            loads.append(pltpu.make_async_copy(blocks[n], x_ref.at[at, :], in_sem.at[n]))
    for load in loads:
        load.start()
    stores = [
        pltpu.make_async_copy(src, dst, out_sem.at[n])
        for n, (src, dst) in enumerate(zip(refs[:6], saved))
    ]
    unpack(y, pack_ref, wqkv_ref, gain_ref, band_ref, pf_ref, wf_ref)
    for store in stores[:2]:
        store.start()
    for load in loads:
        load.wait()
    stores[2].start()
    gain = gain_ref[:1, :]

    def project(i, _):
        at = pl.ds(pl.multiple_of(i * PROJ, PROJ), PROJ)
        x = x_ref[at, :].astype(f32)
        hb = (x * lax.rsqrt(jnp.mean(x * x, axis=-1, keepdims=True) + eps) * gain).astype(bf16)
        doc = seg_ref[at, :]
        lane = iota((PROJ, HD), 1)
        same = lane == doc
        q_mark = jnp.where(same, -1e30, 0.0).astype(bf16)
        k_mark = jnp.where((lane < 3) & jnp.logical_not(same), 1.0, 0.0).astype(bf16)
        q = (mm(hb, wqkv_ref[:, :COLS]).astype(bf16).astype(f32) * 0.125).astype(bf16)
        k = mm(hb, wqkv_ref[:, COLS : 2 * COLS]).astype(bf16)
        v_ref[at, :] = mm(hb, wqkv_ref[:, 2 * COLS :]).astype(bf16)
        q_parts, k_parts = [], []
        for h in range(GROUP):
            q_parts += [q[:, HD * h : HD * h + HD], q_mark]
            k_parts += [k[:, HD * h : HD * h + HD], k_mark]
        qe_ref[at, :] = jnp.concatenate(q_parts, axis=1)
        ke_ref[at, :] = jnp.concatenate(k_parts, axis=1)
        return 0

    lax.fori_loop(0, LEN // PROJ, project, 0)
    for store in stores[3:]:
        store.start()

    def attend(k, _):
        yq = lax.rem(y + k, 4)
        pq = 2 * yq + c
        at = pl.ds(pl.multiple_of(pq * TOK, TOK), TOK)
        lane = iota((TOK, 128), 1)
        lse_all = jnp.zeros((TOK, 128), f32)
        outs = []
        for h in range(GROUP):
            s = mm_nt(qe_ref[at, 128 * h : 128 * h + 128], ke_ref[:, 128 * h : 128 * h + 128])
            s = s + banded(band_ref, h, pq)
            top = jnp.max(s, axis=-1, keepdims=True)
            e = jnp.exp(s - top)
            total = jnp.sum(e, axis=-1, keepdims=True)
            p = (e * (1.0 / total)).astype(bf16)
            outs.append(mm(p, v_ref[:, HD * h : HD * h + HD]))
            lse_all = jnp.where(lane == h, top + jnp.log(total), lse_all)
        os_ref[k] = jnp.concatenate(outs, axis=1).astype(bf16)
        lse_ref[yq] = lse_all
        return 0

    lax.fori_loop(0, 4, attend, 0, unroll=2)
    o0_ref[...] = os_ref[0]
    o1_ref[...] = os_ref[1]
    o2_ref[...] = os_ref[2]
    o3_ref[...] = os_ref[3]
    for store in stores:
        store.wait()


def attend(idx, pack, seg_col, blocks):
    saved = [
        sds(WIDTH, 3 * COLS), sds(GROUP, TOK, BAND, dtype=f32),
        sds(LEN, WIDTH), sds(LEN, 384), sds(LEN, 384), sds(LEN, COLS),
    ]
    outs = [sds(TOK, COLS)] * 4 + [sds(8, WIDTH, dtype=f32), sds(4, TOK, 128, dtype=f32)]
    place = pl.BlockSpec(memory_space=pl.ANY)
    return pl.pallas_call(
        attend_kernel,
        out_shape=outs + saved,
        in_specs=[smem, vmem, vmem] + [place] * 8,
        out_specs=[vmem] * 6 + [place] * 6,
        scratch_shapes=[pltpu.VMEM(v.shape, v.dtype) for v in saved]
        + [
            pltpu.VMEM((5, WIDTH, 128), f32),
            pltpu.VMEM((5, WIDTH, 128), f32),
            pltpu.VMEM((4, TOK, COLS), bf16),
            pltpu.SemaphoreType.DMA((8,)),
            pltpu.SemaphoreType.DMA((6,)),
        ],
        compiler_params=params(56),
        cost_estimate=cost(14),
        name="attend",
    )(idx, pack, seg_col, *blocks)


def dispatch_kernel(
    idx_ref, x_ref, o0_ref, o1_ref, o2_ref, o3_ref, wo_ref, router_ref, gain_ref,
    route_ref, cot_ref,
    x1_ref, h2_ref, prob_ref, hot_ref, send_ref,
    sf_ref,
):
    y = idx_ref[0]
    x1 = x_ref[...].astype(f32)
    for k, o_ref in enumerate((o0_ref, o1_ref, o2_ref, o3_ref)):
        src = lax.rem(y + 4 - k, 4)
        x1 = x1 + mm(o_ref[...], wo_ref[pl.ds(pl.multiple_of(src * COLS, COLS), COLS), :])
    x1_ref[...] = x1
    r2 = lax.rsqrt(jnp.mean(x1 * x1, axis=-1, keepdims=True) + eps)
    h2 = (x1 * r2 * gain_ref[1:2, :]).astype(bf16)
    h2_ref[...] = h2
    logits = mm(h2, router_ref[...])
    e = jnp.exp(logits - jnp.max(logits, axis=-1, keepdims=True))
    prob = e / jnp.sum(e, axis=-1, keepdims=True)
    prob_ref[...] = prob
    expert = iota((TOK, 128), 1)
    picked = (route_ref[...] == expert).astype(f32)
    gate = jnp.sum(prob * picked, axis=-1, keepdims=True)
    earlier = (iota((TOK, TOK), 0) > iota((TOK, TOK), 1)).astype(bf16)
    slot = jnp.sum(mm(earlier, picked.astype(bf16)) * picked, axis=-1, keepdims=True)
    geo = (gate * cot_ref[...].astype(f32)).astype(bf16)
    for s in range(2):
        hot = jnp.where((slot > 0.5) == (s == 1), picked, 0.0).astype(bf16)
        hot_ref[s] = hot
        for kind, src in enumerate((h2, geo)):
            placed = mm_tn(hot, src)
            for half in range(2):
                part = placed[:, HALF * half : HALF * half + HALF]
                store_rows(sf_ref, kind * 4 + s * 2 + half, 8, part)
    send_ref[...] = whole(sf_ref, 0, 3).astype(bf16)


def dispatch(idx, x_own, o_parts, wo, router, gains, route_col, cot):
    outs = [
        sds(TOK, WIDTH, dtype=f32), sds(TOK, WIDTH), sds(TOK, 128, dtype=f32),
        sds(2, TOK, 128), sds(LEN, HALF),
    ]
    return call(
        dispatch_kernel,
        outs,
        [smem] + [vmem] * 10,
        [pltpu.VMEM((3, LEN, 128), f32)],
        name="dispatch",
        mib=10,
    )(idx, x_own, *o_parts, wo, router, gains, route_col, cot)


def expert_kernel(
    recv_ref, wi_hbm, wo_hbm, ret_ref, gi_hbm, go_hbm,
    rf_ref, x_ref, xt_ref, g_ref, eo_ref, gx_ref, wi_ref, wo_ref, gi_ref, go_ref, in_sem, out_sem,
):
    tiles = FF // FF_TILE
    loads, stores = [], []
    for i in range(tiles):
        at = pl.ds(i * FF_TILE, FF_TILE)
        loads.append(
            (
                pltpu.make_async_copy(wi_hbm.at[0, :, at], wi_ref.at[i], in_sem.at[0, i]),
                pltpu.make_async_copy(wo_hbm.at[0, at, :], wo_ref.at[i], in_sem.at[1, i]),
            )
        )
        stores.append(
            (
                pltpu.make_async_copy(gi_ref.at[i], gi_hbm.at[0, :, at], out_sem.at[0, i]),
                pltpu.make_async_copy(go_ref.at[i], go_hbm.at[0, at, :], out_sem.at[1, i]),
            )
        )
    for pair in loads:
        for load in pair:
            load.start()
    fill(rf_ref, recv_ref)
    for kind, dst in enumerate((x_ref, g_ref)):
        for s in range(2):
            for half in range(2):
                dst[TOK * s : TOK * s + TOK, HALF * half : HALF * half + HALF] = load_rows(
                    rf_ref, kind * 4 + s * 2 + half, 8
                ).astype(bf16)
    xt_ref[...] = x_ref[...].T
    for i in range(tiles):
        for load in loads[i]:
            load.wait()
        wi = wi_ref[i]
        wo = wo_ref[i]
        g = g_ref[...]
        a = mm(x_ref[...], wi)
        gu = mm_nt(g, wo)
        cc = 0.7978845608028654
        sq = a * a
        t = jnp.tanh(cc * (a + 0.044715 * (sq * a)))
        u = (0.5 * a * (1.0 + t)).astype(bf16)
        slope = 0.5 * (1.0 + t) + (0.5 * cc) * a * (1.0 - t * t) * (1.0 + 0.134145 * sq)
        ga = (gu * slope).astype(bf16)
        go_ref[i] = mm_tn(u, g).astype(bf16)
        gi_ref[i] = mm(xt_ref[...], ga).astype(bf16)
        for store in stores[i]:
            store.start()
        if i == 0:
            eo_ref[...] = mm(u, wo)
            gx_ref[...] = mm_nt(ga, wi)
        else:
            eo_ref[...] += mm(u, wo)
            gx_ref[...] += mm_nt(ga, wi)
    for kind, src in enumerate((eo_ref, gx_ref)):
        for s in range(2):
            for half in range(2):
                part = src[TOK * s : TOK * s + TOK, HALF * half : HALF * half + HALF]
                store_rows(rf_ref, kind * 4 + s * 2 + half, 8, part)
    ret_ref[...] = whole(rf_ref, 0, 3).astype(bf16)
    for pair in stores:
        for store in pair:
            store.wait()


def experts(recv, w_inner, w_outer):
    place = pl.BlockSpec(memory_space=pl.ANY)
    tiles = FF // FF_TILE
    return pl.pallas_call(
        expert_kernel,
        out_shape=[sds(LEN, HALF), sds(1, WIDTH, FF), sds(1, FF, WIDTH)],
        in_specs=[vmem, place, place],
        out_specs=[vmem, place, place],
        scratch_shapes=[
            pltpu.VMEM((3, LEN, 128), f32),
            pltpu.VMEM((2 * TOK, WIDTH), bf16),
            pltpu.VMEM((WIDTH, 2 * TOK), bf16),
            pltpu.VMEM((2 * TOK, WIDTH), bf16),
            pltpu.VMEM((2 * TOK, WIDTH), f32),
            pltpu.VMEM((2 * TOK, WIDTH), f32),
            pltpu.VMEM((tiles, WIDTH, FF_TILE), bf16),
            pltpu.VMEM((tiles, FF_TILE, WIDTH), bf16),
            pltpu.VMEM((tiles, WIDTH, FF_TILE), bf16),
            pltpu.VMEM((tiles, FF_TILE, WIDTH), bf16),
            pltpu.SemaphoreType.DMA((2, tiles)),
            pltpu.SemaphoreType.DMA((2, tiles)),
        ],
        compiler_params=params(56),
        cost_estimate=cost(12),
        name="experts",
    )(recv, w_inner, w_outer)


def return_kernel(
    idx_ref, back_ref, x1_ref, h2_ref, prob_ref, hot_ref, cot_ref, router_ref, gain_ref, wo_ref,
    o0_ref, o1_ref, o2_ref, o3_ref,
    out_ref, dx1_ref, g0_ref, g1_ref, g2_ref, g3_ref, keep_ref, give_ref, dgain_ref,
    bf_ref,
):
    y, c = idx_ref[0], idx_ref[1]
    fill(bf_ref, back_ref)
    parts = []
    for kind in range(2):
        halves = []
        for half in range(2):
            got = jnp.zeros((TOK, HALF), f32)
            for s in range(2):
                rows = load_rows(bf_ref, kind * 4 + s * 2 + half, 8).astype(bf16)
                got = got + mm(hot_ref[s], rows)
            halves.append(got)
        parts.append(jnp.concatenate(halves, axis=1))
    eo, gx = parts
    x1 = x1_ref[...]
    prob = prob_ref[...]
    picked = hot_ref[0].astype(f32) + hot_ref[1].astype(f32)
    gate = jnp.sum(prob * picked, axis=-1, keepdims=True)
    out_ref[...] = (x1 + gate * eo).astype(bf16)
    dy = cot_ref[...].astype(f32)
    dgate = jnp.sum(dy * eo, axis=-1, keepdims=True)
    gz = (dgate * gate * (picked - prob)).astype(bf16)
    dh2 = gx + mm_nt(gz, router_ref[...])
    routed = mm_tn(h2_ref[...], gz)
    blank = jnp.zeros((WIDTH, 64), f32)
    near = jnp.concatenate([routed[:, :64], blank], axis=1)
    far = jnp.concatenate([routed[:, 64:], blank], axis=1)
    keep_ref[:, HALF:] = jnp.where(c == 0, near, far).astype(bf16)
    give_ref[:, HALF:] = jnp.where(c == 0, far, near).astype(bf16)
    r2 = lax.rsqrt(jnp.mean(x1 * x1, axis=-1, keepdims=True) + eps)
    scaled = x1 * r2
    dgain = jnp.sum(dh2 * scaled, axis=0, keepdims=True)
    dgain_ref[...] = jnp.broadcast_to(dgain, (8, WIDTH))
    gd = gain_ref[1:2, :] * dh2
    dx1 = dy + r2 * (gd - scaled * jnp.mean(gd * scaled, axis=-1, keepdims=True))
    dx1_ref[...] = dx1
    gw = dx1.astype(bf16)
    for k, g_ref in enumerate((g0_ref, g1_ref, g2_ref, g3_ref)):
        dst = lax.rem(y + k, 4)
        rows = wo_ref[pl.ds(pl.multiple_of(dst * COLS, COLS), COLS), :]
        g_ref[...] = mm_nt(gw, rows).astype(bf16)
    for k, o_ref in enumerate((o0_ref, o1_ref, o2_ref, o3_ref)):
        src = lax.rem(y + 4 - k, 4)
        rows = pl.ds(pl.multiple_of(src * COLS, COLS), COLS)
        terms = mm_tn(o_ref[...], gw)
        near, far = terms[:, :HALF], terms[:, HALF:]
        keep_ref[rows, :HALF] = jnp.where(c == 0, near, far).astype(bf16)
        give_ref[rows, :HALF] = jnp.where(c == 0, far, near).astype(bf16)


def returned(idx, back, x1, h2, prob, hot, cot, router, gains, wo, o_parts):
    outs = (
        [sds(TOK, WIDTH), sds(TOK, WIDTH, dtype=f32)]
        + [sds(TOK, COLS)] * 4
        + [sds(WIDTH, LATE), sds(WIDTH, LATE), sds(8, WIDTH, dtype=f32)]
    )
    return call(
        return_kernel,
        outs,
        [smem] + [vmem] * 13,
        [pltpu.VMEM((3, LEN, 128), f32)],
        name="returned",
        mib=14,
    )(idx, back, x1, h2, prob, hot, cot, router, gains, wo, *o_parts)


def backward_kernel(
    idx_ref, g0_ref, g1_ref, g2_ref, g3_ref, x_ref, wqkv_ref, qe_ref, ke_ref, v_ref,
    band_ref, lse_ref, gain_ref,
    own_ref, other_ref, dq_ref, line_ref, acc_ref, h_ref,
    gs_ref, gk_ref, gv_ref,
):
    y, c = idx_ref[0], idx_ref[1]
    for k, g_ref in enumerate((g0_ref, g1_ref, g2_ref, g3_ref)):
        gs_ref[k] = g_ref[...]
    gk_ref[...] = jnp.zeros_like(gk_ref)
    gv_ref[...] = jnp.zeros_like(gv_ref)
    acc_ref[...] = jnp.zeros_like(acc_ref)

    def block(k, _):
        yq = lax.rem(y + 4 - k, 4)
        pq = 2 * yq + c
        at = pl.ds(pl.multiple_of(pq * TOK, TOK), TOK)
        not_at = pl.ds(pl.multiple_of((pq + 1 - 2 * c) * TOK, TOK), TOK)
        lse = lse_ref[yq]
        go = gs_ref[k]
        outs = []
        for h in range(GROUP):
            q = qe_ref[at, 128 * h : 128 * h + 128]
            keys = ke_ref[:, 128 * h : 128 * h + 128]
            g = go[:, HD * h : HD * h + HD]
            s = mm_nt(q, keys) + banded(band_ref, h, pq)
            p = jnp.exp(s - lse[:, h : h + 1])
            pd = p * mm_nt(g, v_ref[:, HD * h : HD * h + HD])
            gs = pd - p * jnp.sum(pd, axis=-1, keepdims=True)
            for j in range(8):
                to = pl.multiple_of(jnp.clip(j - pq + 2, 0, 4) * TOK, TOK)
                acc_ref[h, :, pl.ds(to, TOK)] += gs[:, TOK * j : TOK * j + TOK]
            low = gs.astype(bf16)
            outs.append(mm(low, keys)[:, :HD] * 0.125)
            gk_ref[HD * h : HD * h + HD, :] += mm_tn(q, low)[:HD]
            gv_ref[HD * h : HD * h + HD, :] += mm_tn(g, p.astype(bf16))
        dq_ref[at, :COLS] = jnp.concatenate(outs, axis=1).astype(bf16)
        dq_ref[not_at, :COLS] = jnp.zeros((TOK, COLS), bf16)
        return 0

    lax.fori_loop(0, 4, block, 0)
    dq_ref[:, COLS : 2 * COLS] = gk_ref[...].T.astype(bf16)
    dq_ref[:, 2 * COLS :] = gv_ref[...].T.astype(bf16)
    lines = jnp.zeros((1, WIDTH), f32)
    for side in range(2):
        rows = []
        for yq in range(4):
            pq = 2 * yq + (c if side == 0 else 1 - c)
            rows.append(pl.ds(pl.multiple_of(pq * TOK, TOK), TOK))
        d = mm_nt(jnp.concatenate([dq_ref[at, :] for at in rows], axis=0), wqkv_ref[...])
        x = jnp.concatenate([x_ref[at, :] for at in rows], axis=0).astype(f32)
        scaled = x * lax.rsqrt(jnp.mean(x * x, axis=-1, keepdims=True) + eps)
        lines = lines + jnp.sum(d * scaled, axis=0, keepdims=True)
        hb = (scaled * gain_ref[:1, :]).astype(bf16)
        for yq in range(4):
            part = slice(TOK * yq, TOK * yq + TOK)
            h_ref[rows[yq], :] = hb[part]
            if side == 0:
                own_ref[yq] = d[part]
            else:
                other_ref[yq] = d[part].astype(bf16)
    line_ref[...] = jnp.broadcast_to(lines, (8, WIDTH))


def attend_back(idx, go_parts, x_all, wqkv, qe, ke, v, band, lse, gains):
    outs = [
        sds(4, TOK, WIDTH, dtype=f32), sds(4, TOK, WIDTH), sds(LEN, 3 * COLS),
        sds(8, WIDTH, dtype=f32), sds(GROUP, TOK, BAND, dtype=f32), sds(LEN, WIDTH),
    ]
    return call(
        backward_kernel,
        outs,
        [smem] + [vmem] * 12,
        [
            pltpu.VMEM((4, TOK, COLS), bf16),
            pltpu.VMEM((COLS, LEN), f32),
            pltpu.VMEM((COLS, LEN), f32),
        ],
        name="attend_back",
        mib=24,
        us=12,
    )(idx, *go_parts, x_all, wqkv, qe, ke, v, band, lse, gains)


def terms_kernel(
    idx_ref, h_ref, dq_ref, line_ref, dgain_ref, acc_ref, keep_ref, got_ref, send_ref
):
    y = idx_ref[0]
    ids = bucket_of(iota((512, 128), 0) - 255)
    flat = iota((512, 128), 1)
    turn = (iota((TOK, TOK), 0) + iota((TOK, TOK), 1) == TOK - 1).astype(f32)
    near = jnp.concatenate([acc_ref[h, :, TOK : 4 * TOK] for h in range(GROUP)], axis=1)
    near = exact(turn, near)
    blank = jnp.zeros((TOK, TOK), f32)
    lane = iota((1, 128), 1)
    diags, sides = [], []
    for h in range(GROUP):
        part = jnp.concatenate([near[:, 3 * TOK * h : 3 * TOK * h + 3 * TOK], blank], axis=1)
        part = pltpu.roll(part, 0, 1, stride=1, stride_axis=0)
        diags.append(jnp.sum(part, axis=0, keepdims=True))
        low = jnp.sum(acc_ref[h, :, :TOK])
        high = jnp.sum(acc_ref[h, :, 4 * TOK :])
        sides.append(jnp.where(lane == 15, low, 0.0) + jnp.where(lane == 31, high, 0.0))
    diags = jnp.concatenate(diags + [jnp.zeros((5, 512), f32)], axis=0)
    sides = jnp.concatenate(sides + [jnp.zeros((5, 128), f32)], axis=0)
    table = exact(diags, (flat == ids).astype(f32)) + sides
    lanes = iota((128, WIDTH), 1)
    group = sixth(lanes)
    entry = 3 * group + lanes - 6 * group
    place = ((entry & 31) == iota((128, WIDTH), 0)).astype(f32)
    lanes = iota((8, WIDTH), 1)
    group = sixth(lanes)
    entry = 3 * group + lanes - 6 * group
    mine = (lanes - 6 * group < 3) & ((entry >> 5) == 3 * y + iota((8, WIDTH), 0))
    mine = mine & (iota((8, WIDTH), 0) < GROUP)
    table = jnp.where(mine, exact(table, place), 0.0)
    table = jnp.sum(table, axis=0, keepdims=True)
    lines = []
    for v in (line_ref[:1, :], dgain_ref[:1, :], table):
        high = v.astype(bf16).astype(f32)
        lines += [high, v - high]
    block = jnp.concatenate(lines + [jnp.zeros((122, WIDTH), f32)], axis=0).T
    block = jnp.concatenate([jnp.zeros((WIDTH, 64), f32), block[:, :64]], axis=1)
    send_ref[:, 512:SENT] = block.astype(bf16)
    send_ref[:, SENT:] = (keep_ref[...].astype(f32) + got_ref[...].astype(f32)).astype(bf16)

    def weights(j, _):
        at = pl.ds(pl.multiple_of(j * 128, 128), 128)
        terms = mm_tn(h_ref[:, at], dq_ref[...])
        send_ref[at, :512] = terms[:, :512].astype(bf16)
        extra = send_ref[at, 512:SENT].astype(f32)
        last = jnp.concatenate([terms[:, 512:], extra[:, 64:]], axis=1)
        send_ref[at, 512:SENT] = last.astype(bf16)
        return 0

    lax.fori_loop(0, 6, weights, 0, unroll=6)


def weight_terms(idx, h, dq, line, dgain, acc, keep, got):
    return call(
        terms_kernel,
        [sds(WIDTH, SENT + LATE)],
        [smem] + [vmem] * 7,
        name="weight_terms",
        mib=14,
        us=5,
    )(idx, h, dq, line, dgain, acc, keep, got)[0]


def pair_kernel(idx_ref, own_ref, got_ref, d0_ref, d1_ref, d2_ref, d3_ref):
    y = idx_ref[0]
    for k, d_ref in enumerate((d0_ref, d1_ref, d2_ref, d3_ref)):
        dst = lax.rem(y + k, 4)
        d_ref[...] = (own_ref[dst] + got_ref[dst].astype(f32)).astype(d_ref.dtype)


def pair_sum(idx, own, got):
    outs = [sds(TOK, WIDTH, dtype=f32)] + [sds(TOK, WIDTH)] * 3
    return call(pair_kernel, outs, [smem, vmem, vmem], name="pair_sum")(idx, own, got)


def tokens_kernel(d0_ref, d1_ref, d2_ref, d3_ref, x_ref, gain_ref, dx1_ref, out_ref):
    dh = d0_ref[...] + d1_ref[...].astype(f32) + d2_ref[...].astype(f32) + d3_ref[...].astype(f32)
    x = x_ref[...].astype(f32)
    r1 = lax.rsqrt(jnp.mean(x * x, axis=-1, keepdims=True) + eps)
    gd = gain_ref[:1, :] * dh
    scaled = x * r1
    out_ref[...] = dx1_ref[...] + r1 * (gd - scaled * jnp.mean(gd * scaled, axis=-1, keepdims=True))


def tokens_last(d_parts, x_own, gains, dx1):
    return call(tokens_kernel, [sds(TOK, WIDTH, dtype=f32)], [vmem] * 7, name="tokens_last")(
        *d_parts, x_own, gains, dx1
    )[0]


def middle_kernel(got_ref, out_ref):
    def total(a, b):
        sums = got_ref[:48, a:b].astype(f32)
        for f in range(1, 16):
            sums = sums + got_ref[48 * f : 48 * f + 48, a:b].astype(f32)
        return sums

    pieces = [total(0, 512)]
    last = total(512, SENT)
    lane = iota((48, 128), 1)
    both = last + pltpu.roll(last, 127, 1)
    high = both.astype(bf16).astype(f32)
    rest = pltpu.roll(both - high, 1, 1)
    last = jnp.where(lane < 64, last, jnp.where(lane % 2 == 0, high, rest))
    pieces += [last, total(SENT, SENT + LATE)]
    sums = jnp.concatenate(pieces, axis=1)
    blank = jnp.zeros((2, SENT + LATE), f32)
    rows = []
    for s in range(8):
        rows += [sums[6 * s : 6 * s + 6], blank]
    out_ref[...] = jnp.concatenate(rows, axis=0).astype(bf16)


def middle_sums(got):
    return call(middle_kernel, [sds(64, SENT + LATE)], [vmem], name="middle_sums", mib=8)(got)[0]


def sums_kernel(recv_ref, q_ref, k_ref, v_ref, o_ref, router_ref, small_ref):
    got = recv_ref[...].astype(f32)
    parts = [got[8 * s : 8 * s + 8] for s in range(8)]
    quads = [parts[2 * y] + parts[2 * y + 1] for y in range(4)]
    for m, ref in enumerate((q_ref, k_ref, v_ref)):
        cols = jnp.concatenate([a[:, COLS * m : COLS * m + COLS] for a in quads], axis=1)
        ref[...] = cols[:6].astype(bf16)
    halves = [parts[c] + parts[2 + c] + parts[4 + c] + parts[6 + c] for c in range(2)]
    o_ref[...] = jnp.concatenate([a[:6, SENT : SENT + HALF] for a in halves], axis=1).astype(bf16)
    routed = [a[:6, SENT + HALF : SENT + HALF + 64] for a in halves]
    router_ref[...] = jnp.concatenate(routed, axis=1).astype(bf16)
    small_ref[...] = halves[0][:, 512:SENT] + halves[1][:, 512:SENT]


def sums_last(recv):
    outs = [sds(6, WIDTH)] * 4 + [sds(6, 128), sds(8, 128, dtype=f32)]
    return call(sums_kernel, outs, [vmem], name="sums_last", mib=4)(recv)


def along_y(v, k):
    return lax.ppermute(v, "seq", [(s, (s + 2 * k) % 8) for s in range(8)])


def exchange(v, axes):
    return lax.all_to_all(v, axes, split_axis=0, concat_axis=0, tiled=True)


def other_core(v):
    return lax.ppermute(v, "seq", [(s, s ^ 1) for s in range(8)])


def on_device(
    tokens, segments, routes, gain_attn, w_query, w_key, w_value, w_output, rel_table, gain_moe,
    w_router, w_inner, w_outer, cotangent,
):
    seq = lax.axis_index("seq")
    idx = jnp.stack([seq // 2, seq % 2]).astype(jnp.int32)
    blocks = [tokens] + [along_y(tokens, k) for k in (1, 2, 3)]
    first = other_core(tokens)
    small = jnp.concatenate([gain_attn, gain_moe, rel_table, jnp.zeros((113,), bf16)])
    pack = pack_weights(w_query, w_key, w_value, w_output, w_router, small.reshape(1, 128))
    heads, more = split_weights(exchange(pack, "fsdp"))
    heads, blocks, first = lax.optimization_barrier((heads, blocks, first))
    heads, more = lax.optimization_barrier((exchange(heads, "seq"), more))
    blocks = blocks + [first] + [other_core(b) for b in blocks[1:]]
    attended = attend(idx, heads, segments.reshape(LEN, 1), blocks)
    more = [more] + [along_y(more, k) for k in (1, 2, 3)]
    more, attended = lax.optimization_barrier((more, attended))
    wo, router = output_weights(idx, more + [other_core(b) for b in more])
    o_parts = attended[:4]
    gains, lse, wqkv, band, x_all, qe, ke, v = attended[4:]
    o_parts = [o_parts[0]] + [along_y(o_parts[k], k) for k in (1, 2, 3)]
    x1, h2, prob, hot, send = dispatch(
        idx, tokens, o_parts, wo, router, gains, routes, cotangent
    )
    ret, grad_inner, grad_outer = experts(exchange(send, BOTH), w_inner, w_outer)
    back = exchange(ret, BOTH)
    layer_out, dx1, *more = returned(
        idx, back, x1, h2, prob, hot, cotangent, router, gains, wo, o_parts
    )
    go_parts = [more[0]] + [along_y(more[k], k) for k in (1, 2, 3)]
    keep, give, dgain = more[4:]
    late = other_core(give)
    own, other, dq_all, line, acc, h = attend_back(
        idx, go_parts, x_all, wqkv, qe, ke, v, band, lse, gains
    )
    got = other_core(other)
    terms = weight_terms(idx, h, dq_all, line, dgain, acc, keep, late)
    d_parts = pair_sum(idx, own, got)
    d_parts = [d_parts[0]] + [along_y(d_parts[k], k) for k in (1, 2, 3)]
    sums = exchange(middle_sums(exchange(terms, "fsdp")), "seq")
    dq, dk, dv, do, dr, small = sums_last(sums)
    tokens_grad = tokens_last(d_parts, tokens, gains, dx1)
    lines = small[:6, 64:70]
    lines = lines[:, 0::2] + lines[:, 1::2]
    return (
        layer_out,
        tokens_grad,
        lines[:, 0].astype(bf16),
        dq,
        dk,
        dv,
        do,
        lines[:3, 2].astype(bf16),
        lines[:, 1].astype(bf16),
        dr,
        grad_inner,
        grad_outer,
    )


def solution(mesh):
    rows = P(BOTH, None)
    flat = P(BOTH)
    cube = P(BOTH, None, None)
    return jax.shard_map(
        on_device,
        mesh=mesh,
        in_specs=(
            rows, P("fsdp", None), rows, flat, rows, rows, rows, rows, flat, flat, rows, cube, cube,
            rows,
        ),
        out_specs=(rows, rows, flat, rows, rows, rows, rows, flat, flat, rows, cube, cube),
        check_vma=False,
    )
```

```python
import functools

import jax
import jax.numpy as jnp
from jax import lax
from jax.experimental import pallas as pl
from jax.experimental.pallas import tpu as pltpu
from jax.sharding import PartitionSpec as P

bf16 = jnp.bfloat16
f32 = jnp.float32

WIDTH = 768
TOK = 128
LEN = 1024
FF = 3072
GROUP = 3
HD = 64
COLS = GROUP * HD
BAND = 5 * TOK
HALF = WIDTH // 2
PACK = 2432
MORE = 896
SENT = 640
SIDE = 320
PART = 384
LATE = 512
FF_TILE = 768
PROJ = 512
eps = 1e-06
bucket_edges = (12, 16, 23, 32, 46, 64, 91)
BOTH = ("fsdp", "seq")


def params(mib):
    return pltpu.CompilerParams(vmem_limit_bytes=mib << 20)


smem = pl.BlockSpec(memory_space=pltpu.SMEM)
vmem = pl.BlockSpec(memory_space=pltpu.VMEM)


def iota(shape, dim):
    return lax.broadcasted_iota(jnp.int32, shape, dim)


def sixth(n):
    return (n * 10923) >> 16


def third(n):
    return (n * 21846) >> 16


def bucket_of(offsets):
    spread = jnp.abs(offsets)
    ids = (offsets > 0).astype(jnp.int32) * 16 + jnp.minimum(spread, 8)
    for border in bucket_edges:
        ids = ids + (spread >= border).astype(jnp.int32)
    return ids


def mm(a, b):
    return jnp.dot(a, b, preferred_element_type=f32)


def mm_nt(a, b):
    return lax.dot_general(a, b, (((1,), (1,)), ((), ())), preferred_element_type=f32)


def mm_tn(a, b):
    return lax.dot_general(a, b, (((0,), (0,)), ((), ())), preferred_element_type=f32)


def exact(a, b):
    return lax.dot_general(
        a,
        b,
        (((1,), (0,)), ((), ())),
        precision=lax.Precision.HIGHEST,
        preferred_element_type=f32,
    )


def cost(us):
    return pl.CostEstimate(flops=int(us * 1.15e9), bytes_accessed=1 << 20, transcendentals=0)


def call(kernel, outs, ins, scratch=(), mib=16, us=2, **kw):
    return pl.pallas_call(
        kernel,
        out_shape=outs,
        in_specs=ins,
        out_specs=jax.tree.map(lambda _: vmem, outs),
        scratch_shapes=list(scratch),
        compiler_params=params(mib),
        cost_estimate=cost(us),
        **kw,
    )


def load_rows(ref, start, stride, count=128):
    return jnp.concatenate(
        [ref[j, pl.ds(start, count, stride=stride), :] for j in range(ref.shape[0])], axis=1
    )


def store_rows(ref, start, stride, value, first=0):
    for j in range(value.shape[1] // 128):
        ref[first + j, pl.ds(start, value.shape[0], stride=stride), :] = value[
            :, 128 * j : 128 * j + 128
        ]


def whole(ref, first, last):
    return jnp.concatenate([ref[j] for j in range(first, last)], axis=1)


def fill(ref, value):
    for j in range(ref.shape[0]):
        ref[j] = value[:, 128 * j : 128 * j + 128].astype(f32)


def sds(*shape, dtype=bf16):
    return jax.ShapeDtypeStruct(shape, dtype)


def pack_kernel(q_ref, k_ref, v_ref, o_ref, r_ref, small_ref, out_ref):
    q, k, v, o, r = (ref[...].astype(f32) for ref in (q_ref, k_ref, v_ref, o_ref, r_ref))
    six = jnp.concatenate([q, k, v, r], axis=1)
    row6 = jnp.concatenate([o[0:1], o[1:2], o[2:3], small_ref[...].astype(f32)], axis=1)
    row7 = jnp.concatenate([o[3:4], o[4:5], o[5:6], jnp.zeros((1, 128), f32)], axis=1)
    block = jnp.concatenate([six, row6, row7] * 2, axis=0).astype(bf16)
    for f in range(8):
        out_ref[16 * f : 16 * f + 16, :] = block


def pack_weights(w_query, w_key, w_value, w_output, w_router, small):
    return call(pack_kernel, [sds(128, PACK)], [vmem] * 6, name="pack_weights", mib=56)(
        w_query, w_key, w_value, w_output, w_router, small
    )[0]


def split_kernel(got_ref, heads_ref, more_ref, gf_ref, qf_ref, mf_ref):
    fill(gf_ref, got_ref)
    small = gf_ref[18, pl.ds(6, 16, stride=8), :]
    for r in range(6):
        for j in range(18):
            qf_ref[j, pl.ds(r, 16, stride=6), :] = gf_ref[j, pl.ds(r, 16, stride=8), :]
        mf_ref[6, pl.ds(r, 16, stride=6), :] = gf_ref[18, pl.ds(r, 16, stride=8), :]
        for j in range(6):
            mf_ref[j, pl.ds(r, 16, stride=6), :] = gf_ref[
                6 * (r % 3) + j, pl.ds(6 + r // 3, 16, stride=8), :
            ]
        third_lane = small[:, 12 + r : 13 + r] if r < 3 else jnp.zeros((16, 1), f32)
        cols = [small[:, r : r + 1], small[:, 6 + r : 7 + r], third_lane, jnp.zeros((16, 125), f32)]
        qf_ref[18, pl.ds(r, 16, stride=6), :] = jnp.concatenate(cols, axis=1)
    q, k, v = (whole(qf_ref, 6 * m, 6 * m + 6) for m in range(3))
    small = qf_ref[18][:, :64]
    for y in range(4):
        at = slice(COLS * y, COLS * y + COLS)
        rows = jnp.concatenate([q[:, at], k[:, at], v[:, at], small], axis=1).astype(bf16)
        heads_ref[192 * y : 192 * y + 96, :] = rows
        heads_ref[192 * y + 96 : 192 * y + 192, :] = rows
    more_ref[...] = whole(mf_ref, 0, 7).astype(bf16)


def split_weights(got):
    return call(
        split_kernel,
        [sds(WIDTH, SENT), sds(96, MORE)],
        [vmem],
        [
            pltpu.VMEM((19, 128, 128), f32),
            pltpu.VMEM((19, 96, 128), f32),
            pltpu.VMEM((7, 96, 128), f32),
        ],
        name="split_weights",
        mib=56,
    )(got)


def output_kernel(idx_ref, *refs):
    near, far_ref, refs = refs[:4], refs[4], refs[5:]
    wo_ref, router_ref, src_ref, dst_ref = refs
    y, c = idx_ref[0], idx_ref[1]
    for side in range(2):
        for k in range(4):
            place = 2 * lax.rem(y + 4 - k, 4) + (c if side == 0 else 1 - c)
            n = 4 * side + k
            for j in range(7):
                at = slice(128 * j, 128 * j + 128)
                block = near[k][:, at] if side == 0 else far_ref[96 * k : 96 * k + 96, at]
                src_ref[n, j] = block.astype(f32)
                for r in range(6):
                    dst_ref[j, pl.ds(place * 6 + r, 16, stride=48), :] = src_ref[
                        n, j, pl.ds(r, 16, stride=6), :
                    ]
    wo_ref[...] = whole(dst_ref, 0, 6).astype(bf16)
    router_ref[...] = dst_ref[6].astype(bf16)


def output_weights(idx, blocks):
    return call(
        output_kernel,
        [sds(WIDTH, WIDTH), sds(WIDTH, 128)],
        [smem] + [vmem] * 5,
        [pltpu.VMEM((8, 7, 96, 128), f32), pltpu.VMEM((7, WIDTH, 128), f32)],
        name="output_weights",
        mib=12,
        us=3,
    )(idx, *blocks)


def unpack(y, pack_ref, wqkv_ref, gain_ref, band_ref, pf_ref, wf_ref):
    fill(pf_ref, pack_ref)
    for s in range(8):
        for r in range(6):
            rows = load_rows(pf_ref, 96 * s + r, 6, 16)
            store_rows(wf_ref, 6 * s + r, 48, rows)
    wqkv_ref[...] = whole(wf_ref, 0, 5)[:, : 3 * COLS].astype(bf16)
    small = wf_ref[4].T
    gain_ref[...] = jnp.concatenate([small[64:66], jnp.zeros((6, WIDTH), f32)], axis=0)
    lanes = iota((8, WIDTH), 1)
    group = sixth(lanes)
    entry = 3 * group + lanes - 6 * group
    mine = (lanes - 6 * group < 3) & ((entry >> 5) == 3 * y + iota((8, WIDTH), 0))
    table = jnp.where(mine, small[66:67], 0.0).astype(bf16)
    rows = iota((WIDTH, 128), 0)
    group = sixth(rows)
    entry = 3 * group + rows - 6 * group
    table = mm(table, ((entry & 31) == iota((WIDTH, 128), 1)).astype(bf16)).astype(bf16)
    hot = bucket_of(iota((128, 512), 1) - 255) == iota((128, 512), 0)
    lines = mm(table, hot.astype(bf16))
    for h in range(GROUP):
        line = lines[h : h + 1]
        wide = pltpu.roll(
            jnp.broadcast_to(line, (TOK, 512)), 385, 1, stride=1, stride_axis=0
        )
        band_ref[h, :, :TOK] = jnp.broadcast_to(line[:, :1], (TOK, TOK))
        band_ref[h, :, TOK : 4 * TOK] = wide[:, : 3 * TOK]
        band_ref[h, :, 4 * TOK :] = jnp.broadcast_to(line[:, 511:], (TOK, TOK))


def banded(band_ref, h, pq):
    parts = []
    for j in range(8):
        at = jnp.clip(j - pq + 2, 0, 4) * TOK
        parts.append(band_ref[h, :, pl.ds(pl.multiple_of(at, TOK), TOK)])
    return jnp.concatenate(parts, axis=1)


def attend_kernel(
    idx_ref, pack_ref, seg_ref, *refs
):
    blocks, refs = refs[:8], refs[8:]
    o0_ref, o1_ref, o2_ref, o3_ref, gain_ref, lse_ref = refs[:6]
    saved, refs = refs[6:12], refs[12:]
    wqkv_ref, band_ref, x_ref, qe_ref, ke_ref, v_ref = refs[:6]
    pf_ref, wf_ref, os_ref, in_sem, out_sem = refs[6:]
    y, c = idx_ref[0], idx_ref[1]
    loads = []
    for side in range(2):
        for k in range(4):
            place = 2 * lax.rem(y + 4 - k, 4) + (c if side == 0 else 1 - c)
            at = pl.ds(pl.multiple_of(place * TOK, TOK), TOK)
            n = 4 * side + k
            loads.append(pltpu.make_async_copy(blocks[n], x_ref.at[at, :], in_sem.at[n]))
    for load in loads:
        load.start()
    stores = [
        pltpu.make_async_copy(src, dst, out_sem.at[n])
        for n, (src, dst) in enumerate(zip(refs[:6], saved))
    ]
    unpack(y, pack_ref, wqkv_ref, gain_ref, band_ref, pf_ref, wf_ref)
    for store in stores[:2]:
        store.start()
    for load in loads:
        load.wait()
    stores[2].start()
    gain = gain_ref[:1, :]

    def project(i, _):
        at = pl.ds(pl.multiple_of(i * PROJ, PROJ), PROJ)
        x = x_ref[at, :].astype(f32)
        hb = (x * lax.rsqrt(jnp.mean(x * x, axis=-1, keepdims=True) + eps) * gain).astype(bf16)
        doc = seg_ref[at, :]
        lane = iota((PROJ, HD), 1)
        same = lane == doc
        q_mark = jnp.where(same, -1e30, 0.0).astype(bf16)
        k_mark = jnp.where((lane < 3) & jnp.logical_not(same), 1.0, 0.0).astype(bf16)
        q = (mm(hb, wqkv_ref[:, :COLS]).astype(bf16).astype(f32) * 0.125).astype(bf16)
        k = mm(hb, wqkv_ref[:, COLS : 2 * COLS]).astype(bf16)
        v_ref[at, :] = mm(hb, wqkv_ref[:, 2 * COLS :]).astype(bf16)
        q_parts, k_parts = [], []
        for h in range(GROUP):
            q_parts += [q[:, HD * h : HD * h + HD], q_mark]
            k_parts += [k[:, HD * h : HD * h + HD], k_mark]
        qe_ref[at, :] = jnp.concatenate(q_parts, axis=1)
        ke_ref[at, :] = jnp.concatenate(k_parts, axis=1)
        return 0

    lax.fori_loop(0, LEN // PROJ, project, 0)
    for store in stores[3:]:
        store.start()

    def attend(k, _):
        yq = lax.rem(y + k, 4)
        pq = 2 * yq + c
        at = pl.ds(pl.multiple_of(pq * TOK, TOK), TOK)
        lane = iota((TOK, 128), 1)
        lse_all = jnp.zeros((TOK, 128), f32)
        outs = []
        for h in range(GROUP):
            s = mm_nt(qe_ref[at, 128 * h : 128 * h + 128], ke_ref[:, 128 * h : 128 * h + 128])
            s = s + banded(band_ref, h, pq)
            top = jnp.max(s, axis=-1, keepdims=True)
            e = jnp.exp(s - top)
            total = jnp.sum(e, axis=-1, keepdims=True)
            p = (e * (1.0 / total)).astype(bf16)
            outs.append(mm(p, v_ref[:, HD * h : HD * h + HD]))
            lse_all = jnp.where(lane == h, top + jnp.log(total), lse_all)
        os_ref[k] = jnp.concatenate(outs, axis=1).astype(bf16)
        lse_ref[yq] = lse_all
        return 0

    lax.fori_loop(0, 4, attend, 0, unroll=2)
    o0_ref[...] = os_ref[0]
    o1_ref[...] = os_ref[1]
    o2_ref[...] = os_ref[2]
    o3_ref[...] = os_ref[3]
    for store in stores:
        store.wait()


def attend(idx, pack, seg_col, blocks):
    saved = [
        sds(WIDTH, 3 * COLS), sds(GROUP, TOK, BAND, dtype=f32),
        sds(LEN, WIDTH), sds(LEN, 384), sds(LEN, 384), sds(LEN, COLS),
    ]
    outs = [sds(TOK, COLS)] * 4 + [sds(8, WIDTH, dtype=f32), sds(4, TOK, 128, dtype=f32)]
    place = pl.BlockSpec(memory_space=pl.ANY)
    return pl.pallas_call(
        attend_kernel,
        out_shape=outs + saved,
        in_specs=[smem, vmem, vmem] + [place] * 8,
        out_specs=[vmem] * 6 + [place] * 6,
        scratch_shapes=[pltpu.VMEM(v.shape, v.dtype) for v in saved]
        + [
            pltpu.VMEM((5, WIDTH, 128), f32),
            pltpu.VMEM((5, WIDTH, 128), f32),
            pltpu.VMEM((4, TOK, COLS), bf16),
            pltpu.SemaphoreType.DMA((8,)),
            pltpu.SemaphoreType.DMA((6,)),
        ],
        compiler_params=params(56),
        cost_estimate=cost(14),
        name="attend",
    )(idx, pack, seg_col, *blocks)


def dispatch_kernel(
    idx_ref, x_ref, o0_ref, o1_ref, o2_ref, o3_ref, wo_ref, router_ref, gain_ref,
    route_ref, cot_ref,
    x1_ref, h2_ref, prob_ref, hot_ref, send_ref,
    sf_ref,
):
    y = idx_ref[0]
    x1 = x_ref[...].astype(f32)
    for k, o_ref in enumerate((o0_ref, o1_ref, o2_ref, o3_ref)):
        src = lax.rem(y + 4 - k, 4)
        x1 = x1 + mm(o_ref[...], wo_ref[pl.ds(pl.multiple_of(src * COLS, COLS), COLS), :])
    x1_ref[...] = x1
    r2 = lax.rsqrt(jnp.mean(x1 * x1, axis=-1, keepdims=True) + eps)
    h2 = (x1 * r2 * gain_ref[1:2, :]).astype(bf16)
    h2_ref[...] = h2
    logits = mm(h2, router_ref[...])
    e = jnp.exp(logits - jnp.max(logits, axis=-1, keepdims=True))
    prob = e / jnp.sum(e, axis=-1, keepdims=True)
    prob_ref[...] = prob
    expert = iota((TOK, 128), 1)
    picked = (route_ref[...] == expert).astype(f32)
    gate = jnp.sum(prob * picked, axis=-1, keepdims=True)
    earlier = (iota((TOK, TOK), 0) > iota((TOK, TOK), 1)).astype(bf16)
    slot = jnp.sum(mm(earlier, picked.astype(bf16)) * picked, axis=-1, keepdims=True)
    geo = (gate * cot_ref[...].astype(f32)).astype(bf16)
    for s in range(2):
        hot = jnp.where((slot > 0.5) == (s == 1), picked, 0.0).astype(bf16)
        hot_ref[s] = hot
        for kind, src in enumerate((h2, geo)):
            placed = mm_tn(hot, src)
            for half in range(2):
                part = placed[:, HALF * half : HALF * half + HALF]
                store_rows(sf_ref, kind * 4 + s * 2 + half, 8, part)
    send_ref[...] = whole(sf_ref, 0, 3).astype(bf16)


def dispatch(idx, x_own, o_parts, wo, router, gains, route_col, cot):
    outs = [
        sds(TOK, WIDTH, dtype=f32), sds(TOK, WIDTH), sds(TOK, 128, dtype=f32),
        sds(2, TOK, 128), sds(LEN, HALF),
    ]
    return call(
        dispatch_kernel,
        outs,
        [smem] + [vmem] * 10,
        [pltpu.VMEM((3, LEN, 128), f32)],
        name="dispatch",
        mib=10,
    )(idx, x_own, *o_parts, wo, router, gains, route_col, cot)


def expert_kernel(
    recv_ref, wi_ref, wo_ref, ret_ref, gi_hbm, go_hbm,
    rf_ref, x_ref, xt_ref, g_ref, eo_ref, gx_ref, gi_ref, go_ref, out_sem,
):
    tiles = FF // FF_TILE
    stores = []
    for i in range(tiles):
        at = pl.ds(i * FF_TILE, FF_TILE)
        stores.append(
            (
                pltpu.make_async_copy(gi_ref.at[i], gi_hbm.at[0, :, at], out_sem.at[0, i]),
                pltpu.make_async_copy(go_ref.at[i], go_hbm.at[0, at, :], out_sem.at[1, i]),
            )
        )
    fill(rf_ref, recv_ref)
    for kind, dst in enumerate((x_ref, g_ref)):
        for s in range(2):
            for half in range(2):
                dst[TOK * s : TOK * s + TOK, HALF * half : HALF * half + HALF] = load_rows(
                    rf_ref, kind * 4 + s * 2 + half, 8
                ).astype(bf16)
    xt_ref[...] = x_ref[...].T
    for i in range(tiles):
        wi = wi_ref[0, :, FF_TILE * i : FF_TILE * i + FF_TILE]
        wo = wo_ref[0, FF_TILE * i : FF_TILE * i + FF_TILE, :]
        g = g_ref[...]
        a = mm(x_ref[...], wi)
        gu = mm_nt(g, wo)
        cc = 0.7978845608028654
        sq = a * a
        t = jnp.tanh(cc * (a + 0.044715 * (sq * a)))
        u = (0.5 * a * (1.0 + t)).astype(bf16)
        slope = 0.5 * (1.0 + t) + (0.5 * cc) * a * (1.0 - t * t) * (1.0 + 0.134145 * sq)
        ga = (gu * slope).astype(bf16)
        go_ref[i] = mm_tn(u, g).astype(bf16)
        gi_ref[i] = mm(xt_ref[...], ga).astype(bf16)
        for store in stores[i]:
            store.start()
        if i == 0:
            eo_ref[...] = mm(u, wo)
            gx_ref[...] = mm_nt(ga, wi)
        else:
            eo_ref[...] += mm(u, wo)
            gx_ref[...] += mm_nt(ga, wi)
    for kind, src in enumerate((eo_ref, gx_ref)):
        for s in range(2):
            for half in range(2):
                part = src[TOK * s : TOK * s + TOK, HALF * half : HALF * half + HALF]
                store_rows(rf_ref, kind * 4 + s * 2 + half, 8, part)
    ret_ref[...] = whole(rf_ref, 0, 3).astype(bf16)
    for pair in stores:
        for store in pair:
            store.wait()


def experts(recv, w_inner, w_outer):
    place = pl.BlockSpec(memory_space=pl.ANY)
    tiles = FF // FF_TILE
    return pl.pallas_call(
        expert_kernel,
        out_shape=[sds(LEN, HALF), sds(1, WIDTH, FF), sds(1, FF, WIDTH)],
        in_specs=[vmem, vmem, vmem],
        out_specs=[vmem, place, place],
        scratch_shapes=[
            pltpu.VMEM((3, LEN, 128), f32),
            pltpu.VMEM((2 * TOK, WIDTH), bf16),
            pltpu.VMEM((WIDTH, 2 * TOK), bf16),
            pltpu.VMEM((2 * TOK, WIDTH), bf16),
            pltpu.VMEM((2 * TOK, WIDTH), f32),
            pltpu.VMEM((2 * TOK, WIDTH), f32),
            pltpu.VMEM((tiles, WIDTH, FF_TILE), bf16),
            pltpu.VMEM((tiles, FF_TILE, WIDTH), bf16),
            pltpu.SemaphoreType.DMA((2, tiles)),
        ],
        compiler_params=params(20),
        cost_estimate=cost(12),
        name="experts",
    )(recv, w_inner, w_outer)


def return_kernel(
    idx_ref, back_ref, x1_ref, h2_ref, prob_ref, hot_ref, cot_ref, router_ref, gain_ref, wo_ref,
    o0_ref, o1_ref, o2_ref, o3_ref,
    out_ref, dx1_ref, g0_ref, g1_ref, g2_ref, g3_ref, keep_ref, give_ref, dgain_ref,
    bf_ref,
):
    y, c = idx_ref[0], idx_ref[1]
    fill(bf_ref, back_ref)
    parts = []
    for kind in range(2):
        halves = []
        for half in range(2):
            got = jnp.zeros((TOK, HALF), f32)
            for s in range(2):
                rows = load_rows(bf_ref, kind * 4 + s * 2 + half, 8).astype(bf16)
                got = got + mm(hot_ref[s], rows)
            halves.append(got)
        parts.append(jnp.concatenate(halves, axis=1))
    eo, gx = parts
    x1 = x1_ref[...]
    prob = prob_ref[...]
    picked = hot_ref[0].astype(f32) + hot_ref[1].astype(f32)
    gate = jnp.sum(prob * picked, axis=-1, keepdims=True)
    out_ref[...] = (x1 + gate * eo).astype(bf16)
    dy = cot_ref[...].astype(f32)
    dgate = jnp.sum(dy * eo, axis=-1, keepdims=True)
    gz = (dgate * gate * (picked - prob)).astype(bf16)
    dh2 = gx + mm_nt(gz, router_ref[...])
    routed = mm_tn(h2_ref[...], gz)
    blank = jnp.zeros((WIDTH, 64), f32)
    near = jnp.concatenate([routed[:, :64], blank], axis=1)
    far = jnp.concatenate([routed[:, 64:], blank], axis=1)
    keep_ref[:, HALF:] = jnp.where(c == 0, near, far).astype(bf16)
    give_ref[:, HALF:] = jnp.where(c == 0, far, near).astype(bf16)
    r2 = lax.rsqrt(jnp.mean(x1 * x1, axis=-1, keepdims=True) + eps)
    scaled = x1 * r2
    dgain = jnp.sum(dh2 * scaled, axis=0, keepdims=True)
    dgain_ref[...] = jnp.broadcast_to(dgain, (8, WIDTH))
    gd = gain_ref[1:2, :] * dh2
    dx1 = dy + r2 * (gd - scaled * jnp.mean(gd * scaled, axis=-1, keepdims=True))
    dx1_ref[...] = dx1
    gw = dx1.astype(bf16)
    for k, g_ref in enumerate((g0_ref, g1_ref, g2_ref, g3_ref)):
        dst = lax.rem(y + k, 4)
        rows = wo_ref[pl.ds(pl.multiple_of(dst * COLS, COLS), COLS), :]
        g_ref[...] = mm_nt(gw, rows).astype(bf16)
    for k, o_ref in enumerate((o0_ref, o1_ref, o2_ref, o3_ref)):
        src = lax.rem(y + 4 - k, 4)
        rows = pl.ds(pl.multiple_of(src * COLS, COLS), COLS)
        terms = mm_tn(o_ref[...], gw)
        near, far = terms[:, :HALF], terms[:, HALF:]
        keep_ref[rows, :HALF] = jnp.where(c == 0, near, far).astype(bf16)
        give_ref[rows, :HALF] = jnp.where(c == 0, far, near).astype(bf16)


def returned(idx, back, x1, h2, prob, hot, cot, router, gains, wo, o_parts):
    outs = (
        [sds(TOK, WIDTH), sds(TOK, WIDTH, dtype=f32)]
        + [sds(TOK, COLS)] * 4
        + [sds(WIDTH, LATE), sds(WIDTH, LATE), sds(8, WIDTH, dtype=f32)]
    )
    return call(
        return_kernel,
        outs,
        [smem] + [vmem] * 13,
        [pltpu.VMEM((3, LEN, 128), f32)],
        name="returned",
        mib=14,
    )(idx, back, x1, h2, prob, hot, cot, router, gains, wo, *o_parts)


def backward_kernel(
    idx_ref, g0_ref, g1_ref, g2_ref, g3_ref, x_ref, wqkv_ref, qe_ref, ke_ref, v_ref,
    band_ref, lse_ref, gain_ref,
    own_ref, other_ref, keep_ref, give_ref, line_ref, acc_ref, h_ref,
    gs_ref, gk_ref, gv_ref, dq_ref,
):
    y, c = idx_ref[0], idx_ref[1]
    for k, g_ref in enumerate((g0_ref, g1_ref, g2_ref, g3_ref)):
        gs_ref[k] = g_ref[...]
    gk_ref[...] = jnp.zeros_like(gk_ref)
    gv_ref[...] = jnp.zeros_like(gv_ref)
    acc_ref[...] = jnp.zeros_like(acc_ref)

    def block(k, _):
        yq = lax.rem(y + 4 - k, 4)
        pq = 2 * yq + c
        at = pl.ds(pl.multiple_of(pq * TOK, TOK), TOK)
        not_at = pl.ds(pl.multiple_of((pq + 1 - 2 * c) * TOK, TOK), TOK)
        lse = lse_ref[yq]
        go = gs_ref[k]
        outs = []
        for h in range(GROUP):
            q = qe_ref[at, 128 * h : 128 * h + 128]
            keys = ke_ref[:, 128 * h : 128 * h + 128]
            g = go[:, HD * h : HD * h + HD]
            s = mm_nt(q, keys) + banded(band_ref, h, pq)
            p = jnp.exp(s - lse[:, h : h + 1])
            pd = p * mm_nt(g, v_ref[:, HD * h : HD * h + HD])
            gs = pd - p * jnp.sum(pd, axis=-1, keepdims=True)
            for j in range(8):
                to = pl.multiple_of(jnp.clip(j - pq + 2, 0, 4) * TOK, TOK)
                acc_ref[h, :, pl.ds(to, TOK)] += gs[:, TOK * j : TOK * j + TOK]
            low = gs.astype(bf16)
            outs.append(mm(low, keys)[:, :HD] * 0.125)
            gk_ref[HD * h : HD * h + HD, :] += mm_tn(q, low)[:HD]
            gv_ref[HD * h : HD * h + HD, :] += mm_tn(g, p.astype(bf16))
        dq_ref[at, :COLS] = jnp.concatenate(outs, axis=1).astype(bf16)
        dq_ref[not_at, :COLS] = jnp.zeros((TOK, COLS), bf16)
        return 0

    lax.fori_loop(0, 4, block, 0)
    dq_ref[:, COLS : 2 * COLS] = gk_ref[...].T.astype(bf16)
    dq_ref[:, 2 * COLS :] = gv_ref[...].T.astype(bf16)
    first = jnp.concatenate([dq_ref[:, :256], jnp.zeros((LEN, 64), bf16)], axis=1)
    second = dq_ref[:, 256:]
    keep_ref[...] = jnp.where(c == 0, first, second)
    give = jnp.where(c == 0, second, first)
    lines = jnp.zeros((1, WIDTH), f32)
    for side in range(2):
        rows = []
        for yq in range(4):
            pq = 2 * yq + (c if side == 0 else 1 - c)
            rows.append(pl.ds(pl.multiple_of(pq * TOK, TOK), TOK))
        d = mm_nt(jnp.concatenate([dq_ref[at, :] for at in rows], axis=0), wqkv_ref[...])
        x = jnp.concatenate([x_ref[at, :] for at in rows], axis=0).astype(f32)
        scaled = x * lax.rsqrt(jnp.mean(x * x, axis=-1, keepdims=True) + eps)
        lines = lines + jnp.sum(d * scaled, axis=0, keepdims=True)
        hb = (scaled * gain_ref[:1, :]).astype(bf16)
        for yq in range(4):
            part = slice(TOK * yq, TOK * yq + TOK)
            h_ref[rows[yq], :] = hb[part]
            if side == 0:
                own_ref[yq] = d[part]
            else:
                other_ref[yq] = d[part].astype(bf16)
    line_ref[...] = jnp.broadcast_to(lines, (8, WIDTH))
    for j in range(6):
        at = slice(128 * j, 128 * j + 128)
        give_ref[at, :SIDE] = mm_tn(h_ref[:, at], give).astype(bf16)
    give_ref[:, SIDE:] = jnp.zeros((WIDTH, PART - SIDE), bf16)


def attend_back(idx, go_parts, x_all, wqkv, qe, ke, v, band, lse, gains):
    outs = [
        sds(4, TOK, WIDTH, dtype=f32), sds(4, TOK, WIDTH), sds(LEN, SIDE), sds(WIDTH, PART),
        sds(8, WIDTH, dtype=f32), sds(GROUP, TOK, BAND, dtype=f32), sds(LEN, WIDTH),
    ]
    return call(
        backward_kernel,
        outs,
        [smem] + [vmem] * 12,
        [
            pltpu.VMEM((4, TOK, COLS), bf16),
            pltpu.VMEM((COLS, LEN), f32),
            pltpu.VMEM((COLS, LEN), f32),
            pltpu.VMEM((LEN, 3 * COLS), bf16),
        ],
        name="attend_back",
        mib=26,
        us=12,
    )(idx, *go_parts, x_all, wqkv, qe, ke, v, band, lse, gains)


def kept_kernel(idx_ref, h_ref, dq_ref, line_ref, dgain_ref, acc_ref, kept_ref):
    y = idx_ref[0]
    ids = bucket_of(iota((512, 128), 0) - 255)
    flat = iota((512, 128), 1)
    turn = (iota((TOK, TOK), 0) + iota((TOK, TOK), 1) == TOK - 1).astype(f32)
    near = jnp.concatenate([acc_ref[h, :, TOK : 4 * TOK] for h in range(GROUP)], axis=1)
    near = exact(turn, near)
    blank = jnp.zeros((TOK, TOK), f32)
    lane = iota((1, 128), 1)
    diags, sides = [], []
    for h in range(GROUP):
        part = jnp.concatenate([near[:, 3 * TOK * h : 3 * TOK * h + 3 * TOK], blank], axis=1)
        part = pltpu.roll(part, 0, 1, stride=1, stride_axis=0)
        diags.append(jnp.sum(part, axis=0, keepdims=True))
        low = jnp.sum(acc_ref[h, :, :TOK])
        high = jnp.sum(acc_ref[h, :, 4 * TOK :])
        sides.append(jnp.where(lane == 15, low, 0.0) + jnp.where(lane == 31, high, 0.0))
    diags = jnp.concatenate(diags + [jnp.zeros((5, 512), f32)], axis=0)
    sides = jnp.concatenate(sides + [jnp.zeros((5, 128), f32)], axis=0)
    table = exact(diags, (flat == ids).astype(f32)) + sides
    lanes = iota((128, WIDTH), 1)
    group = sixth(lanes)
    entry = 3 * group + lanes - 6 * group
    place = ((entry & 31) == iota((128, WIDTH), 0)).astype(f32)
    lanes = iota((8, WIDTH), 1)
    group = sixth(lanes)
    entry = 3 * group + lanes - 6 * group
    mine = (lanes - 6 * group < 3) & ((entry >> 5) == 3 * y + iota((8, WIDTH), 0))
    mine = mine & (iota((8, WIDTH), 0) < GROUP)
    table = jnp.where(mine, exact(table, place), 0.0)
    table = jnp.sum(table, axis=0, keepdims=True)
    lines = []
    for v in (line_ref[:1, :], dgain_ref[:1, :], table):
        high = v.astype(bf16).astype(f32)
        lines += [high, v - high]
    block = jnp.concatenate(lines + [jnp.zeros((122, WIDTH), f32)], axis=0).T
    kept_ref[:, SIDE:] = block[:, :64]
    for j in range(6):
        at = slice(128 * j, 128 * j + 128)
        kept_ref[at, :SIDE] = mm_tn(h_ref[:, at], dq_ref[...])


def kept_terms(idx, h, dq, line, dgain, acc):
    return call(
        kept_kernel,
        [sds(WIDTH, PART, dtype=f32)],
        [smem] + [vmem] * 5,
        name="kept_terms",
        mib=12,
        us=4,
    )(idx, h, dq, line, dgain, acc)[0]


def joined_kernel(kept_ref, got_ref, keep_ref, late_ref, out_ref):
    out_ref[:, :PART] = (kept_ref[...] + got_ref[...].astype(f32)).astype(bf16)
    out_ref[:, PART:] = (keep_ref[...].astype(f32) + late_ref[...].astype(f32)).astype(bf16)


def joined_terms(kept, got, keep, late):
    return call(
        joined_kernel, [sds(WIDTH, PART + LATE)], [vmem] * 4, name="joined_terms", mib=8
    )(kept, got, keep, late)[0]


def pair_kernel(idx_ref, own_ref, got_ref, d0_ref, d1_ref, d2_ref, d3_ref):
    y = idx_ref[0]
    for k, d_ref in enumerate((d0_ref, d1_ref, d2_ref, d3_ref)):
        dst = lax.rem(y + k, 4)
        d_ref[...] = (own_ref[dst] + got_ref[dst].astype(f32)).astype(d_ref.dtype)


def pair_sum(idx, own, got):
    outs = [sds(TOK, WIDTH, dtype=f32)] + [sds(TOK, WIDTH)] * 3
    return call(pair_kernel, outs, [smem, vmem, vmem], name="pair_sum")(idx, own, got)


def tokens_kernel(d0_ref, d1_ref, d2_ref, d3_ref, x_ref, gain_ref, dx1_ref, out_ref):
    dh = d0_ref[...] + d1_ref[...].astype(f32) + d2_ref[...].astype(f32) + d3_ref[...].astype(f32)
    x = x_ref[...].astype(f32)
    r1 = lax.rsqrt(jnp.mean(x * x, axis=-1, keepdims=True) + eps)
    gd = gain_ref[:1, :] * dh
    scaled = x * r1
    out_ref[...] = dx1_ref[...] + r1 * (gd - scaled * jnp.mean(gd * scaled, axis=-1, keepdims=True))


def tokens_last(d_parts, x_own, gains, dx1):
    return call(tokens_kernel, [sds(TOK, WIDTH, dtype=f32)], [vmem] * 7, name="tokens_last")(
        *d_parts, x_own, gains, dx1
    )[0]


def middle_kernel(got_ref, out_ref):
    def total(a, b):
        sums = got_ref[:48, a:b].astype(f32)
        for f in range(1, 16):
            sums = sums + got_ref[48 * f : 48 * f + 48, a:b].astype(f32)
        return sums

    pieces = [total(0, 256)]
    last = total(256, PART)
    lane = iota((48, 128), 1)
    both = last + pltpu.roll(last, 127, 1)
    high = both.astype(bf16).astype(f32)
    rest = pltpu.roll(both - high, 1, 1)
    last = jnp.where(lane < 64, last, jnp.where(lane % 2 == 0, high, rest))
    pieces += [last, total(PART, PART + LATE)]
    sums = jnp.concatenate(pieces, axis=1)
    blank = jnp.zeros((2, PART + LATE), f32)
    rows = []
    for s in range(8):
        rows += [sums[6 * s : 6 * s + 6], blank]
    out_ref[...] = jnp.concatenate(rows, axis=0).astype(bf16)


def middle_sums(got):
    return call(middle_kernel, [sds(64, PART + LATE)], [vmem], name="middle_sums", mib=8)(got)[0]


def sums_kernel(recv_ref, q_ref, k_ref, v_ref, o_ref, router_ref, small_ref):
    got = recv_ref[...].astype(f32)
    parts = [got[8 * s : 8 * s + 8] for s in range(8)]
    quads = [
        jnp.concatenate([parts[2 * y][:, :256], parts[2 * y + 1][:, :SIDE]], axis=1) for y in range(4)
    ]
    for m, ref in enumerate((q_ref, k_ref, v_ref)):
        cols = jnp.concatenate([a[:, COLS * m : COLS * m + COLS] for a in quads], axis=1)
        ref[...] = cols[:6].astype(bf16)
    halves = [parts[c] + parts[2 + c] + parts[4 + c] + parts[6 + c] for c in range(2)]
    o_ref[...] = jnp.concatenate([a[:6, PART : PART + HALF] for a in halves], axis=1).astype(bf16)
    routed = [a[:6, PART + HALF : PART + HALF + 64] for a in halves]
    router_ref[...] = jnp.concatenate(routed, axis=1).astype(bf16)
    small_ref[...] = halves[0][:, 256:PART] + halves[1][:, 256:PART]


def sums_last(recv):
    outs = [sds(6, WIDTH)] * 4 + [sds(6, 128), sds(8, 128, dtype=f32)]
    return call(sums_kernel, outs, [vmem], name="sums_last", mib=4)(recv)


def along_y(v, k):
    return lax.ppermute(v, "seq", [(s, (s + 2 * k) % 8) for s in range(8)])


def exchange(v, axes):
    return lax.all_to_all(v, axes, split_axis=0, concat_axis=0, tiled=True)


def other_core(v):
    return lax.ppermute(v, "seq", [(s, s ^ 1) for s in range(8)])


def on_device(
    tokens, segments, routes, gain_attn, w_query, w_key, w_value, w_output, rel_table, gain_moe,
    w_router, w_inner, w_outer, cotangent,
):
    seq = lax.axis_index("seq")
    idx = jnp.stack([seq // 2, seq % 2]).astype(jnp.int32)
    blocks = [tokens] + [along_y(tokens, k) for k in (1, 2, 3)]
    first = other_core(tokens)
    small = jnp.concatenate([gain_attn, gain_moe, rel_table, jnp.zeros((113,), bf16)])
    pack = pack_weights(w_query, w_key, w_value, w_output, w_router, small.reshape(1, 128))
    heads, more = split_weights(exchange(pack, "fsdp"))
    heads, blocks, first = lax.optimization_barrier((heads, blocks, first))
    heads, more = lax.optimization_barrier((exchange(heads, "seq"), more))
    blocks = blocks + [first] + [other_core(b) for b in blocks[1:]]
    attended = attend(idx, heads, segments.reshape(LEN, 1), blocks)
    more = [more] + [along_y(more, k) for k in (1, 2, 3)]
    more, attended = lax.optimization_barrier((more, attended))
    wo, router = output_weights(idx, more + [other_core(jnp.concatenate(more, axis=0))])
    o_parts = attended[:4]
    gains, lse, wqkv, band, x_all, qe, ke, v = attended[4:]
    o_parts = [o_parts[0]] + [along_y(o_parts[k], k) for k in (1, 2, 3)]
    x1, h2, prob, hot, send = dispatch(
        idx, tokens, o_parts, wo, router, gains, routes, cotangent
    )
    ret, grad_inner, grad_outer = experts(exchange(send, BOTH), w_inner, w_outer)
    back = exchange(ret, BOTH)
    layer_out, dx1, *more = returned(
        idx, back, x1, h2, prob, hot, cotangent, router, gains, wo, o_parts
    )
    go_parts = [more[0]] + [along_y(more[k], k) for k in (1, 2, 3)]
    keep, give, dgain = more[4:]
    late = other_core(give)
    own, other, dq_keep, give_terms, line, acc, h = attend_back(
        idx, go_parts, x_all, wqkv, qe, ke, v, band, lse, gains
    )
    got_terms = other_core(give_terms)
    kept = kept_terms(idx, h, dq_keep, line, dgain, acc)
    terms = joined_terms(kept, got_terms, keep, late)
    got = other_core(other)
    d_parts = pair_sum(idx, own, got)
    d_parts = [d_parts[0]] + [along_y(d_parts[k], k) for k in (1, 2, 3)]
    sums = exchange(middle_sums(exchange(terms, "fsdp")), "seq")
    dq, dk, dv, do, dr, small = sums_last(sums)
    tokens_grad = tokens_last(d_parts, tokens, gains, dx1)
    lines = small[:6, 64:70]
    lines = lines[:, 0::2] + lines[:, 1::2]
    return (
        layer_out,
        tokens_grad,
        lines[:, 0].astype(bf16),
        dq,
        dk,
        dv,
        do,
        lines[:3, 2].astype(bf16),
        lines[:, 1].astype(bf16),
        dr,
        grad_inner,
        grad_outer,
    )


def solution(mesh):
    rows = P(BOTH, None)
    flat = P(BOTH)
    cube = P(BOTH, None, None)
    return jax.shard_map(
        on_device,
        mesh=mesh,
        in_specs=(
            rows, P("fsdp", None), rows, flat, rows, rows, rows, rows, flat, flat, rows, cube, cube,
            rows,
        ),
        out_specs=(rows, rows, flat, rows, rows, rows, rows, flat, flat, rows, cube, cube),
        check_vma=False,
    )
```

```python
import functools

import jax
import jax.numpy as jnp
from jax import lax
from jax.experimental import pallas as pl
from jax.experimental.pallas import tpu as pltpu
from jax.sharding import PartitionSpec as P

bf16 = jnp.bfloat16
f32 = jnp.float32

WIDTH = 768
TOK = 128
LEN = 1024
FF = 3072
GROUP = 3
HD = 64
COLS = GROUP * HD
BAND = 5 * TOK
HALF = WIDTH // 2
PACK = 2432
MORE = 896
SENT = 640
SIDE = 320
PART = 384
LATE = 512
FF_TILE = 512
PROJ = 512
eps = 1e-06
bucket_edges = (12, 16, 23, 32, 46, 64, 91)
BOTH = ("fsdp", "seq")


def params(mib):
    return pltpu.CompilerParams(vmem_limit_bytes=mib << 20)


smem = pl.BlockSpec(memory_space=pltpu.SMEM)
vmem = pl.BlockSpec(memory_space=pltpu.VMEM)


def iota(shape, dim):
    return lax.broadcasted_iota(jnp.int32, shape, dim)


def sixth(n):
    return (n * 10923) >> 16


def third(n):
    return (n * 21846) >> 16


def bucket_of(offsets):
    spread = jnp.abs(offsets)
    ids = (offsets > 0).astype(jnp.int32) * 16 + jnp.minimum(spread, 8)
    for border in bucket_edges:
        ids = ids + (spread >= border).astype(jnp.int32)
    return ids


def mm(a, b):
    return jnp.dot(a, b, preferred_element_type=f32)


def mm_nt(a, b):
    return lax.dot_general(a, b, (((1,), (1,)), ((), ())), preferred_element_type=f32)


def mm_tn(a, b):
    return lax.dot_general(a, b, (((0,), (0,)), ((), ())), preferred_element_type=f32)


def exact(a, b):
    return lax.dot_general(
        a,
        b,
        (((1,), (0,)), ((), ())),
        precision=lax.Precision.HIGHEST,
        preferred_element_type=f32,
    )


def cost(us):
    return pl.CostEstimate(flops=int(us * 1.15e9), bytes_accessed=1 << 20, transcendentals=0)


def call(kernel, outs, ins, scratch=(), mib=16, us=2, **kw):
    return pl.pallas_call(
        kernel,
        out_shape=outs,
        in_specs=ins,
        out_specs=jax.tree.map(lambda _: vmem, outs),
        scratch_shapes=list(scratch),
        compiler_params=params(mib),
        cost_estimate=cost(us),
        **kw,
    )


def load_rows(ref, start, stride, count=128):
    return jnp.concatenate(
        [ref[j, pl.ds(start, count, stride=stride), :] for j in range(ref.shape[0])], axis=1
    )


def store_rows(ref, start, stride, value, first=0):
    for j in range(value.shape[1] // 128):
        ref[first + j, pl.ds(start, value.shape[0], stride=stride), :] = value[
            :, 128 * j : 128 * j + 128
        ]


def whole(ref, first, last):
    return jnp.concatenate([ref[j] for j in range(first, last)], axis=1)


def fill(ref, value):
    for j in range(ref.shape[0]):
        ref[j] = value[:, 128 * j : 128 * j + 128].astype(f32)


def sds(*shape, dtype=bf16):
    return jax.ShapeDtypeStruct(shape, dtype)


def pack_kernel(q_ref, k_ref, v_ref, o_ref, r_ref, small_ref, out_ref):
    q, k, v, o, r = (ref[...].astype(f32) for ref in (q_ref, k_ref, v_ref, o_ref, r_ref))
    six = jnp.concatenate([q, k, v, r], axis=1)
    row6 = jnp.concatenate([o[0:1], o[1:2], o[2:3], small_ref[...].astype(f32)], axis=1)
    row7 = jnp.concatenate([o[3:4], o[4:5], o[5:6], jnp.zeros((1, 128), f32)], axis=1)
    block = jnp.concatenate([six, row6, row7] * 2, axis=0).astype(bf16)
    for f in range(8):
        out_ref[16 * f : 16 * f + 16, :] = block


def pack_weights(w_query, w_key, w_value, w_output, w_router, small):
    return call(pack_kernel, [sds(128, PACK)], [vmem] * 6, name="pack_weights", mib=56)(
        w_query, w_key, w_value, w_output, w_router, small
    )[0]


def split_kernel(got_ref, heads_ref, more_ref, gf_ref, qf_ref, mf_ref):
    fill(gf_ref, got_ref)
    small = gf_ref[18, pl.ds(6, 16, stride=8), :]
    for r in range(6):
        for j in range(18):
            qf_ref[j, pl.ds(r, 16, stride=6), :] = gf_ref[j, pl.ds(r, 16, stride=8), :]
        mf_ref[6, pl.ds(r, 16, stride=6), :] = gf_ref[18, pl.ds(r, 16, stride=8), :]
        for j in range(6):
            mf_ref[j, pl.ds(r, 16, stride=6), :] = gf_ref[
                6 * (r % 3) + j, pl.ds(6 + r // 3, 16, stride=8), :
            ]
        third_lane = small[:, 12 + r : 13 + r] if r < 3 else jnp.zeros((16, 1), f32)
        cols = [small[:, r : r + 1], small[:, 6 + r : 7 + r], third_lane, jnp.zeros((16, 125), f32)]
        qf_ref[18, pl.ds(r, 16, stride=6), :] = jnp.concatenate(cols, axis=1)
    q, k, v = (whole(qf_ref, 6 * m, 6 * m + 6) for m in range(3))
    small = qf_ref[18][:, :64]
    for y in range(4):
        at = slice(COLS * y, COLS * y + COLS)
        rows = jnp.concatenate([q[:, at], k[:, at], v[:, at], small], axis=1).astype(bf16)
        heads_ref[192 * y : 192 * y + 96, :] = rows
        heads_ref[192 * y + 96 : 192 * y + 192, :] = rows
    more_ref[...] = whole(mf_ref, 0, 7).astype(bf16)


def split_weights(got):
    return call(
        split_kernel,
        [sds(WIDTH, SENT), sds(96, MORE)],
        [vmem],
        [
            pltpu.VMEM((19, 128, 128), f32),
            pltpu.VMEM((19, 96, 128), f32),
            pltpu.VMEM((7, 96, 128), f32),
        ],
        name="split_weights",
        mib=56,
    )(got)


def output_kernel(idx_ref, *refs):
    near, far_ref, refs = refs[:4], refs[4], refs[5:]
    wo_ref, router_ref, src_ref, dst_ref = refs
    y, c = idx_ref[0], idx_ref[1]
    for side in range(2):
        for k in range(4):
            place = 2 * lax.rem(y + 4 - k, 4) + (c if side == 0 else 1 - c)
            n = 4 * side + k
            for j in range(7):
                at = slice(128 * j, 128 * j + 128)
                block = near[k][:, at] if side == 0 else far_ref[96 * k : 96 * k + 96, at]
                src_ref[n, j] = block.astype(f32)
                for r in range(6):
                    dst_ref[j, pl.ds(place * 6 + r, 16, stride=48), :] = src_ref[
                        n, j, pl.ds(r, 16, stride=6), :
                    ]
    wo_ref[...] = whole(dst_ref, 0, 6).astype(bf16)
    router_ref[...] = dst_ref[6].astype(bf16)


def output_weights(idx, blocks):
    return call(
        output_kernel,
        [sds(WIDTH, WIDTH), sds(WIDTH, 128)],
        [smem] + [vmem] * 5,
        [pltpu.VMEM((8, 7, 96, 128), f32), pltpu.VMEM((7, WIDTH, 128), f32)],
        name="output_weights",
        mib=12,
        us=3,
    )(idx, *blocks)


def unpack(y, pack_ref, wqkv_ref, gain_ref, band_ref, pf_ref, wf_ref):
    fill(pf_ref, pack_ref)
    for s in range(8):
        for r in range(6):
            rows = load_rows(pf_ref, 96 * s + r, 6, 16)
            store_rows(wf_ref, 6 * s + r, 48, rows)
    wqkv_ref[...] = whole(wf_ref, 0, 5)[:, : 3 * COLS].astype(bf16)
    small = wf_ref[4].T
    gain_ref[...] = jnp.concatenate([small[64:66], jnp.zeros((6, WIDTH), f32)], axis=0)
    lanes = iota((8, WIDTH), 1)
    group = sixth(lanes)
    entry = 3 * group + lanes - 6 * group
    mine = (lanes - 6 * group < 3) & ((entry >> 5) == 3 * y + iota((8, WIDTH), 0))
    table = jnp.where(mine, small[66:67], 0.0).astype(bf16)
    rows = iota((WIDTH, 128), 0)
    group = sixth(rows)
    entry = 3 * group + rows - 6 * group
    table = mm(table, ((entry & 31) == iota((WIDTH, 128), 1)).astype(bf16)).astype(bf16)
    hot = bucket_of(iota((128, 512), 1) - 255) == iota((128, 512), 0)
    lines = mm(table, hot.astype(bf16))
    for h in range(GROUP):
        line = lines[h : h + 1]
        wide = pltpu.roll(
            jnp.broadcast_to(line, (TOK, 512)), 385, 1, stride=1, stride_axis=0
        )
        band_ref[h, :, :TOK] = jnp.broadcast_to(line[:, :1], (TOK, TOK))
        band_ref[h, :, TOK : 4 * TOK] = wide[:, : 3 * TOK]
        band_ref[h, :, 4 * TOK :] = jnp.broadcast_to(line[:, 511:], (TOK, TOK))


def banded(band_ref, h, pq):
    parts = []
    for j in range(8):
        at = jnp.clip(j - pq + 2, 0, 4) * TOK
        parts.append(band_ref[h, :, pl.ds(pl.multiple_of(at, TOK), TOK)])
    return jnp.concatenate(parts, axis=1)


def attend_kernel(
    idx_ref, pack_ref, seg_ref, *refs
):
    blocks, refs = refs[:8], refs[8:]
    o0_ref, o1_ref, o2_ref, o3_ref, gain_ref, lse_ref = refs[:6]
    saved, refs = refs[6:12], refs[12:]
    wqkv_ref, band_ref, x_ref, qe_ref, ke_ref, v_ref = refs[:6]
    pf_ref, wf_ref, os_ref, in_sem, out_sem = refs[6:]
    y, c = idx_ref[0], idx_ref[1]
    loads = []
    for side in range(2):
        for k in range(4):
            place = 2 * lax.rem(y + 4 - k, 4) + (c if side == 0 else 1 - c)
            at = pl.ds(pl.multiple_of(place * TOK, TOK), TOK)
            n = 4 * side + k
            loads.append(pltpu.make_async_copy(blocks[n], x_ref.at[at, :], in_sem.at[n]))
    for load in loads:
        load.start()
    stores = [
        pltpu.make_async_copy(src, dst, out_sem.at[n])
        for n, (src, dst) in enumerate(zip(refs[:6], saved))
    ]
    unpack(y, pack_ref, wqkv_ref, gain_ref, band_ref, pf_ref, wf_ref)
    for store in stores[:2]:
        store.start()
    for load in loads:
        load.wait()
    stores[2].start()
    gain = gain_ref[:1, :]

    def project(i, _):
        at = pl.ds(pl.multiple_of(i * PROJ, PROJ), PROJ)
        x = x_ref[at, :].astype(f32)
        hb = (x * lax.rsqrt(jnp.mean(x * x, axis=-1, keepdims=True) + eps) * gain).astype(bf16)
        doc = seg_ref[at, :]
        lane = iota((PROJ, HD), 1)
        same = lane == doc
        q_mark = jnp.where(same, -1e30, 0.0).astype(bf16)
        k_mark = jnp.where((lane < 3) & jnp.logical_not(same), 1.0, 0.0).astype(bf16)
        q = (mm(hb, wqkv_ref[:, :COLS]).astype(bf16).astype(f32) * 0.125).astype(bf16)
        k = mm(hb, wqkv_ref[:, COLS : 2 * COLS]).astype(bf16)
        v_ref[at, :] = mm(hb, wqkv_ref[:, 2 * COLS :]).astype(bf16)
        q_parts, k_parts = [], []
        for h in range(GROUP):
            q_parts += [q[:, HD * h : HD * h + HD], q_mark]
            k_parts += [k[:, HD * h : HD * h + HD], k_mark]
        qe_ref[at, :] = jnp.concatenate(q_parts, axis=1)
        ke_ref[at, :] = jnp.concatenate(k_parts, axis=1)
        return 0

    lax.fori_loop(0, LEN // PROJ, project, 0)
    for store in stores[3:]:
        store.start()

    def attend(k, _):
        yq = lax.rem(y + k, 4)
        pq = 2 * yq + c
        at = pl.ds(pl.multiple_of(pq * TOK, TOK), TOK)
        lane = iota((TOK, 128), 1)
        lse_all = jnp.zeros((TOK, 128), f32)
        outs = []
        for h in range(GROUP):
            s = mm_nt(qe_ref[at, 128 * h : 128 * h + 128], ke_ref[:, 128 * h : 128 * h + 128])
            s = s + banded(band_ref, h, pq)
            top = jnp.max(s, axis=-1, keepdims=True)
            e = jnp.exp(s - top)
            total = jnp.sum(e, axis=-1, keepdims=True)
            p = (e * (1.0 / total)).astype(bf16)
            outs.append(mm(p, v_ref[:, HD * h : HD * h + HD]))
            lse_all = jnp.where(lane == h, top + jnp.log(total), lse_all)
        os_ref[k] = jnp.concatenate(outs, axis=1).astype(bf16)
        lse_ref[yq] = lse_all
        return 0

    lax.fori_loop(0, 4, attend, 0, unroll=2)
    o0_ref[...] = os_ref[0]
    o1_ref[...] = os_ref[1]
    o2_ref[...] = os_ref[2]
    o3_ref[...] = os_ref[3]
    for store in stores:
        store.wait()


def attend(idx, pack, seg_col, blocks):
    saved = [
        sds(WIDTH, 3 * COLS), sds(GROUP, TOK, BAND, dtype=f32),
        sds(LEN, WIDTH), sds(LEN, 384), sds(LEN, 384), sds(LEN, COLS),
    ]
    outs = [sds(TOK, COLS)] * 4 + [sds(8, WIDTH, dtype=f32), sds(4, TOK, 128, dtype=f32)]
    place = pl.BlockSpec(memory_space=pl.ANY)
    return pl.pallas_call(
        attend_kernel,
        out_shape=outs + saved,
        in_specs=[smem, vmem, vmem] + [place] * 8,
        out_specs=[vmem] * 6 + [place] * 6,
        scratch_shapes=[pltpu.VMEM(v.shape, v.dtype) for v in saved]
        + [
            pltpu.VMEM((5, WIDTH, 128), f32),
            pltpu.VMEM((5, WIDTH, 128), f32),
            pltpu.VMEM((4, TOK, COLS), bf16),
            pltpu.SemaphoreType.DMA((8,)),
            pltpu.SemaphoreType.DMA((6,)),
        ],
        compiler_params=params(56),
        cost_estimate=cost(14),
        name="attend",
    )(idx, pack, seg_col, *blocks)


def dispatch_kernel(
    idx_ref, x_ref, o0_ref, o1_ref, o2_ref, o3_ref, wo_ref, router_ref, gain_ref,
    route_ref, cot_ref,
    x1_ref, h2_ref, prob_ref, hot_ref, send_ref,
    sf_ref,
):
    y = idx_ref[0]
    x1 = x_ref[...].astype(f32)
    for k, o_ref in enumerate((o0_ref, o1_ref, o2_ref, o3_ref)):
        src = lax.rem(y + 4 - k, 4)
        x1 = x1 + mm(o_ref[...], wo_ref[pl.ds(pl.multiple_of(src * COLS, COLS), COLS), :])
    x1_ref[...] = x1
    r2 = lax.rsqrt(jnp.mean(x1 * x1, axis=-1, keepdims=True) + eps)
    h2 = (x1 * r2 * gain_ref[1:2, :]).astype(bf16)
    h2_ref[...] = h2
    logits = mm(h2, router_ref[...])
    e = jnp.exp(logits - jnp.max(logits, axis=-1, keepdims=True))
    prob = e / jnp.sum(e, axis=-1, keepdims=True)
    prob_ref[...] = prob
    expert = iota((TOK, 128), 1)
    picked = (route_ref[...] == expert).astype(f32)
    gate = jnp.sum(prob * picked, axis=-1, keepdims=True)
    earlier = (iota((TOK, TOK), 0) > iota((TOK, TOK), 1)).astype(bf16)
    slot = jnp.sum(mm(earlier, picked.astype(bf16)) * picked, axis=-1, keepdims=True)
    geo = (gate * cot_ref[...].astype(f32)).astype(bf16)
    for s in range(2):
        hot = jnp.where((slot > 0.5) == (s == 1), picked, 0.0).astype(bf16)
        hot_ref[s] = hot
        for kind, src in enumerate((h2, geo)):
            placed = mm_tn(hot, src)
            for half in range(2):
                part = placed[:, HALF * half : HALF * half + HALF]
                store_rows(sf_ref, kind * 4 + s * 2 + half, 8, part)
    send_ref[...] = whole(sf_ref, 0, 3).astype(bf16)


def dispatch(idx, x_own, o_parts, wo, router, gains, route_col, cot):
    outs = [
        sds(TOK, WIDTH, dtype=f32), sds(TOK, WIDTH), sds(TOK, 128, dtype=f32),
        sds(2, TOK, 128), sds(LEN, HALF),
    ]
    return call(
        dispatch_kernel,
        outs,
        [smem] + [vmem] * 10,
        [pltpu.VMEM((3, LEN, 128), f32)],
        name="dispatch",
        mib=10,
    )(idx, x_own, *o_parts, wo, router, gains, route_col, cot)


def expert_kernel(
    recv_ref, wi_ref, wo_ref, ret_ref, gi_hbm, go_hbm,
    rf_ref, x_ref, xt_ref, g_ref, eo_ref, gx_ref, gi_ref, go_ref, out_sem,
):
    tiles = FF // FF_TILE
    stores = []
    for i in range(tiles):
        at = pl.ds(i * FF_TILE, FF_TILE)
        stores.append(
            (
                pltpu.make_async_copy(gi_ref.at[i], gi_hbm.at[0, :, at], out_sem.at[0, i]),
                pltpu.make_async_copy(go_ref.at[i], go_hbm.at[0, at, :], out_sem.at[1, i]),
            )
        )
    fill(rf_ref, recv_ref)
    for kind, dst in enumerate((x_ref, g_ref)):
        for s in range(2):
            for half in range(2):
                dst[TOK * s : TOK * s + TOK, HALF * half : HALF * half + HALF] = load_rows(
                    rf_ref, kind * 4 + s * 2 + half, 8
                ).astype(bf16)
    xt_ref[...] = x_ref[...].T
    for i in range(tiles):
        wi = wi_ref[0, :, FF_TILE * i : FF_TILE * i + FF_TILE]
        wo = wo_ref[0, FF_TILE * i : FF_TILE * i + FF_TILE, :]
        g = g_ref[...]
        a = mm(x_ref[...], wi)
        gu = mm_nt(g, wo)
        cc = 0.7978845608028654
        sq = a * a
        t = jnp.tanh(cc * (a + 0.044715 * (sq * a)))
        u = (0.5 * a * (1.0 + t)).astype(bf16)
        slope = 0.5 * (1.0 + t) + (0.5 * cc) * a * (1.0 - t * t) * (1.0 + 0.134145 * sq)
        ga = (gu * slope).astype(bf16)
        go_ref[i] = mm_tn(u, g).astype(bf16)
        gi_ref[i] = mm(xt_ref[...], ga).astype(bf16)
        for store in stores[i]:
            store.start()
        if i == 0:
            eo_ref[...] = mm(u, wo)
            gx_ref[...] = mm_nt(ga, wi)
        else:
            eo_ref[...] += mm(u, wo)
            gx_ref[...] += mm_nt(ga, wi)
    for kind, src in enumerate((eo_ref, gx_ref)):
        for s in range(2):
            for half in range(2):
                part = src[TOK * s : TOK * s + TOK, HALF * half : HALF * half + HALF]
                store_rows(rf_ref, kind * 4 + s * 2 + half, 8, part)
    ret_ref[...] = whole(rf_ref, 0, 3).astype(bf16)
    for pair in stores:
        for store in pair:
            store.wait()


def experts(recv, w_inner, w_outer):
    place = pl.BlockSpec(memory_space=pl.ANY)
    tiles = FF // FF_TILE
    return pl.pallas_call(
        expert_kernel,
        out_shape=[sds(LEN, HALF), sds(1, WIDTH, FF), sds(1, FF, WIDTH)],
        in_specs=[vmem, vmem, vmem],
        out_specs=[vmem, place, place],
        scratch_shapes=[
            pltpu.VMEM((3, LEN, 128), f32),
            pltpu.VMEM((2 * TOK, WIDTH), bf16),
            pltpu.VMEM((WIDTH, 2 * TOK), bf16),
            pltpu.VMEM((2 * TOK, WIDTH), bf16),
            pltpu.VMEM((2 * TOK, WIDTH), f32),
            pltpu.VMEM((2 * TOK, WIDTH), f32),
            pltpu.VMEM((tiles, WIDTH, FF_TILE), bf16),
            pltpu.VMEM((tiles, FF_TILE, WIDTH), bf16),
            pltpu.SemaphoreType.DMA((2, tiles)),
        ],
        compiler_params=params(20),
        cost_estimate=cost(12),
        name="experts",
    )(recv, w_inner, w_outer)


def return_kernel(
    idx_ref, back_ref, x1_ref, h2_ref, prob_ref, hot_ref, cot_ref, router_ref, gain_ref, wo_ref,
    o0_ref, o1_ref, o2_ref, o3_ref,
    out_ref, dx1_ref, g0_ref, g1_ref, g2_ref, g3_ref, keep_ref, give_ref, dgain_ref,
    bf_ref,
):
    y, c = idx_ref[0], idx_ref[1]
    fill(bf_ref, back_ref)
    parts = []
    for kind in range(2):
        halves = []
        for half in range(2):
            got = jnp.zeros((TOK, HALF), f32)
            for s in range(2):
                rows = load_rows(bf_ref, kind * 4 + s * 2 + half, 8).astype(bf16)
                got = got + mm(hot_ref[s], rows)
            halves.append(got)
        parts.append(jnp.concatenate(halves, axis=1))
    eo, gx = parts
    x1 = x1_ref[...]
    prob = prob_ref[...]
    picked = hot_ref[0].astype(f32) + hot_ref[1].astype(f32)
    gate = jnp.sum(prob * picked, axis=-1, keepdims=True)
    out_ref[...] = (x1 + gate * eo).astype(bf16)
    dy = cot_ref[...].astype(f32)
    dgate = jnp.sum(dy * eo, axis=-1, keepdims=True)
    gz = (dgate * gate * (picked - prob)).astype(bf16)
    dh2 = gx + mm_nt(gz, router_ref[...])
    routed = mm_tn(h2_ref[...], gz)
    blank = jnp.zeros((WIDTH, 64), f32)
    near = jnp.concatenate([routed[:, :64], blank], axis=1)
    far = jnp.concatenate([routed[:, 64:], blank], axis=1)
    keep_ref[:, HALF:] = jnp.where(c == 0, near, far).astype(bf16)
    give_ref[:, HALF:] = jnp.where(c == 0, far, near).astype(bf16)
    r2 = lax.rsqrt(jnp.mean(x1 * x1, axis=-1, keepdims=True) + eps)
    scaled = x1 * r2
    dgain = jnp.sum(dh2 * scaled, axis=0, keepdims=True)
    dgain_ref[...] = jnp.broadcast_to(dgain, (8, WIDTH))
    gd = gain_ref[1:2, :] * dh2
    dx1 = dy + r2 * (gd - scaled * jnp.mean(gd * scaled, axis=-1, keepdims=True))
    dx1_ref[...] = dx1
    gw = dx1.astype(bf16)
    for k, g_ref in enumerate((g0_ref, g1_ref, g2_ref, g3_ref)):
        dst = lax.rem(y + k, 4)
        rows = wo_ref[pl.ds(pl.multiple_of(dst * COLS, COLS), COLS), :]
        g_ref[...] = mm_nt(gw, rows).astype(bf16)
    for k, o_ref in enumerate((o0_ref, o1_ref, o2_ref, o3_ref)):
        src = lax.rem(y + 4 - k, 4)
        rows = pl.ds(pl.multiple_of(src * COLS, COLS), COLS)
        terms = mm_tn(o_ref[...], gw)
        near, far = terms[:, :HALF], terms[:, HALF:]
        keep_ref[rows, :HALF] = jnp.where(c == 0, near, far).astype(bf16)
        give_ref[rows, :HALF] = jnp.where(c == 0, far, near).astype(bf16)


def returned(idx, back, x1, h2, prob, hot, cot, router, gains, wo, o_parts):
    outs = (
        [sds(TOK, WIDTH), sds(TOK, WIDTH, dtype=f32)]
        + [sds(TOK, COLS)] * 4
        + [sds(WIDTH, LATE), sds(WIDTH, LATE), sds(8, WIDTH, dtype=f32)]
    )
    return call(
        return_kernel,
        outs,
        [smem] + [vmem] * 13,
        [pltpu.VMEM((3, LEN, 128), f32)],
        name="returned",
        mib=14,
    )(idx, back, x1, h2, prob, hot, cot, router, gains, wo, *o_parts)


def backward_kernel(
    idx_ref, g0_ref, g1_ref, g2_ref, g3_ref, x_ref, wqkv_ref, qe_ref, ke_ref, v_ref,
    band_ref, lse_ref, gain_ref,
    own_ref, other_ref, keep_ref, give_ref, line_ref, acc_ref, h_ref,
    gs_ref, gk_ref, gv_ref, dq_ref,
):
    y, c = idx_ref[0], idx_ref[1]
    for k, g_ref in enumerate((g0_ref, g1_ref, g2_ref, g3_ref)):
        gs_ref[k] = g_ref[...]
    gk_ref[...] = jnp.zeros_like(gk_ref)
    gv_ref[...] = jnp.zeros_like(gv_ref)
    acc_ref[...] = jnp.zeros_like(acc_ref)

    def block(k, _):
        yq = lax.rem(y + 4 - k, 4)
        pq = 2 * yq + c
        at = pl.ds(pl.multiple_of(pq * TOK, TOK), TOK)
        not_at = pl.ds(pl.multiple_of((pq + 1 - 2 * c) * TOK, TOK), TOK)
        lse = lse_ref[yq]
        go = gs_ref[k]
        outs = []
        for h in range(GROUP):
            q = qe_ref[at, 128 * h : 128 * h + 128]
            keys = ke_ref[:, 128 * h : 128 * h + 128]
            g = go[:, HD * h : HD * h + HD]
            s = mm_nt(q, keys) + banded(band_ref, h, pq)
            p = jnp.exp(s - lse[:, h : h + 1])
            pd = p * mm_nt(g, v_ref[:, HD * h : HD * h + HD])
            gs = pd - p * jnp.sum(pd, axis=-1, keepdims=True)
            for j in range(8):
                to = pl.multiple_of(jnp.clip(j - pq + 2, 0, 4) * TOK, TOK)
                acc_ref[h, :, pl.ds(to, TOK)] += gs[:, TOK * j : TOK * j + TOK]
            low = gs.astype(bf16)
            outs.append(mm(low, keys)[:, :HD] * 0.125)
            gk_ref[HD * h : HD * h + HD, :] += mm_tn(q, low)[:HD]
            gv_ref[HD * h : HD * h + HD, :] += mm_tn(g, p.astype(bf16))
        dq_ref[at, :COLS] = jnp.concatenate(outs, axis=1).astype(bf16)
        dq_ref[not_at, :COLS] = jnp.zeros((TOK, COLS), bf16)
        return 0

    lax.fori_loop(0, 4, block, 0)
    dq_ref[:, COLS : 2 * COLS] = gk_ref[...].T.astype(bf16)
    dq_ref[:, 2 * COLS :] = gv_ref[...].T.astype(bf16)
    first = jnp.concatenate([dq_ref[:, :256], jnp.zeros((LEN, 64), bf16)], axis=1)
    second = dq_ref[:, 256:]
    keep_ref[...] = jnp.where(c == 0, first, second)
    give = jnp.where(c == 0, second, first)
    lines = jnp.zeros((1, WIDTH), f32)
    for side in range(2):
        rows = []
        for yq in range(4):
            pq = 2 * yq + (c if side == 0 else 1 - c)
            rows.append(pl.ds(pl.multiple_of(pq * TOK, TOK), TOK))
        d = mm_nt(jnp.concatenate([dq_ref[at, :] for at in rows], axis=0), wqkv_ref[...])
        x = jnp.concatenate([x_ref[at, :] for at in rows], axis=0).astype(f32)
        scaled = x * lax.rsqrt(jnp.mean(x * x, axis=-1, keepdims=True) + eps)
        lines = lines + jnp.sum(d * scaled, axis=0, keepdims=True)
        hb = (scaled * gain_ref[:1, :]).astype(bf16)
        for yq in range(4):
            part = slice(TOK * yq, TOK * yq + TOK)
            h_ref[rows[yq], :] = hb[part]
            if side == 0:
                own_ref[yq] = d[part]
            else:
                other_ref[yq] = d[part].astype(bf16)
    line_ref[...] = jnp.broadcast_to(lines, (8, WIDTH))
    for j in range(6):
        at = slice(128 * j, 128 * j + 128)
        give_ref[at, :SIDE] = mm_tn(h_ref[:, at], give).astype(bf16)
    give_ref[:, SIDE:] = jnp.zeros((WIDTH, PART - SIDE), bf16)


def attend_back(idx, go_parts, x_all, wqkv, qe, ke, v, band, lse, gains):
    outs = [
        sds(4, TOK, WIDTH, dtype=f32), sds(4, TOK, WIDTH), sds(LEN, SIDE), sds(WIDTH, PART),
        sds(8, WIDTH, dtype=f32), sds(GROUP, TOK, BAND, dtype=f32), sds(LEN, WIDTH),
    ]
    return call(
        backward_kernel,
        outs,
        [smem] + [vmem] * 12,
        [
            pltpu.VMEM((4, TOK, COLS), bf16),
            pltpu.VMEM((COLS, LEN), f32),
            pltpu.VMEM((COLS, LEN), f32),
            pltpu.VMEM((LEN, 3 * COLS), bf16),
        ],
        name="attend_back",
        mib=26,
        us=12,
    )(idx, *go_parts, x_all, wqkv, qe, ke, v, band, lse, gains)


def kept_kernel(idx_ref, h_ref, dq_ref, line_ref, dgain_ref, acc_ref, kept_ref):
    y = idx_ref[0]
    ids = bucket_of(iota((512, 128), 0) - 255)
    flat = iota((512, 128), 1)
    turn = (iota((TOK, TOK), 0) + iota((TOK, TOK), 1) == TOK - 1).astype(f32)
    near = jnp.concatenate([acc_ref[h, :, TOK : 4 * TOK] for h in range(GROUP)], axis=1)
    near = exact(turn, near)
    blank = jnp.zeros((TOK, TOK), f32)
    lane = iota((1, 128), 1)
    diags, sides = [], []
    for h in range(GROUP):
        part = jnp.concatenate([near[:, 3 * TOK * h : 3 * TOK * h + 3 * TOK], blank], axis=1)
        part = pltpu.roll(part, 0, 1, stride=1, stride_axis=0)
        diags.append(jnp.sum(part, axis=0, keepdims=True))
        low = jnp.sum(acc_ref[h, :, :TOK])
        high = jnp.sum(acc_ref[h, :, 4 * TOK :])
        sides.append(jnp.where(lane == 15, low, 0.0) + jnp.where(lane == 31, high, 0.0))
    diags = jnp.concatenate(diags + [jnp.zeros((5, 512), f32)], axis=0)
    sides = jnp.concatenate(sides + [jnp.zeros((5, 128), f32)], axis=0)
    table = exact(diags, (flat == ids).astype(f32)) + sides
    lanes = iota((128, WIDTH), 1)
    group = sixth(lanes)
    entry = 3 * group + lanes - 6 * group
    place = ((entry & 31) == iota((128, WIDTH), 0)).astype(f32)
    lanes = iota((8, WIDTH), 1)
    group = sixth(lanes)
    entry = 3 * group + lanes - 6 * group
    mine = (lanes - 6 * group < 3) & ((entry >> 5) == 3 * y + iota((8, WIDTH), 0))
    mine = mine & (iota((8, WIDTH), 0) < GROUP)
    table = jnp.where(mine, exact(table, place), 0.0)
    table = jnp.sum(table, axis=0, keepdims=True)
    lines = []
    for v in (line_ref[:1, :], dgain_ref[:1, :], table):
        high = v.astype(bf16).astype(f32)
        lines += [high, v - high]
    block = jnp.concatenate(lines + [jnp.zeros((122, WIDTH), f32)], axis=0).T
    kept_ref[:, SIDE:] = block[:, :64]
    for j in range(6):
        at = slice(128 * j, 128 * j + 128)
        kept_ref[at, :SIDE] = mm_tn(h_ref[:, at], dq_ref[...])


def kept_terms(idx, h, dq, line, dgain, acc):
    return call(
        kept_kernel,
        [sds(WIDTH, PART, dtype=f32)],
        [smem] + [vmem] * 5,
        name="kept_terms",
        mib=12,
        us=4,
    )(idx, h, dq, line, dgain, acc)[0]


def joined_kernel(kept_ref, got_ref, keep_ref, late_ref, out_ref):
    out_ref[:, :PART] = (kept_ref[...] + got_ref[...].astype(f32)).astype(bf16)
    out_ref[:, PART:] = (keep_ref[...].astype(f32) + late_ref[...].astype(f32)).astype(bf16)


def joined_terms(kept, got, keep, late):
    return call(
        joined_kernel, [sds(WIDTH, PART + LATE)], [vmem] * 4, name="joined_terms", mib=8
    )(kept, got, keep, late)[0]


def pair_kernel(idx_ref, own_ref, got_ref, d0_ref, d1_ref, d2_ref, d3_ref):
    y = idx_ref[0]
    for k, d_ref in enumerate((d0_ref, d1_ref, d2_ref, d3_ref)):
        dst = lax.rem(y + k, 4)
        d_ref[...] = (own_ref[dst] + got_ref[dst].astype(f32)).astype(d_ref.dtype)


def pair_sum(idx, own, got):
    outs = [sds(TOK, WIDTH, dtype=f32)] + [sds(TOK, WIDTH)] * 3
    return call(pair_kernel, outs, [smem, vmem, vmem], name="pair_sum")(idx, own, got)


def tokens_kernel(d0_ref, d1_ref, d2_ref, d3_ref, x_ref, gain_ref, dx1_ref, out_ref):
    dh = d0_ref[...] + d1_ref[...].astype(f32) + d2_ref[...].astype(f32) + d3_ref[...].astype(f32)
    x = x_ref[...].astype(f32)
    r1 = lax.rsqrt(jnp.mean(x * x, axis=-1, keepdims=True) + eps)
    gd = gain_ref[:1, :] * dh
    scaled = x * r1
    out_ref[...] = dx1_ref[...] + r1 * (gd - scaled * jnp.mean(gd * scaled, axis=-1, keepdims=True))


def tokens_last(d_parts, x_own, gains, dx1):
    return call(tokens_kernel, [sds(TOK, WIDTH, dtype=f32)], [vmem] * 7, name="tokens_last")(
        *d_parts, x_own, gains, dx1
    )[0]


def middle_kernel(got_ref, out_ref):
    def total(a, b):
        sums = got_ref[:48, a:b].astype(f32)
        for f in range(1, 16):
            sums = sums + got_ref[48 * f : 48 * f + 48, a:b].astype(f32)
        return sums

    pieces = [total(0, 256)]
    last = total(256, PART)
    lane = iota((48, 128), 1)
    both = last + pltpu.roll(last, 127, 1)
    high = both.astype(bf16).astype(f32)
    rest = pltpu.roll(both - high, 1, 1)
    last = jnp.where(lane < 64, last, jnp.where(lane % 2 == 0, high, rest))
    pieces += [last, total(PART, PART + LATE)]
    sums = jnp.concatenate(pieces, axis=1)
    blank = jnp.zeros((2, PART + LATE), f32)
    rows = []
    for s in range(8):
        rows += [sums[6 * s : 6 * s + 6], blank]
    out_ref[...] = jnp.concatenate(rows, axis=0).astype(bf16)


def middle_sums(got):
    return call(middle_kernel, [sds(64, PART + LATE)], [vmem], name="middle_sums", mib=8)(got)[0]


def sums_kernel(recv_ref, q_ref, k_ref, v_ref, o_ref, router_ref, small_ref):
    got = recv_ref[...].astype(f32)
    parts = [got[8 * s : 8 * s + 8] for s in range(8)]
    quads = [
        jnp.concatenate([parts[2 * y][:, :256], parts[2 * y + 1][:, :SIDE]], axis=1) for y in range(4)
    ]
    for m, ref in enumerate((q_ref, k_ref, v_ref)):
        cols = jnp.concatenate([a[:, COLS * m : COLS * m + COLS] for a in quads], axis=1)
        ref[...] = cols[:6].astype(bf16)
    halves = [parts[c] + parts[2 + c] + parts[4 + c] + parts[6 + c] for c in range(2)]
    o_ref[...] = jnp.concatenate([a[:6, PART : PART + HALF] for a in halves], axis=1).astype(bf16)
    routed = [a[:6, PART + HALF : PART + HALF + 64] for a in halves]
    router_ref[...] = jnp.concatenate(routed, axis=1).astype(bf16)
    small_ref[...] = halves[0][:, 256:PART] + halves[1][:, 256:PART]


def sums_last(recv):
    outs = [sds(6, WIDTH)] * 4 + [sds(6, 128), sds(8, 128, dtype=f32)]
    return call(sums_kernel, outs, [vmem], name="sums_last", mib=4)(recv)


def along_y(v, k):
    return lax.ppermute(v, "seq", [(s, (s + 2 * k) % 8) for s in range(8)])


def exchange(v, axes):
    return lax.all_to_all(v, axes, split_axis=0, concat_axis=0, tiled=True)


def other_core(v):
    return lax.ppermute(v, "seq", [(s, s ^ 1) for s in range(8)])


def on_device(
    tokens, segments, routes, gain_attn, w_query, w_key, w_value, w_output, rel_table, gain_moe,
    w_router, w_inner, w_outer, cotangent,
):
    seq = lax.axis_index("seq")
    idx = jnp.stack([seq // 2, seq % 2]).astype(jnp.int32)
    blocks = [tokens] + [along_y(tokens, k) for k in (1, 2, 3)]
    first = other_core(tokens)
    small = jnp.concatenate([gain_attn, gain_moe, rel_table, jnp.zeros((113,), bf16)])
    pack = pack_weights(w_query, w_key, w_value, w_output, w_router, small.reshape(1, 128))
    heads, more = split_weights(exchange(pack, "fsdp"))
    heads, blocks, first = lax.optimization_barrier((heads, blocks, first))
    heads, more = lax.optimization_barrier((exchange(heads, "seq"), more))
    blocks = blocks + [first] + [other_core(b) for b in blocks[1:]]
    attended = attend(idx, heads, segments.reshape(LEN, 1), blocks)
    more = [more] + [along_y(more, k) for k in (1, 2, 3)]
    more, attended = lax.optimization_barrier((more, attended))
    wo, router = output_weights(idx, more + [other_core(jnp.concatenate(more, axis=0))])
    o_parts = attended[:4]
    gains, lse, wqkv, band, x_all, qe, ke, v = attended[4:]
    o_parts = [o_parts[0]] + [along_y(o_parts[k], k) for k in (1, 2, 3)]
    x1, h2, prob, hot, send = dispatch(
        idx, tokens, o_parts, wo, router, gains, routes, cotangent
    )
    ret, grad_inner, grad_outer = experts(exchange(send, BOTH), w_inner, w_outer)
    back = exchange(ret, BOTH)
    layer_out, dx1, *more = returned(
        idx, back, x1, h2, prob, hot, cotangent, router, gains, wo, o_parts
    )
    go_parts = [more[0]] + [along_y(more[k], k) for k in (1, 2, 3)]
    keep, give, dgain = more[4:]
    late = other_core(give)
    own, other, dq_keep, give_terms, line, acc, h = attend_back(
        idx, go_parts, x_all, wqkv, qe, ke, v, band, lse, gains
    )
    got_terms = other_core(give_terms)
    kept = kept_terms(idx, h, dq_keep, line, dgain, acc)
    terms = joined_terms(kept, got_terms, keep, late)
    d_parts = pair_sum(idx, own, other_core(other))
    terms, d_parts = lax.optimization_barrier((terms, d_parts))
    d_parts = [d_parts[0]] + [along_y(d_parts[k], k) for k in (1, 2, 3)]
    sums = exchange(middle_sums(exchange(terms, "fsdp")), "seq")
    dq, dk, dv, do, dr, small = sums_last(sums)
    tokens_grad = tokens_last(d_parts, tokens, gains, dx1)
    lines = small[:6, 64:70]
    lines = lines[:, 0::2] + lines[:, 1::2]
    return (
        layer_out,
        tokens_grad,
        lines[:, 0].astype(bf16),
        dq,
        dk,
        dv,
        do,
        lines[:3, 2].astype(bf16),
        lines[:, 1].astype(bf16),
        dr,
        grad_inner,
        grad_outer,
    )


def solution(mesh):
    rows = P(BOTH, None)
    flat = P(BOTH)
    cube = P(BOTH, None, None)
    return jax.shard_map(
        on_device,
        mesh=mesh,
        in_specs=(
            rows, P("fsdp", None), rows, flat, rows, rows, rows, rows, flat, flat, rows, cube, cube,
            rows,
        ),
        out_specs=(rows, rows, flat, rows, rows, rows, rows, flat, flat, rows, cube, cube),
        check_vma=False,
    )
```
